32 devices in a mesh: dp: 8 (over y, x, core), tp: 4 (over z).
Axes of the slice: x: 2, y: 2, z: 4, core: 2. Of those that a mesh axis runs over, the one named last changes fastest.
Arguments:
- tokens: bfloat16 [8, 1024, 768], P('dp', 'tp')
- w_qkv: bfloat16 [768, 2304], replicated, may hold values from -0.21875 to 0.21875
- bias_query: bfloat16 [768], replicated, may hold values from -1.5 to 1.5
- bias_value: bfloat16 [768], replicated, may hold values from -1.5 to 1.5
- w_out: bfloat16 [768, 768], replicated, may hold values from -1.25 to 1.25
- bias_out: bfloat16 [768], replicated, may hold values from -1.5 to 1.5
- gain_attn: bfloat16 [768], replicated, may hold values from 0.25 to 1.75
- shift_attn: bfloat16 [768], replicated, may hold values from -1.5 to 1.5
- w_in: bfloat16 [768, 3072], P(None, 'tp'), may hold values from -0.21875 to 0.21875
- bias_in: bfloat16 [3072], P('tp'), may hold values from -1.5 to 1.5
- w_back: bfloat16 [3072, 768], P('tp'), may hold values from -0.109375 to 0.109375
- bias_back: bfloat16 [768], replicated, may hold values from -1.5 to 1.5
- gain_ffn: bfloat16 [768], replicated, may hold values from 0.25 to 1.75
- shift_ffn: bfloat16 [768], replicated, may hold values from -1.5 to 1.5
- random_blocks: int32 [8, 12, 16, 3], P('dp'), may hold values from 1 to 14, as said below
- cotangent: bfloat16 [8, 1024, 768], P('dp', 'tp'), may hold values from -6 to 6
Outputs:
- layer_out: bfloat16 [8, 1024, 768], P('dp', 'tp')
- grad_tokens: bfloat16 [8, 1024, 768], P('dp', 'tp')
- grad_w_qkv: float32 [768, 2304], replicated
- grad_bias_query: float32 [768], replicated
- grad_bias_value: float32 [768], replicated
- grad_w_out: float32 [768, 768], replicated
- grad_bias_out: float32 [768], replicated
- grad_gain_attn: float32 [768], replicated
- grad_shift_attn: float32 [768], replicated
- grad_w_in: float32 [768, 3072], P(None, 'tp')
- grad_bias_in: float32 [3072], P('tp')
- grad_w_back: float32 [3072, 768], P('tp')
- grad_bias_back: float32 [768], replicated
- grad_gain_ffn: float32 [768], replicated
- grad_shift_ffn: float32 [768], replicated
The draws below stay inside these ranges and needn't reach their ends.
Inputs may be any that keep to these rules, and one draw needn't show every extreme that they name: `random_blocks`: for each sequence, head and query block i, the 3 entries are different block numbers, none of them 0, 15, i - 1, i or i + 1.
All inputs are finite; a program needn't handle non-finite values.
Results may differ from the reference program's by a relative error of at most 0.017.
Values may be sent and summed in bfloat16 or wider, within the bound.
No kernel may reach another device: no remote copies, remote signals or barrier semaphores. Data moves between devices by JAX's collectives and lax.ppermute only.
A program may use at most 192 MiB of HBM per device.

```python
import math
import jax
import jax.numpy as jnp
from jax import lax

D = 768
HEADS = 12
FF = 3072
BLOCK = 64
RAND = 3
LENGTH = 1024
NB = 16
SEQS = 8


def draw_tokens(key, part):
    key = jax.random.fold_in(key, 3)
    key_base, key_cols, key_rows = jax.random.split(key, 3)
    col_scale = jnp.exp(jax.random.uniform(key_cols, (D,), jnp.float32, math.log(0.3), math.log(3.0)))
    row_scale = jnp.exp(jax.random.uniform(key_rows, (SEQS, LENGTH, 1), jnp.float32, math.log(0.7), math.log(1.4)))
    base_draw = jax.random.normal(key_base, (SEQS, LENGTH, D), jnp.float32)
    return (base_draw * col_scale * row_scale).astype(jnp.bfloat16)


def draw_random_blocks(key, part):
    key = jax.random.fold_in(key, 7)
    scores = jax.random.randint(key, (SEQS, HEADS, NB, NB), 0, 1 << 20, jnp.int32)
    block_ids = jnp.arange(NB, dtype=jnp.int32)[None, :]
    query_ids = jnp.arange(NB, dtype=jnp.int32)[:, None]
    scores = scores * NB + block_ids
    banned = (block_ids == 0) | (block_ids == NB - 1) | (jnp.abs(block_ids - query_ids) <= 1)
    scores = jnp.where(banned, -1, scores)
    picked_scores, picked = lax.top_k(scores, RAND)
    return picked.astype(jnp.int32)


def steps_of(stream_key, extent, cuts, least, top_value):
    level, own = 1.0, jax.random.fold_in(stream_key, 6)
    for position, blocks in cuts:
        heights = jnp.exp(jax.random.uniform(jax.random.fold_in(own, position), (blocks,), jnp.float32, least / len(cuts), top_value / len(cuts)))
        level = level * jnp.repeat(heights, extent[position] // blocks).reshape([-1 if axis == position else 1 for axis in range(len(extent))])
    return level


def gaussian(stream_key, extent, spread, limit, cuts=(), held_as=jnp.bfloat16):
    factor_of = steps_of(stream_key, extent, cuts, -0.22, 0.18) if cuts else 1.0
    drawn = jax.random.normal(stream_key, extent, jnp.float32) * spread * factor_of
    return jnp.minimum(jnp.maximum(drawn, -limit), limit).astype(held_as)


def setup_inputs(seed: int = 0) -> dict:
    arg_keys = jax.random.split(jax.random.key(seed), 17)
    return {
        "tokens": draw_tokens(jax.random.fold_in(arg_keys[16], 71), 0),
        "w_qkv": gaussian(arg_keys[1], (D, 3 * D), D ** -0.5, 0.21875),
        "bias_query": gaussian(arg_keys[2], (D,), 0.3, 1.5),
        "bias_value": gaussian(arg_keys[3], (D,), 0.3, 1.5),
        "w_out": gaussian(arg_keys[4], (D, D), (max(D // 32, 1)) ** -0.5, 1.25),
        "bias_out": gaussian(arg_keys[5], (D,), 0.3, 1.5),
        "gain_attn": jnp.clip(1.0 + 0.15 * jax.random.normal(arg_keys[6], (D,), jnp.float32), 0.25, 1.75).astype(jnp.bfloat16),
        "shift_attn": gaussian(arg_keys[7], (D,), 0.3, 1.5),
        "w_in": gaussian(arg_keys[8], (D, FF), D ** -0.5, 0.21875, ((1, 4),)),
        "bias_in": gaussian(arg_keys[9], (FF,), 0.3, 1.5, ((0, 4),)),
        "w_back": gaussian(arg_keys[10], (FF, D), FF ** -0.5, 0.109375, ((0, 4),)),
        "bias_back": gaussian(arg_keys[11], (D,), 0.3, 1.5),
        "gain_ffn": jnp.clip(1.0 + 0.15 * jax.random.normal(arg_keys[12], (D,), jnp.float32), 0.25, 1.75).astype(jnp.bfloat16),
        "shift_ffn": gaussian(arg_keys[13], (D,), 0.3, 1.5),
        "random_blocks": draw_random_blocks(jax.random.fold_in(arg_keys[16], 71), 0),
        "cotangent": gaussian(arg_keys[15], (SEQS, LENGTH, D), 1.0, 6.0, ((0, 8), (1, 4))),
    }


@jax.custom_vjp
def low(v):
    return lax.optimization_barrier(v.astype(jnp.bfloat16)).astype(jnp.float32)

@jax.custom_vjp
def low_back(v):
    return v

def low_keep(v):
    return (low(v), None)

def low_pass(kept, grad):
    return (grad,)

def back_keep(v):
    return (v, None)

def back_low(kept, grad):
    return (low(grad),)
low.defvjp(low_keep, low_pass)
low_back.defvjp(back_keep, back_low)
highest = lax.Precision.HIGHEST
epsilon = 1e-05
masked_score = -1e+30

def exact_dot(left, right):
    return jnp.dot(left, right, precision=highest)

def normalize(hidden_in, gain_vec, shift_vec):
    row_mean = lax.optimization_barrier(jnp.mean(hidden_in, axis=-1, keepdims=True))
    centred = hidden_in - row_mean
    variance = lax.optimization_barrier(jnp.mean(centred * centred, axis=-1, keepdims=True))
    return centred * lax.rsqrt(variance + epsilon) * gain_vec + shift_vec

def softmax_rows(scores):
    row_max = lax.optimization_barrier(jnp.max(scores, axis=-1, keepdims=True))
    shifted = jnp.exp(scores - row_max)
    return shifted / lax.optimization_barrier(jnp.sum(shifted, axis=-1, keepdims=True))

def to_heads(flat_rows):
    rows_count, model_width = flat_rows.shape
    shaped = flat_rows.reshape(rows_count // BLOCK, BLOCK, HEADS, model_width // HEADS)
    return shaped.transpose(2, 0, 1, 3)

def from_heads(blocked):
    heads_count, blocks_count, block_rows, head_dim = blocked.shape
    return blocked.transpose(1, 2, 0, 3).reshape(blocks_count * block_rows, heads_count * head_dim)

def block_lists(random_rows, first_block, local_blocks, total_blocks):
    block_ids = first_block + jnp.arange(local_blocks, dtype=jnp.int32)
    before_ids = block_ids - 1
    after_ids = block_ids + 1
    fixed_ids = jnp.stack([jnp.zeros_like(block_ids), jnp.full_like(block_ids, total_blocks - 1), before_ids, block_ids, after_ids], axis=-1)
    fixed_ok = jnp.stack([block_ids >= 0, block_ids >= 0, before_ids >= 1, (block_ids >= 1) & (block_ids <= total_blocks - 2), after_ids <= total_blocks - 2], axis=-1)
    fixed_ids = jnp.clip(fixed_ids, 0, total_blocks - 1).astype(jnp.int32)
    heads_count = random_rows.shape[0]
    key_lists = jnp.concatenate([jnp.broadcast_to(fixed_ids[None], (heads_count,) + fixed_ids.shape), random_rows.astype(jnp.int32)], axis=-1)
    key_valid = jnp.concatenate([fixed_ok, jnp.ones(random_rows.shape[1:], jnp.bool_)], axis=-1)
    return (key_lists, key_valid)

def gather_blocks(blocks, key_lists):
    picked = jax.vmap(lambda block_set, index_set: block_set[index_set])(blocks, key_lists)
    heads_count, local_blocks, picks_count, block_rows, head_dim = picked.shape
    return picked.reshape(heads_count, local_blocks, picks_count * block_rows, head_dim)

def global_rows(query_block, full_keys, full_values, score_scale):
    raw_scores = jnp.einsum('hbe,hje->hbj', query_block, full_keys, precision=highest)
    prob_low = low(softmax_rows(low_back(score_scale * raw_scores)))
    return jnp.einsum('hbj,hje->hbe', prob_low, full_values, precision=highest)

def attention(queries, keys_all, values, random_seq):
    query_blocks = to_heads(queries)
    key_heads = to_heads(keys_all)
    value_heads = to_heads(values)
    heads_count, total_blocks, block_rows, head_dim = key_heads.shape
    score_scale = head_dim ** (-0.5)
    key_lists, key_valid = block_lists(random_seq, 0, total_blocks, total_blocks)
    keep_mask = jnp.repeat(key_valid, block_rows, axis=-1)[None, :, None, :]
    picked_keys = gather_blocks(key_heads, key_lists)
    picked_values = gather_blocks(value_heads, key_lists)
    raw_scores = jnp.einsum('hqbe,hqje->hqbj', query_blocks, picked_keys, precision=highest)
    scores = low_back(jnp.where(keep_mask, score_scale * raw_scores, masked_score))
    prob_low = low(softmax_rows(scores))
    sparse_out = jnp.einsum('hqbj,hqje->hqbe', prob_low, picked_values, precision=highest)
    full_keys = key_heads.reshape(heads_count, total_blocks * block_rows, head_dim)
    full_values = value_heads.reshape(heads_count, total_blocks * block_rows, head_dim)
    first_out = global_rows(query_blocks[:, 0], full_keys, full_values, score_scale)
    last_out = global_rows(query_blocks[:, -1], full_keys, full_values, score_scale)
    attended = jnp.concatenate([first_out[:, None], sparse_out[:, 1:-1], last_out[:, None]], axis=1)
    return from_heads(attended)

def encoder_layer(params, token_rows, random_seq):
    w_qkv, bias_query, bias_value, w_out, bias_out, gain_attn, shift_attn, w_in, bias_in, w_back, bias_back, gain_ffn, shift_ffn = params
    projected = exact_dot(token_rows, w_qkv)
    queries = low_back(low(projected[:, :D] + bias_query))
    keys_all = low_back(low(projected[:, D:2 * D]))
    values = low_back(low(projected[:, 2 * D:] + bias_value))
    attended = low_back(low(attention(queries, keys_all, values, random_seq)))
    mixed_out = low_back(exact_dot(attended, w_out) + bias_out)
    first_norm = normalize(token_rows + mixed_out, gain_attn, shift_attn)
    pre_act = low_back(exact_dot(low(first_norm), w_in) + bias_in)
    activated = low(jax.nn.gelu(pre_act))
    branch = low_back(exact_dot(activated, w_back) + bias_back)
    return normalize(first_norm + branch, gain_ffn, shift_ffn)

def reference(tokens, w_qkv, bias_query, bias_value, w_out, bias_out, gain_attn, shift_attn, w_in, bias_in, w_back, bias_back, gain_ffn, shift_ffn, random_blocks, cotangent):
    params = (w_qkv.astype(jnp.float32), bias_query.astype(jnp.float32), bias_value.astype(jnp.float32), w_out.astype(jnp.float32), bias_out.astype(jnp.float32), gain_attn.astype(jnp.float32), shift_attn.astype(jnp.float32), w_in.astype(jnp.float32), bias_in.astype(jnp.float32), w_back.astype(jnp.float32), bias_back.astype(jnp.float32), gain_ffn.astype(jnp.float32), shift_ffn.astype(jnp.float32))
    start_totals = tuple((jnp.zeros(weight_arg.shape, jnp.float32) for weight_arg in params))

    def one_sequence(totals, inputs):
        token_rows, random_seq, cot_rows = inputs

        def forward(param_set, row_set):
            return encoder_layer(param_set, row_set, random_seq)
        outputs, pullback = jax.vjp(forward, params, token_rows.astype(jnp.float32))
        grad_params, grad_rows = pullback(cot_rows.astype(jnp.float32))
        totals = tuple((running + fresh_grad for running, fresh_grad in zip(totals, grad_params)))
        return (totals, (outputs.astype(jnp.bfloat16), grad_rows.astype(jnp.bfloat16)))
    totals, (layer_out, grad_tokens) = lax.scan(one_sequence, start_totals, (tokens, random_blocks, cotangent))
    grad_w_qkv, grad_bias_query, grad_bias_value, grad_w_out, grad_bias_out, grad_gain_attn, grad_shift_attn, grad_w_in, grad_bias_in, grad_w_back, grad_bias_back, grad_gain_ffn, grad_shift_ffn = totals
    return (layer_out, grad_tokens, grad_w_qkv, grad_bias_query, grad_bias_value, grad_w_out, grad_bias_out, grad_gain_attn, grad_shift_attn, grad_w_in, grad_bias_in, grad_w_back, grad_bias_back, grad_gain_ffn, grad_shift_ffn)
```

```python
import functools

import jax
import jax.numpy as jnp
from jax import lax
from jax.experimental import pallas as pl
from jax.experimental.pallas import tpu as pltpu
from jax.sharding import PartitionSpec as P

HEADS = 12
BLOCK = 64
HEAD_DIM = 64
TP = 4
GROUP = HEADS // TP
QUARTER = 256
LENGTH = TP * QUARTER
WIDTH = HEADS * HEAD_DIM
GROUP_WIDTH = GROUP * HEAD_DIM
SLOTS = 8
SLICE = WIDTH // SLOTS
CORE, X_BIT, Y_BIT = 1, 2, 4
PLANE_MASKS = (0, X_BIT, Y_BIT, X_BIT | Y_BIT)

epsilon = 1e-05
masked_score = -1e30
score_scale = HEAD_DIM ** (-0.5)
f32 = jnp.float32
bf16 = jnp.bfloat16

VMEM_LIMIT = 56 * 1024 * 1024


def mm(left, right):
    return jnp.dot(left, right, preferred_element_type=f32)


def mm_nt(left, right):
    return lax.dot_general(left, right, (((1,), (1,)), ((), ())), preferred_element_type=f32)


def total(*terms):
    acc = terms[0].astype(f32)
    for term in terms[1:]:
        acc = acc + term.astype(f32)
    return acc


def add_low(*terms):
    return total(*terms).astype(bf16)


def hop(array, dp_mask, z_mask):
    dp_count = lax.axis_size("dp")
    pairs = [
        (d * TP + z, (d ^ dp_mask) * TP + (z ^ z_mask)) for d in range(dp_count) for z in range(TP)
    ]
    return lax.ppermute(array, ("dp", "tp"), pairs)


def after(array, *others):
    return lax.optimization_barrier((array, *others))[0]


def place(array):
    dp_count = lax.axis_size("dp")
    pairs = []
    for d in range(dp_count):
        for z in range(TP):
            here = d * TP + z
            away = (d ^ CORE) * TP + (z ^ 2)
            pairs.append((here, here if (d & 1) == z // 2 else away))
    return lax.ppermute(array, ("dp", "tp"), pairs)


def block_bias(quarter, random_ref, head, chunk):
    shape = (LENGTH // BLOCK, QUARTER)
    row = lax.broadcasted_iota(jnp.int32, shape, 0)
    lane_block = lax.broadcasted_iota(jnp.int32, shape, 1) // BLOCK
    key_block = ((row // TP) ^ quarter) * TP + (row % TP)
    base = TP * (quarter ^ chunk)
    query_block = base + lane_block
    last = LENGTH // BLOCK - 1
    allowed = (key_block == 0) | (key_block == last)
    allowed |= (query_block == 0) | (query_block == last)
    allowed |= jnp.abs(key_block - query_block) <= 1
    for pick in range(3):
        chosen = jnp.zeros(shape, jnp.int32)
        for b in range(TP):
            value = random_ref[(head * (LENGTH // BLOCK) + base + b) * 3 + pick]
            chosen = jnp.where(lane_block == b, value, chosen)
        allowed |= key_block == chosen
    return jnp.where(allowed, 0.0, masked_score).astype(f32)


def biased(scores, bias):
    blocks = LENGTH // BLOCK
    spread = scores.reshape(blocks, BLOCK, QUARTER) + bias.reshape(blocks, 1, QUARTER)
    return spread.reshape(LENGTH, QUARTER)


def pack_heads(ref, pieces):
    ref[0:QUARTER, 0:64] = pieces[0]
    ref[0:QUARTER, 64:128] = pieces[1]
    ref[QUARTER:, 0:64] = pieces[2][: QUARTER // 2]
    ref[QUARTER:, 64:128] = pieces[2][QUARTER // 2 :]


def unpack_heads(ref):
    third = jnp.concatenate([ref[QUARTER:, 0:64], ref[QUARTER:, 64:128]], axis=0)
    return [ref[0:QUARTER, 0:64], ref[0:QUARTER, 64:128], third]


def attention_kernel(
    info, random_ref, t0, t1, t2, t3, w_ref, b_ref, a0, a1, a2, a3, q_ref, k_ref, v_ref, lse_ref, out_scr
):
    quarter = info[0]
    for slot, t_ref in enumerate((t0, t1, t2, t3)):
        rows = pl.ds(slot * QUARTER, QUARTER)
        proj = mm(t_ref[...], w_ref[...]) + b_ref[...]
        for h in range(GROUP):
            cols = slice(h * HEAD_DIM, (h + 1) * HEAD_DIM)
            q_ref[h, rows, :] = (proj[:, cols].astype(bf16).astype(f32) * score_scale).astype(bf16)
            k_ref[h, rows, :] = proj[:, GROUP_WIDTH:][:, cols].astype(bf16)
            v_ref[h, rows, :] = proj[:, 2 * GROUP_WIDTH :][:, cols].astype(bf16)
    for h in range(GROUP):
        keys = k_ref[h]
        values_t = v_ref[h].T

        def chunk_step(chunk, carry, h=h, keys=keys, values_t=values_t):
            rows = pl.ds(pl.multiple_of(chunk * QUARTER, QUARTER), QUARTER)
            scores = mm_nt(keys, q_ref[h, rows, :])
            scores = biased(scores, block_bias(quarter, random_ref, quarter * GROUP + h, chunk))
            row_max = jnp.max(scores, axis=0, keepdims=True)
            probs = jnp.exp(scores - row_max)
            row_sum = jnp.sum(probs, axis=0, keepdims=True)
            out_t = mm(values_t, probs.astype(bf16)) / row_sum
            out_scr[h, rows, :] = out_t.T.astype(bf16)
            lse_ref[pl.ds(h * TP + chunk, 1), :] = row_max + jnp.log(row_sum)
            return carry

        lax.fori_loop(0, TP, chunk_step, 0)
    for slot, a_ref in enumerate((a0, a1, a2, a3)):
        rows = slice(slot * QUARTER, (slot + 1) * QUARTER)
        pack_heads(a_ref, [out_scr[h, rows, :] for h in range(GROUP)])


def attention_back_kernel(
    info, random_ref, q_ref, k_ref, v_ref, lse_ref, g0, g1, g2, g3, gq_ref, sums_ref, do_scr, dk_scr, dv_scr, dq_scr
):
    quarter = info[0]
    for slot, g_ref in enumerate((g0, g1, g2, g3)):
        rows = slice(slot * QUARTER, (slot + 1) * QUARTER)
        for h, piece in enumerate(unpack_heads(g_ref)):
            do_scr[h, rows, :] = piece
    for h in range(GROUP):
        keys = k_ref[h]
        keys_t = keys.T
        values = v_ref[h]
        dk_scr[...] = jnp.zeros_like(dk_scr)
        dv_scr[...] = jnp.zeros_like(dv_scr)

        def chunk_step(chunk, carry, h=h, keys=keys, keys_t=keys_t, values=values):
            rows = pl.ds(pl.multiple_of(chunk * QUARTER, QUARTER), QUARTER)
            queries = q_ref[h, rows, :]
            grad_out = do_scr[h, rows, :]
            scores = mm_nt(keys, queries)
            scores = biased(scores, block_bias(quarter, random_ref, quarter * GROUP + h, chunk))
            probs = jnp.exp(scores - lse_ref[pl.ds(h * TP + chunk, 1), :])
            grad_probs = mm_nt(values, grad_out)
            delta = jnp.sum(probs * grad_probs, axis=0, keepdims=True)
            grad_scores = (probs * (grad_probs - delta)).astype(bf16)
            dv_scr[...] += mm(probs.astype(bf16), grad_out)
            dk_scr[...] += mm(grad_scores, queries)
            dq_t = mm(keys_t, grad_scores) * score_scale
            dq_scr[rows, :] = dq_t.T
            return carry

        lax.fori_loop(0, TP, chunk_step, 0)
        lo = h * HEAD_DIM
        gq_ref[:, lo : lo + HEAD_DIM] = dq_scr[...].astype(bf16)
        gq_ref[:, GROUP_WIDTH + lo : GROUP_WIDTH + lo + HEAD_DIM] = dk_scr[...].astype(bf16)
        gq_ref[:, 2 * GROUP_WIDTH + lo : 2 * GROUP_WIDTH + lo + HEAD_DIM] = dv_scr[...].astype(bf16)
    sums_ref[...] = jnp.zeros_like(sums_ref)
    sums_ref[0:1, :] = jnp.sum(gq_ref[...].astype(f32), axis=0, keepdims=True)


def ffn_kernel(
    info,
    t_ref,
    a0,
    a1,
    a2,
    a3,
    vec_in,
    bias_in_ref,
    cot_ref,
    w_out_hbm,
    w_in_hbm,
    w_back_hbm,
    *rest,
):
    sources = rest[: 2 * (TP - 1)]
    (
        lo_ref,
        g0,
        g1,
        g2,
        g3,
        gin_ref,
        x_ref,
        gb_ref,
        act_ref,
        gpre_ref,
        att_ref,
        gmix_ref,
        vec_ref,
        w_out_s,
        w_in_s,
        w_back_s,
        gp_scr,
        sems,
    ) = rest[2 * (TP - 1) :]
    quarter, mine, z_here = info[0], info[1], info[2]
    first = []
    for slot in range(TP):
        start = pl.multiple_of((quarter ^ slot) * GROUP_WIDTH, GROUP_WIDTH)
        first.append(
            pltpu.make_async_copy(
                w_out_hbm.at[pl.ds(start, GROUP_WIDTH), :],
                w_out_s.at[pl.ds(slot * GROUP_WIDTH, GROUP_WIDTH), :],
                sems.at[slot],
            )
        )
    first.append(pltpu.make_async_copy(w_in_hbm, w_in_s.at[0], sems.at[4]))
    first.append(pltpu.make_async_copy(w_back_hbm, w_back_s.at[0], sems.at[5]))
    held = (w_in_s, w_back_s)
    copies = [[] for _ in range(TP)]
    n = 6
    for q in range(1, TP):
        for side in range(2):
            source = sources[(q - 1) * 2 + side]
            for p in range(4):
                start = pl.multiple_of((mine ^ PLANE_MASKS[p] ^ side) * SLICE, SLICE)
                for part in range(2):
                    copies[q].append(
                        pltpu.make_async_copy(
                            source.at[p, part], held[part].at[q, pl.ds(start, SLICE), :], sems.at[n]
                        )
                    )
                    n += 1
    for copy in first + sum(copies, []):
        copy.start()

    bias_out, gain_one, shift_one = vec_in[0:1, :], vec_in[1:2, :], vec_in[2:3, :]
    bias_back, gain_two, shift_two = vec_in[3:4, :], vec_in[4:5, :], vec_in[5:6, :]
    for slot, a_ref in enumerate((a0, a1, a2, a3)):
        for h, piece in enumerate(unpack_heads(a_ref)):
            lo = slot * GROUP_WIDTH + h * HEAD_DIM
            att_ref[:, lo : lo + HEAD_DIM] = piece
    for copy in first[:4]:
        copy.wait()
    mixed = mm(att_ref[...], w_out_s[...]) + bias_out
    first_in = t_ref[...].astype(f32) + mixed

    def spread(h):
        centred = h - jnp.mean(h, axis=-1, keepdims=True)
        scale = lax.rsqrt(jnp.mean(centred * centred, axis=-1, keepdims=True) + epsilon)
        return centred * scale, scale

    def spread_back(grad, gain, normal, scale):
        weighted = grad * gain
        mean_one = jnp.mean(weighted, axis=-1, keepdims=True)
        mean_two = jnp.mean(weighted * normal, axis=-1, keepdims=True)
        return scale * (weighted - mean_one - normal * mean_two)

    normal_one, scale_one = spread(first_in)
    first_norm = normal_one * gain_one + shift_one
    x = first_norm.astype(bf16)
    x_ref[...] = x
    for copy in first[4:]:
        copy.wait()
    branch = jnp.zeros((QUARTER, WIDTH), f32)
    for q in range(TP):
        for copy in copies[q]:
            copy.wait()
        cols = slice(q * WIDTH, (q + 1) * WIDTH)
        bias_q = bias_in_ref[q : q + 1, :]
        pre = mm(x, w_in_s[q]) + bias_q
        inner = 0.7978845608028654 * (pre + 0.044715 * pre * pre * pre)
        tanh = jnp.tanh(inner)
        half = 0.5 * (1.0 + tanh)
        act = (pre * half).astype(bf16)
        act_ref[:, cols] = act
        slope = 0.7978845608028654 * (1.0 + 3.0 * 0.044715 * pre * pre)
        gp_scr[:, cols] = half + 0.5 * pre * (1.0 - tanh * tanh) * slope
        branch = branch + mm_nt(act, w_back_s[q])
    second_in = first_norm + branch + bias_back
    normal_two, scale_two = spread(second_in)
    lo_ref[...] = (normal_two * gain_two + shift_two).astype(bf16)
    grad_out = cot_ref[...].astype(f32)
    vec_ref[...] = jnp.zeros_like(vec_ref)
    vec_ref[0:1, :] = jnp.sum(grad_out, axis=0, keepdims=True)
    vec_ref[1:2, :] = jnp.sum(grad_out * normal_two, axis=0, keepdims=True)
    grad_second = spread_back(grad_out, gain_two, normal_two, scale_two)
    grad_branch = grad_second.astype(bf16)
    gb_ref[...] = grad_branch
    vec_ref[2:3, :] = jnp.sum(grad_branch.astype(f32), axis=0, keepdims=True)
    grad_first = grad_second
    for q in range(TP):
        cols = slice(q * WIDTH, (q + 1) * WIDTH)
        grad_pre = (mm(grad_branch, w_back_s[q]) * gp_scr[:, cols]).astype(bf16)
        gpre_ref[:, cols] = grad_pre
        vec_ref[pl.ds(6 + (z_here ^ q), 1), :] = jnp.sum(grad_pre.astype(f32), axis=0, keepdims=True)
        grad_first = grad_first + mm_nt(grad_pre, w_in_s[q])
    vec_ref[3:4, :] = jnp.sum(grad_first, axis=0, keepdims=True)
    vec_ref[4:5, :] = jnp.sum(grad_first * normal_one, axis=0, keepdims=True)
    grad_in = spread_back(grad_first, gain_one, normal_one, scale_one)
    gin_ref[...] = grad_in
    grad_mixed = grad_in.astype(bf16)
    gmix_ref[...] = grad_mixed
    vec_ref[5:6, :] = jnp.sum(grad_mixed.astype(f32), axis=0, keepdims=True)
    grad_att = mm_nt(grad_mixed, w_out_s[...]).astype(bf16)
    for slot, g_ref in enumerate((g0, g1, g2, g3)):
        lo = slot * GROUP_WIDTH
        pack_heads(
            g_ref, [grad_att[:, lo + h * HEAD_DIM : lo + (h + 1) * HEAD_DIM] for h in range(GROUP)]
        )


def position_mask(position, order):
    mask = 0
    for n, bit in enumerate(order):
        if (position >> (2 - n)) & 1:
            mask |= bit
    return mask


ORDER_A = (CORE, X_BIT, Y_BIT)
ORDER_B = (CORE, Y_BIT, X_BIT)


def weight_grad_kernel(
    info,
    x_ref,
    gb_ref,
    act_ref,
    gpre_ref,
    att_ref,
    gmix_ref,
    ga_keep,
    ga_send,
    gb_keep,
    gb_send,
    go_keep,
    go_send,
    flip_scr,
    lhs_scr,
):
    mine = info[1]
    for left, right, keep, send, order in (
        (gb_ref, act_ref, gb_keep, gb_send, ORDER_B),
        (x_ref, gpre_ref, ga_keep, ga_send, ORDER_A),
    ):
        flip_scr[...] = left[...].T
        for p in range(SLOTS):
            start = pl.multiple_of((mine ^ position_mask(p, order)) * SLICE, SLICE)
            lhs_scr[p * SLICE : (p + 1) * SLICE, :] = flip_scr[pl.ds(start, SLICE), :]
        for q in range(TP):
            product = mm(lhs_scr[...], right[:, q * WIDTH : (q + 1) * WIDTH]).astype(bf16)
            for p in range(SLOTS):
                out = send if p >= SLOTS // 2 else keep
                out[p % (SLOTS // 2), q] = product[p * SLICE : (p + 1) * SLICE, :]
    product = mm(gmix_ref[...].T, att_ref[...]).astype(bf16)
    go_keep[...] = product[:, : 2 * GROUP_WIDTH]
    go_send[...] = product[:, 2 * GROUP_WIDTH :]


ORDER_LA = (4, 2, 1)
ORDER_LB = (2, 4, 1)


VEC_ROWS = 16
HALF = WIDTH // 2
HELD = SLOTS // 2 * SLICE


def flip_kernel(t0, t1, t2, t3, out_ref):
    for slot, t_ref in enumerate((t0, t1, t2, t3)):
        out_ref[:, slot * QUARTER : (slot + 1) * QUARTER] = t_ref[...].T


def qkv_grad_kernel(
    info, tokens_t, gq_ref, go_ref, vec_ref, sums_ref, la_keep, la_send, lb_keep, lb_send, out_scr
):
    quarter, here = info[0], info[3]
    out_scr[:, : 3 * GROUP_WIDTH] = mm(tokens_t[...], gq_ref[...]).astype(bf16)
    out_scr[:, 3 * GROUP_WIDTH :] = go_ref[...]
    for keep, send, order, lo in (
        (la_keep, la_send, ORDER_LA, 0),
        (lb_keep, lb_send, ORDER_LB, HALF),
    ):
        for p in range(SLOTS):
            start = pl.multiple_of((here ^ position_mask(p, order)) * SLICE, SLICE)
            out = send if p >= SLOTS // 2 else keep
            row = p % (SLOTS // 2) * SLICE
            out[row : row + SLICE, :] = out_scr[pl.ds(start, SLICE), lo : lo + HALF]
    sums = sums_ref[0:1, :]
    placed = []
    for kind in (0, 2):
        piece = sums[:, kind * GROUP_WIDTH : (kind + 1) * GROUP_WIDTH]
        placed.append(
            jnp.concatenate([jnp.where(quarter == g, piece, 0.0) for g in range(TP)], axis=1)
        )
    vectors = jnp.concatenate([vec_ref[0:10, :]] + placed + [vec_ref[12:VEC_ROWS, :]], axis=0)
    vectors = vectors.astype(bf16)
    for out in (la_keep, la_send):
        out[HELD : HELD + VEC_ROWS, :] = vectors[:, :HALF]
        out[HELD + VEC_ROWS :, :] = vectors[:, HALF:]


def token_grad_kernel(gq_ref, w_ref, keep_ref, send_ref):
    half = LENGTH // 2
    keep_ref[...] = mm_nt(gq_ref[:half, :], w_ref[...]).astype(bf16)
    send_ref[...] = mm_nt(gq_ref[half:, :], w_ref[...]).astype(bf16)


def ffn_out_kernel(info, f_ref, f_other, w_in_out, w_back_out, flip_scr):
    mine = info[1]
    for side, ref in enumerate((f_ref, f_other)):
        for place_xy in range(4):
            mask = side | (X_BIT if place_xy & 1 else 0) | (Y_BIT if place_xy & 2 else 0)
            start = pl.multiple_of((mine ^ mask) * SLICE, SLICE)
            w_in_out[pl.ds(start, SLICE), :] = ref[place_xy, 0].astype(f32)
            flip_scr[pl.ds(start, SLICE), :] = ref[place_xy, 1].astype(f32)
    w_back_out[...] = flip_scr[...].T


def qkv_out_kernel(info, c_ref, c_other, qkv_out, out_out, *rest):
    vec_outs, (all_scr, flip_scr) = rest[:9], rest[9:]
    quarter, z_here, here = info[0], info[2], info[3]
    count = 16 * SLICE
    for side, ref in enumerate((c_ref, c_other)):
        for n in range(16):
            all_scr[side * 16 + n] = ref[n * SLICE : (n + 1) * SLICE, :]
    vectors = total(c_ref[count:, :], c_other[count:, :])
    bias_in = jnp.zeros((1, WIDTH), f32)
    for q in range(TP):
        bias_in = jnp.where(z_here == q, vectors[6 + q : 7 + q, :], bias_in)
    for out, n in zip(vec_outs[:8], (0, 1, 2, 3, 4, 5, 10, 11)):
        out[...] = vectors[n]
    vec_outs[8][...] = bias_in[0]
    for block in range(SLOTS):
        pieces = []
        for group in range(TP):
            group_off = quarter ^ group
            block_off = here ^ block
            xy = ((block_off >> 2) & 1) + (block_off & 2)
            z_off = (group_off & 1) + 2 * (block_off & 1)
            slot = (group_off >> 1) * 16 + xy * 4 + z_off
            pieces.append(all_scr[slot])
        rows = slice(block * SLICE, (block + 1) * SLICE)
        for kind in range(4):
            cols = slice(kind * GROUP_WIDTH, (kind + 1) * GROUP_WIDTH)
            joined = jnp.concatenate([piece[:, cols] for piece in pieces], axis=1).astype(f32)
            if kind < 3:
                qkv_out[rows, kind * WIDTH : (kind + 1) * WIDTH] = joined
            else:
                flip_scr[rows, :] = joined
    out_out[...] = flip_scr[...].T


VMEM = pl.BlockSpec(memory_space=pltpu.VMEM)
SMEM = pl.BlockSpec(memory_space=pltpu.SMEM)
HBM = pl.BlockSpec(memory_space=pl.ANY)


def call(kernel, in_specs, outs, scratch, flops, moved, name):
    return pl.pallas_call(
        kernel,
        out_shape=[jax.ShapeDtypeStruct(shape, dtype) for shape, dtype in outs],
        in_specs=in_specs,
        out_specs=[VMEM] * len(outs),
        scratch_shapes=scratch,
        compiler_params=pltpu.CompilerParams(vmem_limit_bytes=VMEM_LIMIT),
        cost_estimate=pl.CostEstimate(flops=flops, bytes_accessed=moved, transcendentals=0),
        name=name,
    )


def per_device(
    tokens,
    w_qkv,
    bias_query,
    bias_value,
    w_out,
    bias_out,
    gain_attn,
    shift_attn,
    w_in,
    bias_in,
    w_back,
    bias_back,
    gain_ffn,
    shift_ffn,
    random_blocks,
    cotangent,
):
    dp_count = lax.axis_size("dp")
    d = lax.axis_index("dp")
    z = lax.axis_index("tp")
    core = d & 1
    quarter = (z & 1) + 2 * core
    mine = d & (SLOTS - 1)
    here = ((d >> 1) & 1) * 4 + ((d >> 2) & 1) * 2 + (z >> 1)
    info = jnp.stack([quarter, mine, z, here]).astype(jnp.int32)
    extra_bits = [1 << b for b in range(3, dp_count.bit_length() - 1)]

    own_tokens = place(tokens[0])
    random_here = place(random_blocks).reshape(-1)
    near_tokens = hop(own_tokens, 0, 1)
    core_tokens = hop(own_tokens, CORE, 0)
    far_tokens = hop(near_tokens, CORE, 0)
    token_slots = (own_tokens, near_tokens, core_tokens, far_tokens)

    w_back_t = w_back.T
    piece = jnp.stack(
        [
            lax.dynamic_slice_in_dim(w_in, mine * SLICE, SLICE, 0),
            lax.dynamic_slice_in_dim(w_back_t, mine * SLICE, SLICE, 0),
        ]
    )
    bias_piece = jnp.broadcast_to(bias_in[None], (16, WIDTH))

    def spread_plane(own, by_rows):
        by_x = hop(own, X_BIT, 0)
        by_y = hop(own, Y_BIT, 0)
        diag = hop(by_x, Y_BIT, 0) if by_rows else hop(by_y, X_BIT, 0)
        held = jnp.stack([own, by_x, by_y, diag])
        return [held, hop(held, CORE, 0)]

    sources = spread_plane(hop(piece, 0, 1), True)
    piece_two = hop(after(piece, own_tokens), 0, 2)
    piece_three = hop(after(piece, near_tokens), 0, 3)
    bias_all = [bias_piece] + [hop(after(bias_piece, near_tokens), 0, q) for q in range(1, TP)]

    start = quarter * GROUP_WIDTH

    def group_cols(array, kind):
        return lax.dynamic_slice_in_dim(array, kind * WIDTH + start, GROUP_WIDTH, 1)

    w_group = jnp.concatenate([group_cols(w_qkv, kind) for kind in range(3)], axis=1)
    bias_query_group = lax.dynamic_slice_in_dim(bias_query, start, GROUP_WIDTH, 0)
    bias_value_group = lax.dynamic_slice_in_dim(bias_value, start, GROUP_WIDTH, 0)
    bias_group = jnp.concatenate(
        [bias_query_group, jnp.zeros_like(bias_query_group), bias_value_group]
    ).astype(f32)[None]
    packed = ((QUARTER + QUARTER // 2, 2 * HEAD_DIM), bf16)
    per_head = ((GROUP, LENGTH, HEAD_DIM), bf16)
    a0, a1, a2, a3, queries, keys, values, lse = call(
        attention_kernel,
        [SMEM, SMEM] + [VMEM] * 6,
        [packed] * 4 + [per_head] * 3 + [((16, QUARTER), f32)],
        [pltpu.VMEM((GROUP, LENGTH, HEAD_DIM), bf16)],
        2 * 10**9,
        8 * 10**6,
        "attention",
    )(info, random_here, *token_slots, w_group, bias_group)
    a0_done = a0
    a1 = hop(a1, 0, 1)
    a2 = hop(a2, CORE, 0)
    a3 = hop(a3, CORE, 1)
    tokens_t = call(
        flip_kernel, [VMEM] * 4, [((WIDTH, LENGTH), bf16)], [], 0, 3 * 10**6, "flip_tokens"
    )(after(own_tokens, a0_done), near_tokens, core_tokens, far_tokens)[0]
    cot = place(after(cotangent[0], a0_done))
    sources += spread_plane(after(piece_two, a0_done), False)
    sources += spread_plane(after(piece_three, a0_done), True)
    bias_all = jnp.concatenate([bias[:1] for bias in bias_all]).astype(f32)

    vec_in = jnp.stack(
        [bias_out, gain_attn, shift_attn, bias_back, gain_ffn, shift_ffn, bias_out, bias_out]
    ).astype(f32)
    rows = ((QUARTER, WIDTH), bf16)
    wide = ((QUARTER, TP * WIDTH), bf16)
    (
        out_here,
        g0,
        g1,
        g2,
        g3,
        grad_in,
        ffn_input,
        grad_branch,
        activated,
        grad_pre,
        attended,
        grad_mixed,
        vectors,
    ) = call(
        ffn_kernel,
        [SMEM] + [VMEM] * 8 + [HBM] * 9,
        [rows] + [packed] * 4 + [((QUARTER, WIDTH), f32), rows, rows, wide, wide, rows, rows, ((16, WIDTH), f32)],
        [
            pltpu.VMEM((WIDTH, WIDTH), bf16),
            pltpu.VMEM((TP, WIDTH, WIDTH), bf16),
            pltpu.VMEM((TP, WIDTH, WIDTH), bf16),
            pltpu.VMEM((QUARTER, TP * WIDTH), f32),
            pltpu.SemaphoreType.DMA((6 + 16 * (TP - 1),)),
        ],
        6 * 10**9,
        25 * 10**6,
        "ffn",
    )(info, own_tokens, a0, a1, a2, a3, vec_in, bias_all, cot, w_out, w_in, w_back_t, *sources)
    g1 = hop(g1, 0, 1)
    g2 = hop(g2, CORE, 0)
    g3 = hop(g3, CORE, 1)

    quads = ((SLOTS // 2, TP, SLICE, WIDTH), bf16)
    halves = ((WIDTH, 2 * GROUP_WIDTH), bf16)
    ga_keep, ga_send, gb_keep, gb_send, go_keep, go_send = call(
        weight_grad_kernel,
        [SMEM] + [VMEM] * 6,
        [quads] * 4 + [halves] * 2,
        [pltpu.VMEM((WIDTH, QUARTER), bf16), pltpu.VMEM((WIDTH, QUARTER), bf16)],
        3 * 10**9,
        14 * 10**6,
        "weight_grads",
    )(info, ffn_input, grad_branch, activated, grad_pre, attended, grad_mixed)

    grad_qkv, qkv_sums = call(
        attention_back_kernel,
        [SMEM, SMEM] + [VMEM] * 8,
        [((LENGTH, 3 * GROUP_WIDTH), bf16), ((8, 3 * GROUP_WIDTH), f32)],
        [
            pltpu.VMEM((GROUP, LENGTH, HEAD_DIM), bf16),
            pltpu.VMEM((LENGTH, HEAD_DIM), f32),
            pltpu.VMEM((LENGTH, HEAD_DIM), f32),
            pltpu.VMEM((LENGTH, HEAD_DIM), f32),
        ],
        4 * 10**9,
        8 * 10**6,
        "attention_back",
    )(info, random_here, queries, keys, values, lse, g0, g1, g2, g3)

    layer_out = place(after(out_here, grad_qkv))[None]

    go_other = hop(go_send, CORE, 0)
    go_near = hop(add_low(go_keep, go_other)[:, GROUP_WIDTH:], 0, 1)
    go_here = add_low(go_keep[:, :GROUP_WIDTH], go_other[:, :GROUP_WIDTH], go_near)

    la_keep, la_send, lb_keep, lb_send = call(
        qkv_grad_kernel,
        [SMEM] + [VMEM] * 5,
        [((HELD + 2 * VEC_ROWS, HALF), bf16)] * 2 + [((HELD, HALF), bf16)] * 2,
        [pltpu.VMEM((WIDTH, 4 * GROUP_WIDTH), bf16)],
        10**9,
        5 * 10**6,
        "qkv_grads",
    )(info, tokens_t, grad_qkv, go_here, vectors, qkv_sums)
    ra = hop(la_send, X_BIT, 0)
    rb = hop(lb_send, Y_BIT, 0)
    two = 2 * SLICE
    ra2 = hop(add_low(la_keep[two:], ra[two:]), Y_BIT, 0)
    rb2 = hop(add_low(lb_keep[two:], rb[two:]), X_BIT, 0)

    def joined(slot):
        rows = slice(slot * SLICE, (slot + 1) * SLICE)
        both = jnp.concatenate(
            [total(la_keep[rows], ra[rows], ra2[rows]), total(lb_keep[rows], rb[rows], rb2[rows])],
            axis=1,
        )
        vec = total(la_keep[HELD:], ra[HELD:], ra2[two:])
        vec = jnp.concatenate([vec[:VEC_ROWS], vec[VEC_ROWS:]], axis=1)
        return jnp.concatenate([both, vec]).astype(bf16)

    sum_l = add_low(joined(0), hop(joined(1), 0, 2))
    for bit in extra_bits:
        sum_l = add_low(sum_l, hop(sum_l, bit, 0))
    z_one, z_two, z_three = hop(sum_l, 0, 1), hop(sum_l, 0, 2), hop(sum_l, 0, 3)
    by_z = jnp.concatenate([part[:SLICE] for part in (sum_l, z_one, z_two, z_three)])
    vec = add_low(sum_l[SLICE:], z_one[SLICE:])
    z_x = hop(by_z, X_BIT, 0)
    z_y = hop(by_z, Y_BIT, 0)
    z_d0 = hop(z_x[:two], Y_BIT, 0)
    z_d1 = hop(z_y[two:], X_BIT, 0)
    plane = jnp.concatenate([by_z, z_x, z_y, z_d0, z_d1, vec])
    grad_w_qkv, grad_w_out, *vec_outs = call(
        qkv_out_kernel,
        [SMEM, VMEM, VMEM],
        [((WIDTH, 3 * WIDTH), f32), ((WIDTH, WIDTH), f32)] + [((WIDTH,), f32)] * 9,
        [pltpu.VMEM((32, SLICE, WIDTH), bf16), pltpu.VMEM((WIDTH, WIDTH), f32)],
        10**6,
        14 * 10**6,
        "qkv_out",
    )(info, plane, hop(plane, CORE, 0))

    keep, send = call(
        token_grad_kernel,
        [VMEM, VMEM],
        [((LENGTH // 2, WIDTH), bf16)] * 2,
        [],
        10**9,
        4 * 10**6,
        "token_grad",
    )(grad_qkv, w_group)
    other = hop(send, CORE, 0)
    near = hop(add_low(keep[QUARTER:], other[QUARTER:]), 0, 1)
    grad_tokens = place(add_low(keep[:QUARTER], other[:QUARTER], near, grad_in))[None]

    ra = hop(ga_send, CORE, 0)
    rb = hop(gb_send, CORE, 0)
    xa = hop(add_low(ga_keep[2:], ra[2:]), X_BIT, 0)
    yb = hop(add_low(gb_keep[2:], rb[2:]), Y_BIT, 0)
    ya = hop(add_low(ga_keep[1], ra[1], xa[1]), Y_BIT, 0)
    xb = hop(add_low(gb_keep[1], rb[1], yb[1]), X_BIT, 0)

    def both(q):
        return jnp.stack(
            [
                total(ga_keep[0, q], ra[0, q], xa[0, q], ya[q]),
                total(gb_keep[0, q], rb[0, q], yb[0, q], xb[q]),
            ]
        )

    parts = [hop(both(q).astype(bf16), 0, q) for q in range(1, TP)]
    sum_f = add_low(both(0), *parts)
    for bit in extra_bits:
        sum_f = add_low(sum_f, hop(sum_f, bit, 0))
    f_x = hop(sum_f, X_BIT, 0)
    f_y = hop(sum_f, Y_BIT, 0)
    f_d = jnp.stack([hop(f_x[0], Y_BIT, 0), hop(f_y[1], X_BIT, 0)])
    f_all = jnp.stack([sum_f, f_x, f_y, f_d])
    grad_w_in, grad_w_back = call(
        ffn_out_kernel,
        [SMEM, VMEM, VMEM],
        [((WIDTH, WIDTH), f32)] * 2,
        [pltpu.VMEM((WIDTH, WIDTH), f32)],
        10**6,
        7 * 10**6,
        "ffn_out",
    )(info, f_all, hop(f_all, CORE, 0))

    (
        grad_shift_ffn,
        grad_gain_ffn,
        grad_bias_back,
        grad_shift_attn,
        grad_gain_attn,
        grad_bias_out,
        grad_bias_query,
        grad_bias_value,
        grad_bias_in,
    ) = vec_outs
    return (
        layer_out,
        grad_tokens,
        grad_w_qkv,
        grad_bias_query,
        grad_bias_value,
        grad_w_out,
        grad_bias_out,
        grad_gain_attn,
        grad_shift_attn,
        grad_w_in,
        grad_bias_in,
        grad_w_back,
        grad_bias_back,
        grad_gain_ffn,
        grad_shift_ffn,
    )


def solution(mesh):
    in_specs = (
        P("dp", "tp", None),
        P(),
        P(),
        P(),
        P(),
        P(),
        P(),
        P(),
        P(None, "tp"),
        P("tp"),
        P("tp", None),
        P(),
        P(),
        P(),
        P("dp", None, None, None),
        P("dp", "tp", None),
    )
    out_specs = (
        P("dp", "tp", None),
        P("dp", "tp", None),
        P(),
        P(),
        P(),
        P(),
        P(),
        P(),
        P(),
        P(None, "tp"),
        P("tp"),
        P("tp", None),
        P(),
        P(),
        P(),
    )
    return jax.shard_map(
        per_device, mesh=mesh, in_specs=in_specs, out_specs=out_specs, check_vma=False
    )
```

```python
import functools

import jax
import jax.numpy as jnp
from jax import lax
from jax.experimental import pallas as pl
from jax.experimental.pallas import tpu as pltpu
from jax.sharding import PartitionSpec as P

HEADS = 12
BLOCK = 64
HEAD_DIM = 64
TP = 4
GROUP = HEADS // TP
QUARTER = 256
LENGTH = TP * QUARTER
WIDTH = HEADS * HEAD_DIM
GROUP_WIDTH = GROUP * HEAD_DIM
SLOTS = 8
SLICE = WIDTH // SLOTS
VEC_ROWS = 16
CORE, X_BIT, Y_BIT = 1, 2, 4
PLANE_MASKS = (0, X_BIT, Y_BIT, X_BIT | Y_BIT)

epsilon = 1e-05
masked_score = -1e30
score_scale = HEAD_DIM ** (-0.5)
f32 = jnp.float32
bf16 = jnp.bfloat16


def mm(left, right):
    return jnp.dot(left, right, preferred_element_type=f32)


def mm_nt(left, right):
    return lax.dot_general(left, right, (((1,), (1,)), ((), ())), preferred_element_type=f32)


def total(*terms):
    acc = terms[0].astype(f32)
    for term in terms[1:]:
        acc = acc + term.astype(f32)
    return acc


def add_low(*terms):
    return total(*terms).astype(bf16)


def hop(array, dp_mask, z_mask):
    dp_count = lax.axis_size("dp")
    pairs = [
        (d * TP + z, (d ^ dp_mask) * TP + (z ^ z_mask)) for d in range(dp_count) for z in range(TP)
    ]
    return lax.ppermute(array, ("dp", "tp"), pairs)


def place(array):
    dp_count = lax.axis_size("dp")
    pairs = []
    for d in range(dp_count):
        for z in range(TP):
            here = d * TP + z
            away = (d ^ CORE) * TP + (z ^ 2)
            pairs.append((here, here if (d & 1) == z // 2 else away))
    return lax.ppermute(array, ("dp", "tp"), pairs)


def piece_kernel(info, w_in_hbm, w_back_ref, bias_ref, piece_ref, flip_scr, sem):
    start = pl.multiple_of(info[1] * SLICE, SLICE)
    copy = pltpu.make_async_copy(
        w_in_hbm.at[pl.ds(start, SLICE), :], piece_ref.at[pl.ds(0, SLICE), :], sem
    )
    copy.start()
    flip_scr[...] = w_back_ref[...].T
    piece_ref[SLICE : 2 * SLICE, :] = flip_scr[pl.ds(start, SLICE), :]
    bias = bias_ref[...].astype(f32).reshape(1, WIDTH)
    piece_ref[2 * SLICE :, :] = jnp.broadcast_to(bias, (VEC_ROWS, WIDTH)).astype(bf16)
    copy.wait()


def group_kernel(info, w_ref, bias_query_ref, bias_value_ref, w_out, b_out):
    bias_query = bias_query_ref[...].astype(f32).reshape(1, WIDTH)
    bias_value = bias_value_ref[...].astype(f32).reshape(1, WIDTH)
    b_out[...] = jnp.zeros_like(b_out)
    for g in range(TP):

        @pl.when(info[0] == g)
        def _(g=g):
            cols = slice(g * GROUP_WIDTH, (g + 1) * GROUP_WIDTH)
            for kind in range(3):
                lo = kind * GROUP_WIDTH
                w_out[:, lo : lo + GROUP_WIDTH] = w_ref[:, kind * WIDTH :][:, cols]
            b_out[:, :GROUP_WIDTH] = bias_query[:, cols]
            b_out[:, 2 * GROUP_WIDTH :] = bias_value[:, cols]


def block_bias(quarter, native, random_refs, head, chunk):
    shape = (LENGTH // BLOCK, QUARTER)
    row = lax.broadcasted_iota(jnp.int32, shape, 0)
    lane_block = lax.broadcasted_iota(jnp.int32, shape, 1) // BLOCK
    key_block = ((row // TP) ^ quarter) * TP + (row % TP)
    base = TP * (quarter ^ chunk)
    query_block = base + lane_block
    last = LENGTH // BLOCK - 1
    allowed = (key_block == 0) | (key_block == last)
    allowed |= (query_block == 0) | (query_block == last)
    allowed |= jnp.abs(key_block - query_block) <= 1
    for pick in range(3):
        chosen = jnp.zeros(shape, jnp.int32)
        for b in range(TP):
            at = (head * (LENGTH // BLOCK) + base + b) * 3 + pick
            value = jnp.where(native == 1, random_refs[0][at], random_refs[1][at])
            chosen = jnp.where(lane_block == b, value, chosen)
        allowed |= key_block == chosen
    return jnp.where(allowed, 0.0, masked_score).astype(f32)


def biased(scores, bias):
    blocks = LENGTH // BLOCK
    spread = scores.reshape(blocks, BLOCK, QUARTER) + bias.reshape(blocks, 1, QUARTER)
    return spread.reshape(LENGTH, QUARTER)


PACKED = QUARTER + QUARTER // 2


def pack_heads(ref, row, pieces):
    end = row + QUARTER
    ref[row:end, 0:64] = pieces[0]
    ref[row:end, 64:128] = pieces[1]
    ref[end : row + PACKED, 0:64] = pieces[2][: QUARTER // 2]
    ref[end : row + PACKED, 64:128] = pieces[2][QUARTER // 2 :]


def unpack_heads(ref, row):
    end = row + QUARTER
    third = jnp.concatenate([ref[end : row + PACKED, 0:64], ref[end : row + PACKED, 64:128]], axis=0)
    return [ref[row:end, 0:64], ref[row:end, 64:128], third]


def attention_kernel(info, rnd_own, rnd_other, t0, t1, t2, t3, w_ref, b_ref, a0, a13, a2, *rest):
    heads, lse_ref, out_scr = rest[:9], rest[9], rest[10]
    quarter, native = info[0], info[4]
    for slot, t_ref in enumerate((t0, t1, t2, t3)):
        rows = pl.ds(slot * QUARTER, QUARTER)
        proj = mm(t_ref[...], w_ref[...]) + b_ref[...]
        for h in range(GROUP):
            for kind in range(3):
                lo = kind * GROUP_WIDTH + h * HEAD_DIM
                piece = proj[:, lo : lo + HEAD_DIM].astype(bf16)
                if kind == 0:
                    piece = (piece.astype(f32) * score_scale).astype(bf16)
                heads[3 * h + kind][rows, :] = piece
    for h in range(GROUP):
        q_ref, k_ref, v_ref = heads[3 * h : 3 * h + 3]
        keys = k_ref[...]
        values_t = v_ref[...].T

        def chunk_step(chunk, carry, h=h, q_ref=q_ref, keys=keys, values_t=values_t):
            rows = pl.ds(pl.multiple_of(chunk * QUARTER, QUARTER), QUARTER)
            scores = mm_nt(keys, q_ref[rows, :])
            head = quarter * GROUP + h
            scores = biased(scores, block_bias(quarter, native, (rnd_own, rnd_other), head, chunk))
            row_max = jnp.max(scores, axis=0, keepdims=True)
            probs = jnp.exp(scores - row_max)
            row_sum = jnp.sum(probs, axis=0, keepdims=True)
            out_t = mm(values_t, probs.astype(bf16)) / row_sum
            out_scr[h, rows, :] = out_t.T.astype(bf16)
            lse_ref[pl.ds(h * TP + chunk, 1), :] = row_max + jnp.log(row_sum)
            return carry

        lax.fori_loop(0, TP, chunk_step, 0, unroll=True)
    for slot, (a_ref, row) in enumerate(((a0, 0), (a13, 0), (a2, 0), (a13, PACKED))):
        rows = slice(slot * QUARTER, (slot + 1) * QUARTER)
        pack_heads(a_ref, row, [out_scr[h, rows, :] for h in range(GROUP)])


def attention_back_kernel(
    h, info, rnd_own, rnd_other, q_ref, k_ref, v_ref, lse_ref, g0, g1, g2, g3, out_ref, sums_ref, do_scr, dk_scr, dv_scr, dq_scr
):
    quarter, native = info[0], info[4]
    for slot, g_ref in enumerate((g0, g1, g2, g3)):
        do_scr[slot * QUARTER : (slot + 1) * QUARTER, :] = unpack_heads(g_ref, 0)[h]
    keys = k_ref[...]
    keys_t = keys.T
    values = v_ref[...]
    dk_scr[...] = jnp.zeros_like(dk_scr)
    dv_scr[...] = jnp.zeros_like(dv_scr)

    def chunk_step(chunk, carry):
        rows = pl.ds(pl.multiple_of(chunk * QUARTER, QUARTER), QUARTER)
        queries = q_ref[rows, :]
        grad_out = do_scr[rows, :]
        scores = mm_nt(keys, queries)
        head = quarter * GROUP + h
        scores = biased(scores, block_bias(quarter, native, (rnd_own, rnd_other), head, chunk))
        probs = jnp.exp(scores - lse_ref[pl.ds(h * TP + chunk, 1), :])
        grad_probs = mm_nt(values, grad_out)
        delta = jnp.sum(probs * grad_probs, axis=0, keepdims=True)
        grad_scores = (probs * (grad_probs - delta)).astype(bf16)
        dv_scr[...] += mm(probs.astype(bf16), grad_out)
        dk_scr[...] += mm(grad_scores, queries)
        dq_t = mm(keys_t, grad_scores) * score_scale
        dq_scr[rows, :] = dq_t.T
        return carry

    lax.fori_loop(0, TP, chunk_step, 0, unroll=True)
    for n, scr in enumerate((dq_scr, dk_scr, dv_scr)):
        out_ref[:, n * HEAD_DIM : (n + 1) * HEAD_DIM] = scr[...].astype(bf16)
    sums_ref[...] = jnp.zeros_like(sums_ref)
    sums_ref[0:1, :] = jnp.sum(out_ref[...].astype(f32), axis=0, keepdims=True)


PIECE = 2 * SLICE + VEC_ROWS


def held_kernel(own, by_x, by_y, third, third_x, third_y, out):
    for q in range(2):
        for p, ref in enumerate((own, by_x, by_y)):
            at = (4 * q + p) * PIECE
            out[at : at + PIECE] = ref[q * PIECE : (q + 1) * PIECE]
        at = (4 * q + 3) * PIECE
        out[at : at + CUT] = third_y[PIECE + q * CUT : PIECE + (q + 1) * CUT]
        out[at + CUT : at + PIECE] = third_x[PIECE + q * (PIECE - CUT) : PIECE + (q + 1) * (PIECE - CUT)]
    for p, ref in enumerate((third, third_x, third_y)):
        at = (8 + p) * PIECE
        out[at : at + PIECE] = ref[:PIECE]


def assemble_kernel(info, held, other, last_in, last_back, other_last, w_out_ref, w_in_s, w_back_s, w_out_s, bias_s):
    quarter, mine = info[0], info[1]
    for slot in range(TP):
        start = pl.multiple_of((quarter ^ slot) * GROUP_WIDTH, GROUP_WIDTH)
        w_out_s[slot * GROUP_WIDTH : (slot + 1) * GROUP_WIDTH, :] = w_out_ref[pl.ds(start, GROUP_WIDTH), :]
    for side, main in enumerate((held, other)):
        for q in range(TP - 1):
            for p in range(4):
                start = pl.multiple_of((mine ^ PLANE_MASKS[p] ^ side) * SLICE, SLICE)
                at = (4 * q + p) * PIECE
                if q == TP - 2 and p == 3:
                    left = other_last[:SLICE] if side else last_in[...]
                    right = other_last[SLICE : 2 * SLICE] if side else last_back[:SLICE]
                else:
                    left, right = main[at : at + SLICE], main[at + SLICE : at + 2 * SLICE]
                w_in_s[q, pl.ds(start, SLICE), :] = left
                w_back_s[q, pl.ds(start, SLICE), :] = right
                if p == 0 and side == 0:
                    bias_s[q] = main[at + 2 * SLICE : at + PIECE]


def row(ref):
    return ref[...].astype(f32).reshape(1, WIDTH)


def spread(h):
    centred = h - jnp.mean(h, axis=-1, keepdims=True)
    scale = lax.rsqrt(jnp.mean(centred * centred, axis=-1, keepdims=True) + epsilon)
    return centred * scale, scale


def spread_back(grad, gain, normal, scale):
    weighted = grad * gain
    mean_one = jnp.mean(weighted, axis=-1, keepdims=True)
    mean_two = jnp.mean(weighted * normal, axis=-1, keepdims=True)
    return scale * (weighted - mean_one - normal * mean_two)


def ffn_kernel(info, t_ref, a0, a1, a2, a3, *rest):
    bias_out_ref, gain_one_ref, shift_one_ref, bias_back_ref, gain_two_ref, shift_two_ref, bias_in_ref = rest[:7]
    cot_ref, w_out_s, w_in_ref, w_back_ref, w_in_s, w_back_s, bias_s = rest[7:14]
    lo_ref, first_ref, second_ref, x_ref, gb_ref, act_ref, gp_ref, att_ref, vec_ref = rest[14:]
    for slot, a_ref in enumerate((a0, a1, a2, a3)):
        for h, piece in enumerate(unpack_heads(a_ref, 0)):
            lo = slot * GROUP_WIDTH + h * HEAD_DIM
            att_ref[:, lo : lo + HEAD_DIM] = piece
    first_in = t_ref[...].astype(f32) + (mm(att_ref[...], w_out_s[...]) + row(bias_out_ref))
    first_ref[...] = first_in
    first_norm = spread(first_in)[0] * row(gain_one_ref) + row(shift_one_ref)
    x = first_norm.astype(bf16)
    x_ref[...] = x
    branch = jnp.zeros((QUARTER, WIDTH), f32)
    for q in range(TP):
        cols = slice(q * WIDTH, (q + 1) * WIDTH)
        bias_q = bias_s[q - 1, 0:1, :].astype(f32) if q else row(bias_in_ref)
        pre = mm(x, w_in_s[q - 1] if q else w_in_ref[...]) + bias_q
        inner = 0.7978845608028654 * (pre + 0.044715 * pre * pre * pre)
        tanh = jnp.tanh(inner)
        half = 0.5 * (1.0 + tanh)
        act = (pre * half).astype(bf16)
        act_ref[:, cols] = act
        slope = 0.7978845608028654 * (1.0 + 3.0 * 0.044715 * pre * pre)
        gp_ref[:, cols] = half + 0.5 * pre * (1.0 - tanh * tanh) * slope
        branch = branch + (mm_nt(act, w_back_s[q - 1]) if q else mm(act, w_back_ref[...]))
    second_in = first_norm + branch + row(bias_back_ref)
    normal_two, scale_two = spread(second_in)
    lo_ref[...] = (normal_two * row(gain_two_ref) + row(shift_two_ref)).astype(bf16)
    grad_out = cot_ref[...].astype(f32)
    grad_second = spread_back(grad_out, row(gain_two_ref), normal_two, scale_two)
    second_ref[...] = grad_second
    grad_branch = grad_second.astype(bf16)
    gb_ref[...] = grad_branch
    vec_ref[...] = jnp.zeros_like(vec_ref)
    vec_ref[0:1, :] = jnp.sum(grad_out, axis=0, keepdims=True)
    vec_ref[1:2, :] = jnp.sum(grad_out * normal_two, axis=0, keepdims=True)
    vec_ref[2:3, :] = jnp.sum(grad_branch.astype(f32), axis=0, keepdims=True)


def position_mask(position, order):
    mask = 0
    for n, bit in enumerate(order):
        if (position >> (2 - n)) & 1:
            mask |= bit
    return mask


FFN_ORDERS = ((CORE, X_BIT, Y_BIT), (CORE, Y_BIT, X_BIT))


def weight_grads(info, left, right, keep, send, flip_scr, lhs_scr):
    mine = info[1]
    flip_scr[...] = left[...].T
    for n, order in enumerate(FFN_ORDERS):
        for p in range(SLOTS):
            start = pl.multiple_of((mine ^ position_mask(p, order)) * SLICE, SLICE)
            lhs_scr[p * SLICE : (p + 1) * SLICE, :] = flip_scr[pl.ds(start, SLICE), :]
        for pair in range(2):
            q = 2 * n + pair
            product = mm(lhs_scr[...], right[:, q * WIDTH : (q + 1) * WIDTH]).astype(bf16)
            for p in range(SLOTS):
                out = send if p >= SLOTS // 2 else keep
                out[n, p % (SLOTS // 2), pair] = product[p * SLICE : (p + 1) * SLICE, :]


def ffn_back_kernel(info, first_ref, second_ref, gb_ref, gp_ref, gain_one_ref, vec_in, *rest):
    w_out_s, w_in_ref, w_back_ref, w_in_s, w_back_s, x_ref, att_ref = rest[:7]
    g0, g13, g2, gin_ref, vec_ref, keep, send, go_keep, go_send = rest[7:16]
    gpre_ref, flip_scr, lhs_scr = rest[16:]
    grad_branch = gb_ref[...]
    grad_first = second_ref[...]
    vec_ref[...] = vec_in[...]
    for q in range(TP):
        cols = slice(q * WIDTH, (q + 1) * WIDTH)
        grad_act = mm(grad_branch, w_back_s[q - 1]) if q else mm_nt(grad_branch, w_back_ref[...])
        grad_pre = (grad_act * gp_ref[:, cols]).astype(bf16)
        gpre_ref[:, cols] = grad_pre
        vec_ref[pl.ds(6 + (info[2] ^ q), 1), :] = jnp.sum(grad_pre.astype(f32), axis=0, keepdims=True)
        grad_first = grad_first + mm_nt(grad_pre, w_in_s[q - 1] if q else w_in_ref[...])
    normal_one, scale_one = spread(first_ref[...])
    vec_ref[3:4, :] = jnp.sum(grad_first, axis=0, keepdims=True)
    vec_ref[4:5, :] = jnp.sum(grad_first * normal_one, axis=0, keepdims=True)
    grad_in = spread_back(grad_first, row(gain_one_ref), normal_one, scale_one)
    gin_ref[...] = grad_in
    grad_mixed = grad_in.astype(bf16)
    vec_ref[5:6, :] = jnp.sum(grad_mixed.astype(f32), axis=0, keepdims=True)
    grad_att = mm_nt(grad_mixed, w_out_s[...]).astype(bf16)
    for slot, (g_ref, row_at) in enumerate(((g0, 0), (g13, 0), (g2, 0), (g13, PACKED))):
        lo = slot * GROUP_WIDTH
        pack_heads(
            g_ref, row_at, [grad_att[:, lo + h * HEAD_DIM : lo + (h + 1) * HEAD_DIM] for h in range(GROUP)]
        )
    weight_grads(info, x_ref, gpre_ref, keep, send, flip_scr, lhs_scr)
    product = mm(grad_mixed.T, att_ref[...]).astype(bf16)
    go_keep[...] = product[:, : 2 * GROUP_WIDTH]
    go_send[...] = product[:, 2 * GROUP_WIDTH :]


ORDER_LA = (4, 2, 1)
ORDER_LB = (2, 4, 1)


HALF = WIDTH // 2
HELD = SLOTS // 2 * SLICE


def flip_kernel(t0, t1, t2, t3, out_ref):
    for slot, t_ref in enumerate((t0, t1, t2, t3)):
        out_ref[:, slot * QUARTER : (slot + 1) * QUARTER] = t_ref[...].T


def qkv_grad_kernel(
    info, tokens_t, gh0, gh1, gh2, go_own, go_near, vec_ref, s0, s1, s2, la_keep, la_send, lb_keep, lb_send, out_scr
):
    quarter, here = info[0], info[3]
    for h, gh_ref in enumerate((gh0, gh1, gh2)):
        product = mm(tokens_t[...], gh_ref[...]).astype(bf16)
        for kind in range(3):
            lo = kind * GROUP_WIDTH + h * HEAD_DIM
            out_scr[:, lo : lo + HEAD_DIM] = product[:, kind * HEAD_DIM : (kind + 1) * HEAD_DIM]
    add_to(out_scr.at[:, 3 * GROUP_WIDTH :], go_own[...], go_near[...])
    for keep, send, order, lo in (
        (la_keep, la_send, ORDER_LA, 0),
        (lb_keep, lb_send, ORDER_LB, HALF),
    ):
        for p in range(SLOTS):
            start = pl.multiple_of((here ^ position_mask(p, order)) * SLICE, SLICE)
            out = send if p >= SLOTS // 2 else keep
            row = p % (SLOTS // 2) * SLICE
            out[row : row + SLICE, :] = out_scr[pl.ds(start, SLICE), lo : lo + HALF]
    placed = []
    for kind in (0, 2):
        cols = slice(kind * HEAD_DIM, (kind + 1) * HEAD_DIM)
        piece = jnp.concatenate([sums[0:1, cols] for sums in (s0, s1, s2)], axis=1)
        placed.append(
            jnp.concatenate([jnp.where(quarter == g, piece, 0.0) for g in range(TP)], axis=1)
        )
    vectors = jnp.concatenate([vec_ref[0:10, :]] + placed + [vec_ref[12:VEC_ROWS, :]], axis=0)
    vectors = vectors.astype(bf16)
    for out in (la_keep, la_send):
        out[HELD : HELD + VEC_ROWS, :] = vectors[:, :HALF]
        out[HELD + VEC_ROWS :, :] = vectors[:, HALF:]


def token_grad_kernel(gh0, gh1, gh2, w_ref, keep_ref, send_ref, all_scr):
    for h, gh_ref in enumerate((gh0, gh1, gh2)):
        for kind in range(3):
            lo = kind * GROUP_WIDTH + h * HEAD_DIM
            all_scr[:, lo : lo + HEAD_DIM] = gh_ref[:, kind * HEAD_DIM : (kind + 1) * HEAD_DIM]
    half = LENGTH // 2
    send_ref[...] = mm_nt(all_scr[half:, :], w_ref[...]).astype(bf16)
    keep_ref[...] = mm_nt(all_scr[:half, :], w_ref[...]).astype(bf16)


def ffn_out_kernel(info, f_ref, f_other, w_in_out, w_back_out, flip_scr):
    mine = info[1]
    for side, ref in enumerate((f_ref, f_other)):
        for place_xy in range(4):
            mask = side | (X_BIT if place_xy & 1 else 0) | (Y_BIT if place_xy & 2 else 0)
            start = pl.multiple_of((mine ^ mask) * SLICE, SLICE)
            w_in_out[pl.ds(start, SLICE), :] = ref[place_xy, 0].astype(f32)
            flip_scr[pl.ds(start, SLICE), :] = ref[place_xy, 1].astype(f32)
    w_back_out[...] = flip_scr[...].T


def qkv_out_kernel(info, c_ref, c_other, qkv_out, out_out, *rest):
    vec_outs, (all_scr, flip_scr) = rest[:9], rest[9:]
    quarter, z_here, here = info[0], info[2], info[3]
    count = 16 * SLICE
    for side, ref in enumerate((c_ref, c_other)):
        for n in range(16):
            all_scr[side * 16 + n] = ref[n * SLICE : (n + 1) * SLICE, :]
    vectors = total(c_ref[count:, :], c_other[count:, :])
    bias_in = jnp.zeros((1, WIDTH), f32)
    for q in range(TP):
        bias_in = jnp.where(z_here == q, vectors[6 + q : 7 + q, :], bias_in)
    for out, n in zip(vec_outs[:8], (0, 1, 2, 3, 4, 5, 10, 11)):
        out[...] = vectors[n]
    vec_outs[8][...] = bias_in[0]
    for block in range(SLOTS):
        pieces = []
        for group in range(TP):
            group_off = quarter ^ group
            block_off = here ^ block
            xy = ((block_off >> 2) & 1) + (block_off & 2)
            z_off = (group_off & 1) + 2 * (block_off & 1)
            slot = (group_off >> 1) * 16 + xy * 4 + z_off
            pieces.append(all_scr[slot])
        rows = slice(block * SLICE, (block + 1) * SLICE)
        for kind in range(4):
            cols = slice(kind * GROUP_WIDTH, (kind + 1) * GROUP_WIDTH)
            joined = jnp.concatenate([piece[:, cols] for piece in pieces], axis=1).astype(f32)
            if kind < 3:
                qkv_out[rows, kind * WIDTH : (kind + 1) * WIDTH] = joined
            else:
                flip_scr[rows, :] = joined
    out_out[...] = flip_scr[...].T


def add_to(out, *terms):
    out[...] = add_low(*terms)


def join_kernel(*refs):
    out, at = refs[-1], 0
    for ref in refs[:-1]:
        out[at : at + ref.shape[0]] = ref[...]
        at += ref.shape[0]


def diag_kernel(by_x, by_y, first, second):
    half = first.shape[0]
    first[...] = by_x[:half]
    second[...] = by_y[half:]


CUT = SLICE


def mix_kernel(by_x, by_y, own, to_x, to_y):
    to_x[:PIECE] = own[...]
    to_y[:PIECE] = own[...]
    for n in range(2):
        to_x[PIECE + n * (PIECE - CUT) : PIECE + (n + 1) * (PIECE - CUT)] = by_y[n * PIECE + CUT : (n + 1) * PIECE]
        to_y[PIECE + n * CUT : PIECE + (n + 1) * CUT] = by_x[n * PIECE : n * PIECE + CUT]


def last_mix_kernel(by_x, by_y, to_x, to_y):
    to_x[...] = by_y[CUT:PIECE]
    to_y[...] = by_x[:CUT]


def level_one_kernel(keep, other, first, second):
    add_to(first, keep[0, 2:], other[0, 2:])
    add_to(second, keep[1, 2:], other[1, 2:])


def level_two_kernel(*refs):
    first, second = refs[-2:]
    for n in range(2):
        keep, other, by_x, by_y = refs[4 * n : 4 * n + 4]
        add_to(first.at[n], keep[0, 1], other[0, 1], by_x[1])
        add_to(second.at[n], keep[1, 1], other[1, 1], by_y[1])


def plane_kernel(*refs):
    by_xy, by_yx, near, kept = refs[-4:]
    for n in range(2):
        keep, other, by_x, by_y = refs[4 * n : 4 * n + 4]
        for q in range(TP):
            order, pair = q // 2, q % 2
            first, second = (by_x, by_xy) if order == 0 else (by_y, by_yx)
            out = near if q % 2 else kept
            add_to(
                out.at[q // 2, n], keep[order, 0, pair], other[order, 0, pair], first[0, pair], second[n, pair]
            )


def far_kernel(kept, near, far):
    add_to(far, kept[1], near[1])


def last_kernel(kept, near, far, out):
    for n in range(2):
        add_to(out.at[n], kept[0, 1 - n], near[0, 1 - n], far[1 - n])


def go_kernel(keep, other, own, send):
    add_to(own, keep[:, :GROUP_WIDTH], other[:, :GROUP_WIDTH])
    add_to(send, keep[:, GROUP_WIDTH:], other[:, GROUP_WIDTH:])


def near_kernel(keep, other, out):
    add_to(out, keep[QUARTER:], other[QUARTER:])


def tokens_kernel(keep, other, near, grad_in, out):
    add_to(out, keep[:QUARTER], other[:QUARTER], near[...], grad_in[...])


TWO = 2 * SLICE


def qkv_two_kernel(la, ra, lb, rb, la_out, lb_out):
    add_to(la_out, la[TWO:], ra[TWO:])
    add_to(lb_out, lb[TWO:], rb[TWO:])


def qkv_three_kernel(la, ra, ra2, lb, rb, rb2, out):
    add_to(out.at[:TWO, :HALF], la[:TWO], ra[:TWO], ra2[:TWO])
    add_to(out.at[:TWO, HALF:], lb[:TWO], rb[:TWO], rb2[...])
    for n in range(2):
        rows = slice(HELD + n * VEC_ROWS, HELD + (n + 1) * VEC_ROWS)
        rows_two = slice(TWO + n * VEC_ROWS, TWO + (n + 1) * VEC_ROWS)
        add_to(out.at[TWO:, n * HALF : (n + 1) * HALF], la[rows], ra[rows], ra2[rows_two])


def qkv_four_kernel(own, other, out):
    add_to(out.at[:SLICE], own[:SLICE], other[SLICE:TWO])
    add_to(out.at[SLICE:TWO], own[SLICE:TWO], other[:SLICE])
    add_to(out.at[TWO:], own[TWO:], other[TWO:])


def mix_l_kernel(by_x, by_y, other, to_x, to_y):
    to_x[:TWO] = other[:TWO]
    to_x[TWO:] = by_y[SLICE:TWO]
    to_y[:TWO] = other[:TWO]
    to_y[TWO:] = by_x[:SLICE]


def diag_l_kernel(by_x, by_y, to_x, to_y):
    to_x[...] = by_y[SLICE:TWO]
    to_y[...] = by_x[:SLICE]


def plane_l_kernel(own, other, x_own, y_own, x_other, y_other, d_x, d_y, out):
    diag_own = (y_other[TWO:], x_other[TWO:])
    diag_other = (d_y[...], d_x[...])
    places = (
        ((own[:SLICE], own[SLICE:TWO]), (other[:SLICE], other[SLICE:TWO])),
        ((x_own[:SLICE], x_own[SLICE:TWO]), (x_other[:SLICE], x_other[SLICE:TWO])),
        ((y_own[:SLICE], y_own[SLICE:TWO]), (y_other[:SLICE], y_other[SLICE:TWO])),
        (diag_own, diag_other),
    )
    for p, (here, there) in enumerate(places):
        for slot in range(TP):
            at = (p * TP + slot) * SLICE
            out[at : at + SLICE] = (there if slot % 2 else here)[slot // 2]
    add_to(out.at[16 * SLICE :], own[TWO:], other[TWO:])


VMEM = pl.BlockSpec(memory_space=pltpu.VMEM)
SMEM = pl.BlockSpec(memory_space=pltpu.SMEM)
HBM = pl.BlockSpec(memory_space=pl.ANY)


def call(kernel, in_specs, outs, scratch, vmem_mib, name, deps=()):
    count, extra = len(in_specs), len(deps)

    def body(*refs):
        kernel(*refs[:count], *refs[count + extra :])

    run = pl.pallas_call(
        body,
        out_shape=[jax.ShapeDtypeStruct(shape, dtype) for shape, dtype in outs],
        in_specs=list(in_specs) + [HBM] * extra,
        out_specs=[VMEM] * len(outs),
        scratch_shapes=scratch,
        compiler_params=pltpu.CompilerParams(vmem_limit_bytes=vmem_mib * 1024 * 1024),
        cost_estimate=pl.CostEstimate(flops=1, bytes_accessed=1, transcendentals=0),
        name=name,
    )
    return lambda *arrays: run(*arrays, *deps)


def step(kernel, name, outs, *arrays, deps=()):
    shapes = [(shape, bf16) for shape in outs]
    result = call(kernel, [VMEM] * len(arrays), shapes, [], 12, name, deps)(*arrays)
    return result[0] if len(outs) == 1 else result


def per_device(
    tokens,
    w_qkv,
    bias_query,
    bias_value,
    w_out,
    bias_out,
    gain_attn,
    shift_attn,
    w_in,
    bias_in,
    w_back,
    bias_back,
    gain_ffn,
    shift_ffn,
    random_blocks,
    cotangent,
):
    dp_count = lax.axis_size("dp")
    d = lax.axis_index("dp")
    z = lax.axis_index("tp")
    core = d & 1
    quarter = (z & 1) + 2 * core
    mine = d & (SLOTS - 1)
    here = ((d >> 1) & 1) * 4 + ((d >> 2) & 1) * 2 + (z >> 1)
    native = (core == z // 2).astype(jnp.int32)
    info = jnp.stack([quarter, mine, z, here, native]).astype(jnp.int32)
    extra_bits = [1 << b for b in range(3, dp_count.bit_length() - 1)]

    own_tokens = place(tokens[0])
    piece = call(
        piece_kernel,
        [SMEM, HBM, VMEM, VMEM],
        [((2 * SLICE + VEC_ROWS, WIDTH), bf16)],
        [pltpu.VMEM((WIDTH, WIDTH), bf16), pltpu.SemaphoreType.DMA],
        8,
        "piece",
    )(info, w_in, w_back, bias_in)[0]
    piece_one = hop(piece, 0, 1)
    piece_two = hop(piece, 0, 2)
    random_own = random_blocks.reshape(-1)
    random_other = hop(random_own, CORE, 0)
    w_group, bias_group = call(
        group_kernel,
        [SMEM, VMEM, VMEM, VMEM],
        [((WIDTH, 3 * GROUP_WIDTH), bf16), ((1, 3 * GROUP_WIDTH), f32)],
        [],
        16,
        "group",
    )(info, w_qkv, bias_query, bias_value)
    near_tokens = hop(own_tokens, 0, 1)
    core_tokens = hop(own_tokens, CORE, 0)
    far_tokens = hop(near_tokens, CORE, 0)
    part_one = step(
        join_kernel, "pair", [(2 * PIECE, WIDTH)], piece_one, piece_two, deps=(own_tokens, w_group)
    )
    x_one = hop(part_one, X_BIT, 0)
    y_one = hop(part_one, Y_BIT, 0)
    piece_three = hop(piece_two, 0, 1)
    cot = place(cotangent[0])
    to_x, to_y = step(
        mix_kernel,
        "mix",
        [(3 * PIECE - 2 * CUT, WIDTH), (PIECE + 2 * CUT, WIDTH)],
        x_one,
        y_one,
        piece_three,
        deps=(near_tokens,),
    )
    x_three = hop(to_x, X_BIT, 0)
    y_three = hop(to_y, Y_BIT, 0)

    packed = ((PACKED, 2 * HEAD_DIM), bf16)
    double = ((2 * PACKED, 2 * HEAD_DIM), bf16)
    per_head = ((LENGTH, HEAD_DIM), bf16)
    token_slots = (own_tokens, near_tokens, core_tokens, far_tokens)
    a0, a13, a2, *heads = call(
        attention_kernel,
        [SMEM] * 3 + [VMEM] * 6,
        [packed, double, packed] + [per_head] * 9 + [((16, QUARTER), f32)],
        [pltpu.VMEM((GROUP, LENGTH, HEAD_DIM), bf16)],
        24,
        "attention",
        (to_x, core_tokens),
    )(info, random_own, random_other, *token_slots, w_group, bias_group)
    heads, lse = heads[:9], heads[9]
    a1 = hop(a13, 0, 1)
    a2 = hop(a2, CORE, 0)
    a3 = hop(a1[PACKED:], CORE, 0)
    to_x, to_y = step(
        last_mix_kernel,
        "mix_last",
        [(PIECE - CUT, WIDTH), (CUT, WIDTH)],
        x_three,
        y_three,
        deps=(a0, cot),
    )
    last_back = hop(to_x, X_BIT, 0)
    last_in = hop(to_y, Y_BIT, 0)
    held = step(
        held_kernel,
        "held",
        [(11 * PIECE, WIDTH)],
        part_one,
        x_one,
        y_one,
        piece_three,
        x_three,
        y_three,
        deps=(a2, cot),
    )
    tokens_t = call(flip_kernel, [VMEM] * 4, [((WIDTH, LENGTH), bf16)], [], 8, "flip_tokens", (a1, held))(
        *token_slots
    )[0]
    last = step(join_kernel, "last_piece", [(PIECE, WIDTH)], last_in, last_back, deps=(tokens_t,))
    quarters = ((TP - 1, WIDTH, WIDTH), bf16)
    w_in_s, w_back_s, w_out_s, bias_s = call(
        assemble_kernel,
        [SMEM] + [VMEM] * 6,
        [quarters, quarters, ((WIDTH, WIDTH), bf16), ((TP - 1, VEC_ROWS, WIDTH), bf16)],
        [],
        20,
        "assemble",
    )(info, held, hop(held, CORE, 0), last_in, last_back, hop(last, CORE, 0), w_out)

    rows = ((QUARTER, WIDTH), bf16)
    wide = ((QUARTER, TP * WIDTH), bf16)
    rows_f32 = ((QUARTER, WIDTH), f32)
    vec_rows = ((VEC_ROWS, WIDTH), f32)
    out_here, first_in, grad_second, ffn_input, grad_branch, activated, gelu_slope, attended, vectors = call(
        ffn_kernel,
        [SMEM] + [VMEM] * 19,
        [rows, rows_f32, rows_f32, rows, rows, wide, ((QUARTER, TP * WIDTH), f32), rows, vec_rows],
        [],
        20,
        "ffn",
        (tokens_t,),
    )(
        info,
        own_tokens,
        a0,
        a1,
        a2,
        a3,
        bias_out,
        gain_attn,
        shift_attn,
        bias_back,
        gain_ffn,
        shift_ffn,
        bias_in,
        cot,
        w_out_s,
        w_in,
        w_back,
        w_in_s,
        w_back_s,
        bias_s,
    )
    pairs = ((2, SLOTS // 2, 2, SLICE, WIDTH), bf16)
    halves = ((WIDTH, 2 * GROUP_WIDTH), bf16)
    flips = [pltpu.VMEM((WIDTH, QUARTER), bf16), pltpu.VMEM((WIDTH, QUARTER), bf16)]
    back_keep, back_send = call(
        weight_grads, [SMEM] + [VMEM] * 2, [pairs] * 2, flips, 12, "back_grads"
    )(info, grad_branch, activated)
    back_other = hop(back_send, CORE, 0)

    g0, g13, g2, grad_in, vectors, in_keep, in_send, go_keep, go_send = call(
        ffn_back_kernel,
        [SMEM] + [VMEM] * 13,
        [packed, double, packed, rows_f32, vec_rows] + [pairs] * 2 + [halves] * 2,
        [pltpu.VMEM((QUARTER, TP * WIDTH), bf16)] + flips,
        20,
        "ffn_back",
        (back_keep,),
    )(
        info,
        first_in,
        grad_second,
        grad_branch,
        gelu_slope,
        gain_attn,
        vectors,
        w_out_s,
        w_in,
        w_back,
        w_in_s,
        w_back_s,
        ffn_input,
        attended,
    )
    g1 = hop(g13, 0, 1)
    g2 = hop(g2, CORE, 0)
    g3 = hop(g1[PACKED:], CORE, 0)

    first_level = [(2, 2, SLICE, WIDTH)] * 2
    def hop_pair(pair, first, second):
        return hop(pair[0], first, 0), hop(pair[1], second, 0)

    back_sums = step(level_one_kernel, "back_one", first_level, back_keep, back_other, deps=(g13,))
    back_x, back_y = hop_pair(back_sums, X_BIT, Y_BIT)
    in_other = hop(in_send, CORE, 0)
    go_other = hop(go_send, CORE, 0)

    def head_back(h, deps):
        return call(
            functools.partial(attention_back_kernel, h),
            [SMEM] * 3 + [VMEM] * 8,
            [((LENGTH, 3 * HEAD_DIM), bf16), ((8, 3 * HEAD_DIM), f32)],
            [
                pltpu.VMEM((LENGTH, HEAD_DIM), bf16),
                pltpu.VMEM((LENGTH, HEAD_DIM), f32),
                pltpu.VMEM((LENGTH, HEAD_DIM), f32),
                pltpu.VMEM((LENGTH, HEAD_DIM), f32),
            ],
            12,
            f"attention_back_{h}",
            deps,
        )(info, random_own, random_other, *heads[3 * h : 3 * h + 3], lse, g0, g1, g2, g3)

    go_own, go_send = step(go_kernel, "go", [(WIDTH, GROUP_WIDTH)] * 2, go_keep, go_other)
    go_near = hop(go_send, 0, 1)
    gh0, s0 = head_back(0, (go_own, back_sums[0]))
    sums = step(level_one_kernel, "in_one", first_level, in_keep, in_other, deps=(gh0, back_x, back_y, go_near))
    in_x, in_y = hop_pair(sums, X_BIT, Y_BIT)
    gh1, s1 = head_back(1, (sums[0],))
    gh2, s2 = head_back(2, (gh1,))
    back_parts = [back_keep, back_other, back_x, back_y]
    in_parts = [in_keep, in_other, in_x, in_y]
    sums = step(
        level_two_kernel, "two", [(2, 2, SLICE, WIDTH)] * 2, *back_parts, *in_parts, deps=(gh2,)
    )
    by_xy, by_yx = hop_pair(sums, Y_BIT, X_BIT)
    layer_out = place(out_here)[None]

    la_keep, la_send, lb_keep, lb_send = call(
        qkv_grad_kernel,
        [SMEM] + [VMEM] * 10,
        [((HELD + 2 * VEC_ROWS, HALF), bf16)] * 2 + [((HELD, HALF), bf16)] * 2,
        [pltpu.VMEM((WIDTH, 4 * GROUP_WIDTH), bf16)],
        16,
        "qkv_grads",
        (layer_out, sums[0]),
    )(info, tokens_t, gh0, gh1, gh2, go_own, go_near, vectors, s0, s1, s2)
    ra = hop(la_send, X_BIT, 0)
    rb = hop(lb_send, Y_BIT, 0)

    keep, send = call(
        token_grad_kernel,
        [VMEM] * 4,
        [((LENGTH // 2, WIDTH), bf16)] * 2,
        [pltpu.VMEM((LENGTH, 3 * GROUP_WIDTH), bf16)],
        16,
        "token_grad",
        (la_keep,),
    )(gh0, gh1, gh2, w_group)
    other = hop(send, CORE, 0)
    near_low = step(near_kernel, "near", [(QUARTER, WIDTH)], keep, other)
    near = hop(near_low, 0, 1)

    la2, lb2 = step(
        qkv_two_kernel,
        "qkv_two",
        [(TWO + 2 * VEC_ROWS, HALF), (TWO, HALF)],
        la_keep,
        ra,
        lb_keep,
        rb,
        deps=(near,),
    )
    ra2 = hop(la2, Y_BIT, 0)
    rb2 = hop(lb2, X_BIT, 0)
    rows_l = (TWO + VEC_ROWS, WIDTH)
    partial = step(qkv_three_kernel, "qkv_three", [rows_l], la_keep, ra, ra2, lb_keep, rb, rb2)
    near_sum, kept = step(
        plane_kernel,
        "plane_sum",
        [(2, 2, SLICE, WIDTH)] * 2,
        *back_parts,
        *in_parts,
        by_xy,
        by_yx,
        deps=(la2,),
    )
    near_f = hop(near_sum, 0, 1)
    far_low = step(far_kernel, "far", [(2, SLICE, WIDTH)], kept, near_f, deps=(partial,))
    far_f = hop(far_low, 0, 2)
    low_tokens = step(
        tokens_kernel, "tokens", [(QUARTER, WIDTH)], keep, other, near, grad_in, deps=(partial,)
    )
    sum_l = step(
        qkv_four_kernel, "qkv_four", [rows_l], partial, hop(partial, 0, 2), deps=(far_low, low_tokens)
    )
    for bit in extra_bits:
        sum_l = add_low(sum_l, hop(sum_l, bit, 0))
    grad_tokens = place(low_tokens)[None]

    own_l = sum_l[:TWO]
    x_own = hop(own_l, X_BIT, 0)
    y_own = hop(own_l, Y_BIT, 0)
    other_l = hop(sum_l, 0, 1)
    to_x, to_y = step(
        mix_l_kernel, "mix_l", [(TWO + SLICE, WIDTH)] * 2, x_own, y_own, other_l
    )
    x_other = hop(to_x, X_BIT, 0)
    y_other = hop(to_y, Y_BIT, 0)
    sum_f = step(last_kernel, "last", [(2, SLICE, WIDTH)], kept, near_f, far_f, deps=(to_x,))
    for bit in extra_bits:
        sum_f = add_low(sum_f, hop(sum_f, bit, 0))
    f_x = hop(sum_f, X_BIT, 0)
    f_y = hop(sum_f, Y_BIT, 0)
    diag_l = step(
        diag_l_kernel, "diag_l", [(SLICE, WIDTH)] * 2, x_other, y_other, deps=(sum_f, grad_tokens)
    )
    d_x, d_y = hop_pair(diag_l, X_BIT, Y_BIT)
    diag_f = step(diag_kernel, "diag_f", [(1, SLICE, WIDTH)] * 2, f_x, f_y, deps=(diag_l[0],))
    f_d0, f_d1 = hop_pair(diag_f, Y_BIT, X_BIT)
    f_all = step(join_kernel, "join_f", [(8, SLICE, WIDTH)], sum_f, f_x, f_y, f_d0, f_d1)
    f_all = f_all.reshape(4, 2, SLICE, WIDTH)
    grad_w_in, grad_w_back = call(
        ffn_out_kernel,
        [SMEM, VMEM, VMEM],
        [((WIDTH, WIDTH), f32)] * 2,
        [pltpu.VMEM((WIDTH, WIDTH), f32)],
        24,
        "ffn_out",
    )(info, f_all, hop(f_all, CORE, 0))
    plane = step(
        plane_l_kernel,
        "join_l",
        [(16 * SLICE + VEC_ROWS, WIDTH)],
        sum_l,
        other_l,
        x_own,
        y_own,
        x_other,
        y_other,
        d_x,
        d_y,
        deps=(f_all,),
    )
    grad_w_qkv, grad_w_out, *vec_outs = call(
        qkv_out_kernel,
        [SMEM, VMEM, VMEM],
        [((WIDTH, 3 * WIDTH), f32), ((WIDTH, WIDTH), f32)] + [((WIDTH,), f32)] * 9,
        [pltpu.VMEM((32, SLICE, WIDTH), bf16), pltpu.VMEM((WIDTH, WIDTH), f32)],
        24,
        "qkv_out",
        (grad_w_in,),
    )(info, plane, hop(plane, CORE, 0))
    (
        grad_shift_ffn,
        grad_gain_ffn,
        grad_bias_back,
        grad_shift_attn,
        grad_gain_attn,
        grad_bias_out,
        grad_bias_query,
        grad_bias_value,
        grad_bias_in,
    ) = vec_outs
    return (
        layer_out,
        grad_tokens,
        grad_w_qkv,
        grad_bias_query,
        grad_bias_value,
        grad_w_out,
        grad_bias_out,
        grad_gain_attn,
        grad_shift_attn,
        grad_w_in,
        grad_bias_in,
        grad_w_back,
        grad_bias_back,
        grad_gain_ffn,
        grad_shift_ffn,
    )


def solution(mesh):
    in_specs = (
        P("dp", "tp", None),
        P(),
        P(),
        P(),
        P(),
        P(),
        P(),
        P(),
        P(None, "tp"),
        P("tp"),
        P("tp", None),
        P(),
        P(),
        P(),
        P("dp", None, None, None),
        P("dp", "tp", None),
    )
    out_specs = (
        P("dp", "tp", None),
        P("dp", "tp", None),
        P(),
        P(),
        P(),
        P(),
        P(),
        P(),
        P(),
        P(None, "tp"),
        P("tp"),
        P("tp", None),
        P(),
        P(),
        P(),
    )
    return jax.shard_map(
        per_device, mesh=mesh, in_specs=in_specs, out_specs=out_specs, check_vma=False
    )
```

```python
import functools

import jax
import jax.numpy as jnp
from jax import lax
from jax.experimental import pallas as pl
from jax.experimental.pallas import tpu as pltpu
from jax.sharding import PartitionSpec as P

HEADS = 12
BLOCK = 64
HEAD_DIM = 64
TP = 4
GROUP = HEADS // TP
QUARTER = 256
LENGTH = TP * QUARTER
WIDTH = HEADS * HEAD_DIM
GROUP_WIDTH = GROUP * HEAD_DIM
SLOTS = 8
SLICE = WIDTH // SLOTS
VEC_ROWS = 16
CORE, X_BIT, Y_BIT = 1, 2, 4
PLANE_MASKS = (0, X_BIT, Y_BIT, X_BIT | Y_BIT)

epsilon = 1e-05
masked_score = -1e30
score_scale = HEAD_DIM ** (-0.5)
f32 = jnp.float32
bf16 = jnp.bfloat16


def mm(left, right):
    return jnp.dot(left, right, preferred_element_type=f32)


def mm_nt(left, right):
    return lax.dot_general(left, right, (((1,), (1,)), ((), ())), preferred_element_type=f32)


def total(*terms):
    acc = terms[0].astype(f32)
    for term in terms[1:]:
        acc = acc + term.astype(f32)
    return acc


def add_low(*terms):
    return total(*terms).astype(bf16)


def hop(array, dp_mask, z_mask):
    dp_count = lax.axis_size("dp")
    pairs = [
        (d * TP + z, (d ^ dp_mask) * TP + (z ^ z_mask)) for d in range(dp_count) for z in range(TP)
    ]
    return lax.ppermute(array, ("dp", "tp"), pairs)


def place(array):
    dp_count = lax.axis_size("dp")
    pairs = []
    for d in range(dp_count):
        for z in range(TP):
            here = d * TP + z
            away = (d ^ CORE) * TP + (z ^ 2)
            pairs.append((here, here if (d & 1) == z // 2 else away))
    return lax.ppermute(array, ("dp", "tp"), pairs)


def piece_kernel(info, w_in_hbm, w_back_ref, bias_ref, piece_ref, flip_scr, sem):
    start = pl.multiple_of(info[1] * SLICE, SLICE)
    copy = pltpu.make_async_copy(
        w_in_hbm.at[pl.ds(start, SLICE), :], piece_ref.at[pl.ds(0, SLICE), :], sem
    )
    copy.start()
    flip_scr[...] = w_back_ref[...].T
    piece_ref[SLICE : 2 * SLICE, :] = flip_scr[pl.ds(start, SLICE), :]
    bias = bias_ref[...].astype(f32).reshape(1, WIDTH)
    piece_ref[2 * SLICE :, :] = jnp.broadcast_to(bias, (VEC_ROWS, WIDTH)).astype(bf16)
    copy.wait()


def group_kernel(info, w_ref, bias_query_ref, bias_value_ref, w_out, b_out):
    bias_query = bias_query_ref[...].astype(f32).reshape(1, WIDTH)
    bias_value = bias_value_ref[...].astype(f32).reshape(1, WIDTH)
    b_out[...] = jnp.zeros_like(b_out)
    for g in range(TP):

        @pl.when(info[0] == g)
        def _(g=g):
            cols = slice(g * GROUP_WIDTH, (g + 1) * GROUP_WIDTH)
            for kind in range(3):
                lo = kind * GROUP_WIDTH
                w_out[:, lo : lo + GROUP_WIDTH] = w_ref[:, kind * WIDTH :][:, cols]
            b_out[:, :GROUP_WIDTH] = bias_query[:, cols]
            b_out[:, 2 * GROUP_WIDTH :] = bias_value[:, cols]


def block_bias(quarter, native, random_refs, head, chunk):
    shape = (LENGTH // BLOCK, QUARTER)
    row = lax.broadcasted_iota(jnp.int32, shape, 0)
    lane_block = lax.broadcasted_iota(jnp.int32, shape, 1) // BLOCK
    key_block = ((row // TP) ^ quarter) * TP + (row % TP)
    base = TP * (quarter ^ chunk)
    query_block = base + lane_block
    last = LENGTH // BLOCK - 1
    allowed = (key_block == 0) | (key_block == last)
    allowed |= (query_block == 0) | (query_block == last)
    allowed |= jnp.abs(key_block - query_block) <= 1
    for pick in range(3):
        chosen = jnp.zeros(shape, jnp.int32)
        for b in range(TP):
            at = (head * (LENGTH // BLOCK) + base + b) * 3 + pick
            value = jnp.where(native == 1, random_refs[0][at], random_refs[1][at])
            chosen = jnp.where(lane_block == b, value, chosen)
        allowed |= key_block == chosen
    return jnp.where(allowed, 0.0, masked_score).astype(f32)


def biased(scores, bias):
    blocks = LENGTH // BLOCK
    spread = scores.reshape(blocks, BLOCK, QUARTER) + bias.reshape(blocks, 1, QUARTER)
    return spread.reshape(LENGTH, QUARTER)


PACKED = QUARTER + QUARTER // 2


def pack_heads(ref, row, pieces):
    end = row + QUARTER
    ref[row:end, 0:64] = pieces[0]
    ref[row:end, 64:128] = pieces[1]
    ref[end : row + PACKED, 0:64] = pieces[2][: QUARTER // 2]
    ref[end : row + PACKED, 64:128] = pieces[2][QUARTER // 2 :]


def unpack_heads(ref, row):
    end = row + QUARTER
    third = jnp.concatenate([ref[end : row + PACKED, 0:64], ref[end : row + PACKED, 64:128]], axis=0)
    return [ref[row:end, 0:64], ref[row:end, 64:128], third]


def attention_kernel(info, rnd_own, rnd_other, t0, t1, t2, t3, w_ref, b_ref, a0, a13, a2, *rest):
    heads, lse_ref, out_scr = rest[:9], rest[9], rest[10]
    quarter, native = info[0], info[4]
    for slot, t_ref in enumerate((t0, t1, t2, t3)):
        rows = pl.ds(slot * QUARTER, QUARTER)
        proj = mm(t_ref[...], w_ref[...]) + b_ref[...]
        for h in range(GROUP):
            for kind in range(3):
                lo = kind * GROUP_WIDTH + h * HEAD_DIM
                piece = proj[:, lo : lo + HEAD_DIM].astype(bf16)
                if kind == 0:
                    piece = (piece.astype(f32) * score_scale).astype(bf16)
                heads[3 * h + kind][rows, :] = piece
    for h in range(GROUP):
        q_ref, k_ref, v_ref = heads[3 * h : 3 * h + 3]
        keys = k_ref[...]
        values_t = v_ref[...].T

        def chunk_step(chunk, carry, h=h, q_ref=q_ref, keys=keys, values_t=values_t):
            rows = pl.ds(pl.multiple_of(chunk * QUARTER, QUARTER), QUARTER)
            scores = mm_nt(keys, q_ref[rows, :])
            head = quarter * GROUP + h
            scores = biased(scores, block_bias(quarter, native, (rnd_own, rnd_other), head, chunk))
            row_max = jnp.max(scores, axis=0, keepdims=True)
            probs = jnp.exp(scores - row_max)
            row_sum = jnp.sum(probs, axis=0, keepdims=True)
            out_t = mm(values_t, probs.astype(bf16)) / row_sum
            out_scr[h, rows, :] = out_t.T.astype(bf16)
            lse_ref[pl.ds(h * TP + chunk, 1), :] = row_max + jnp.log(row_sum)
            return carry

        lax.fori_loop(0, TP, chunk_step, 0, unroll=True)
    for slot, (a_ref, row) in enumerate(((a0, 0), (a13, 0), (a2, 0), (a13, PACKED))):
        rows = slice(slot * QUARTER, (slot + 1) * QUARTER)
        pack_heads(a_ref, row, [out_scr[h, rows, :] for h in range(GROUP)])


def attention_back_kernel(
    h, info, rnd_own, rnd_other, q_ref, k_ref, v_ref, lse_ref, g0, g1, g2, g3, out_ref, sums_ref, do_scr, dk_scr, dv_scr, dq_scr
):
    quarter, native = info[0], info[4]
    for slot, g_ref in enumerate((g0, g1, g2, g3)):
        do_scr[slot * QUARTER : (slot + 1) * QUARTER, :] = unpack_heads(g_ref, 0)[h]
    keys = k_ref[...]
    keys_t = keys.T
    values = v_ref[...]
    dk_scr[...] = jnp.zeros_like(dk_scr)
    dv_scr[...] = jnp.zeros_like(dv_scr)

    def chunk_step(chunk, carry):
        rows = pl.ds(pl.multiple_of(chunk * QUARTER, QUARTER), QUARTER)
        queries = q_ref[rows, :]
        grad_out = do_scr[rows, :]
        scores = mm_nt(keys, queries)
        head = quarter * GROUP + h
        scores = biased(scores, block_bias(quarter, native, (rnd_own, rnd_other), head, chunk))
        probs = jnp.exp(scores - lse_ref[pl.ds(h * TP + chunk, 1), :])
        grad_probs = mm_nt(values, grad_out)
        delta = jnp.sum(probs * grad_probs, axis=0, keepdims=True)
        grad_scores = (probs * (grad_probs - delta)).astype(bf16)
        dv_scr[...] += mm(probs.astype(bf16), grad_out)
        dk_scr[...] += mm(grad_scores, queries)
        dq_t = mm(keys_t, grad_scores) * score_scale
        dq_scr[rows, :] = dq_t.T
        return carry

    lax.fori_loop(0, TP, chunk_step, 0, unroll=True)
    for n, scr in enumerate((dq_scr, dk_scr, dv_scr)):
        out_ref[:, n * HEAD_DIM : (n + 1) * HEAD_DIM] = scr[...].astype(bf16)
    sums_ref[...] = jnp.zeros_like(sums_ref)
    sums_ref[0:1, :] = jnp.sum(out_ref[...].astype(f32), axis=0, keepdims=True)


PIECE = 2 * SLICE + VEC_ROWS


def held_kernel(own, by_x, by_y, third, third_x, third_y, out):
    for q in range(2):
        for p, ref in enumerate((own, by_x, by_y)):
            at = (4 * q + p) * PIECE
            out[at : at + PIECE] = ref[q * PIECE : (q + 1) * PIECE]
        at = (4 * q + 3) * PIECE
        out[at : at + CUT] = third_y[PIECE + q * CUT : PIECE + (q + 1) * CUT]
        out[at + CUT : at + PIECE] = third_x[PIECE + q * (PIECE - CUT) : PIECE + (q + 1) * (PIECE - CUT)]
    for p, ref in enumerate((third, third_x, third_y)):
        at = (8 + p) * PIECE
        out[at : at + PIECE] = ref[:PIECE]


def assemble_kernel(info, held, other, last_in, last_back, other_last, w_out_ref, w_in_s, w_back_s, w_out_s, bias_s):
    quarter, mine = info[0], info[1]
    for slot in range(TP):
        start = pl.multiple_of((quarter ^ slot) * GROUP_WIDTH, GROUP_WIDTH)
        w_out_s[slot * GROUP_WIDTH : (slot + 1) * GROUP_WIDTH, :] = w_out_ref[pl.ds(start, GROUP_WIDTH), :]
    for side, main in enumerate((held, other)):
        for q in range(TP - 1):
            for p in range(4):
                start = pl.multiple_of((mine ^ PLANE_MASKS[p] ^ side) * SLICE, SLICE)
                at = (4 * q + p) * PIECE
                if q == TP - 2 and p == 3:
                    left = other_last[:SLICE] if side else last_in[...]
                    right = other_last[SLICE : 2 * SLICE] if side else last_back[:SLICE]
                else:
                    left, right = main[at : at + SLICE], main[at + SLICE : at + 2 * SLICE]
                w_in_s[q, pl.ds(start, SLICE), :] = left
                w_back_s[q, pl.ds(start, SLICE), :] = right
                if p == 0 and side == 0:
                    bias_s[q] = main[at + 2 * SLICE : at + PIECE]


def row(ref):
    return ref[...].astype(f32).reshape(1, WIDTH)


def spread(h):
    centred = h - jnp.mean(h, axis=-1, keepdims=True)
    scale = lax.rsqrt(jnp.mean(centred * centred, axis=-1, keepdims=True) + epsilon)
    return centred * scale, scale


def spread_back(grad, gain, normal, scale):
    weighted = grad * gain
    mean_one = jnp.mean(weighted, axis=-1, keepdims=True)
    mean_two = jnp.mean(weighted * normal, axis=-1, keepdims=True)
    return scale * (weighted - mean_one - normal * mean_two)


def ffn_kernel(info, t_ref, a0, a1, a2, a3, *rest):
    bias_out_ref, gain_one_ref, shift_one_ref, bias_back_ref, gain_two_ref, shift_two_ref, bias_in_ref = rest[:7]
    cot_ref, w_out_s, w_in_ref, w_back_ref, w_in_s, w_back_s, bias_s = rest[7:14]
    lo_ref, first_ref, second_ref, x_ref, gb_ref, act_ref, gp_ref, att_ref, vec_ref = rest[14:]
    for slot, a_ref in enumerate((a0, a1, a2, a3)):
        for h, piece in enumerate(unpack_heads(a_ref, 0)):
            lo = slot * GROUP_WIDTH + h * HEAD_DIM
            att_ref[:, lo : lo + HEAD_DIM] = piece
    first_in = t_ref[...].astype(f32) + (mm(att_ref[...], w_out_s[...]) + row(bias_out_ref))
    first_ref[...] = first_in
    first_norm = spread(first_in)[0] * row(gain_one_ref) + row(shift_one_ref)
    x = first_norm.astype(bf16)
    x_ref[...] = x
    branch = jnp.zeros((QUARTER, WIDTH), f32)
    for q in range(TP):
        cols = slice(q * WIDTH, (q + 1) * WIDTH)
        bias_q = bias_s[q - 1, 0:1, :].astype(f32) if q else row(bias_in_ref)
        pre = mm(x, w_in_s[q - 1] if q else w_in_ref[...]) + bias_q
        inner = 0.7978845608028654 * (pre + 0.044715 * pre * pre * pre)
        tanh = jnp.tanh(inner)
        half = 0.5 * (1.0 + tanh)
        act = (pre * half).astype(bf16)
        act_ref[:, cols] = act
        slope = 0.7978845608028654 * (1.0 + 3.0 * 0.044715 * pre * pre)
        gp_ref[:, cols] = half + 0.5 * pre * (1.0 - tanh * tanh) * slope
        branch = branch + (mm_nt(act, w_back_s[q - 1]) if q else mm(act, w_back_ref[...]))
    second_in = first_norm + branch + row(bias_back_ref)
    normal_two, scale_two = spread(second_in)
    lo_ref[...] = (normal_two * row(gain_two_ref) + row(shift_two_ref)).astype(bf16)
    grad_out = cot_ref[...].astype(f32)
    grad_second = spread_back(grad_out, row(gain_two_ref), normal_two, scale_two)
    second_ref[...] = grad_second
    grad_branch = grad_second.astype(bf16)
    gb_ref[...] = grad_branch
    vec_ref[...] = jnp.zeros_like(vec_ref)
    vec_ref[0:1, :] = jnp.sum(grad_out, axis=0, keepdims=True)
    vec_ref[1:2, :] = jnp.sum(grad_out * normal_two, axis=0, keepdims=True)
    vec_ref[2:3, :] = jnp.sum(grad_branch.astype(f32), axis=0, keepdims=True)


def position_mask(position, order):
    mask = 0
    for n, bit in enumerate(order):
        if (position >> (2 - n)) & 1:
            mask |= bit
    return mask


FFN_ORDERS = ((CORE, X_BIT, Y_BIT), (CORE, Y_BIT, X_BIT))


def weight_grads(info, left, right, keep, send, flip_scr, lhs_scr):
    mine = info[1]
    flip_scr[...] = left[...].T
    for n, order in enumerate(FFN_ORDERS):
        for p in range(SLOTS):
            start = pl.multiple_of((mine ^ position_mask(p, order)) * SLICE, SLICE)
            lhs_scr[p * SLICE : (p + 1) * SLICE, :] = flip_scr[pl.ds(start, SLICE), :]
        for pair in range(2):
            q = 2 * n + pair
            product = mm(lhs_scr[...], right[:, q * WIDTH : (q + 1) * WIDTH]).astype(bf16)
            for p in range(SLOTS):
                out = send if p >= SLOTS // 2 else keep
                out[n, p % (SLOTS // 2), pair] = product[p * SLICE : (p + 1) * SLICE, :]


def ffn_back_kernel(info, first_ref, second_ref, gb_ref, gp_ref, gain_one_ref, vec_in, *rest):
    w_out_s, w_in_ref, w_back_ref, w_in_s, w_back_s, x_ref, att_ref = rest[:7]
    g0, g13, g2, gin_ref, vec_ref, keep, send, go_keep, go_send = rest[7:16]
    gpre_ref, flip_scr, lhs_scr = rest[16:]
    grad_branch = gb_ref[...]
    grad_first = second_ref[...]
    vec_ref[...] = vec_in[...]
    for q in range(TP):
        cols = slice(q * WIDTH, (q + 1) * WIDTH)
        grad_act = mm(grad_branch, w_back_s[q - 1]) if q else mm_nt(grad_branch, w_back_ref[...])
        grad_pre = (grad_act * gp_ref[:, cols]).astype(bf16)
        gpre_ref[:, cols] = grad_pre
        vec_ref[pl.ds(6 + (info[2] ^ q), 1), :] = jnp.sum(grad_pre.astype(f32), axis=0, keepdims=True)
        grad_first = grad_first + mm_nt(grad_pre, w_in_s[q - 1] if q else w_in_ref[...])
    normal_one, scale_one = spread(first_ref[...])
    vec_ref[3:4, :] = jnp.sum(grad_first, axis=0, keepdims=True)
    vec_ref[4:5, :] = jnp.sum(grad_first * normal_one, axis=0, keepdims=True)
    grad_in = spread_back(grad_first, row(gain_one_ref), normal_one, scale_one)
    gin_ref[...] = grad_in
    grad_mixed = grad_in.astype(bf16)
    vec_ref[5:6, :] = jnp.sum(grad_mixed.astype(f32), axis=0, keepdims=True)
    grad_att = mm_nt(grad_mixed, w_out_s[...]).astype(bf16)
    for slot, (g_ref, row_at) in enumerate(((g0, 0), (g13, 0), (g2, 0), (g13, PACKED))):
        lo = slot * GROUP_WIDTH
        pack_heads(
            g_ref, row_at, [grad_att[:, lo + h * HEAD_DIM : lo + (h + 1) * HEAD_DIM] for h in range(GROUP)]
        )
    weight_grads(info, x_ref, gpre_ref, keep, send, flip_scr, lhs_scr)
    product = mm(grad_mixed.T, att_ref[...]).astype(bf16)
    go_keep[...] = product[:, : 2 * GROUP_WIDTH]
    go_send[...] = product[:, 2 * GROUP_WIDTH :]


ORDER_LA = (4, 2, 1)
ORDER_LB = (2, 4, 1)


HALF = WIDTH // 2
HELD = SLOTS // 2 * SLICE


def flip_kernel(t0, t1, t2, t3, out_ref):
    for slot, t_ref in enumerate((t0, t1, t2, t3)):
        out_ref[:, slot * QUARTER : (slot + 1) * QUARTER] = t_ref[...].T


def qkv_grad_kernel(
    info, tokens_t, gh0, gh1, gh2, go_own, go_near, vec_ref, s0, s1, s2, la_keep, la_send, lb_keep, lb_send, out_scr
):
    quarter, here = info[0], info[3]
    for h, gh_ref in enumerate((gh0, gh1, gh2)):
        product = mm(tokens_t[...], gh_ref[...]).astype(bf16)
        for kind in range(3):
            lo = kind * GROUP_WIDTH + h * HEAD_DIM
            out_scr[:, lo : lo + HEAD_DIM] = product[:, kind * HEAD_DIM : (kind + 1) * HEAD_DIM]
    add_to(out_scr.at[:, 3 * GROUP_WIDTH :], go_own[...], go_near[...])
    for keep, send, order, lo in (
        (la_keep, la_send, ORDER_LA, 0),
        (lb_keep, lb_send, ORDER_LB, HALF),
    ):
        for p in range(SLOTS):
            start = pl.multiple_of((here ^ position_mask(p, order)) * SLICE, SLICE)
            out = send if p >= SLOTS // 2 else keep
            row = p % (SLOTS // 2) * SLICE
            out[row : row + SLICE, :] = out_scr[pl.ds(start, SLICE), lo : lo + HALF]
    placed = []
    for kind in (0, 2):
        cols = slice(kind * HEAD_DIM, (kind + 1) * HEAD_DIM)
        piece = jnp.concatenate([sums[0:1, cols] for sums in (s0, s1, s2)], axis=1)
        placed.append(
            jnp.concatenate([jnp.where(quarter == g, piece, 0.0) for g in range(TP)], axis=1)
        )
    vectors = jnp.concatenate([vec_ref[0:10, :]] + placed + [vec_ref[12:VEC_ROWS, :]], axis=0)
    vectors = vectors.astype(bf16)
    for out in (la_keep, la_send, lb_keep, lb_send):
        out[HELD : HELD + VEC_ROWS, :] = vectors[:, :HALF]
        out[HELD + VEC_ROWS :, :] = vectors[:, HALF:]


def token_grad_kernel(gh0, gh1, gh2, w_ref, keep_ref, send_ref, all_scr):
    for h, gh_ref in enumerate((gh0, gh1, gh2)):
        for kind in range(3):
            lo = kind * GROUP_WIDTH + h * HEAD_DIM
            all_scr[:, lo : lo + HEAD_DIM] = gh_ref[:, kind * HEAD_DIM : (kind + 1) * HEAD_DIM]
    half = LENGTH // 2
    send_ref[...] = mm_nt(all_scr[half:, :], w_ref[...]).astype(bf16)
    keep_ref[...] = mm_nt(all_scr[:half, :], w_ref[...]).astype(bf16)


def final_kernel(info, c_ref, c_other, f_ref, f_other, low_tokens, low_out, *rest):
    qkv_out, out_out, w_in_out, w_back_out, layer_out, token_out = rest[:6]
    vec_outs, (all_scr, flip_scr, out_scr, back_scr) = rest[6:15], rest[15:]
    quarter, mine, z_here, here = info[0], info[1], info[2], info[3]
    block = pl.program_id(0)
    count = 16 * SLICE

    def piece(group, at):
        group_off, block_off = quarter ^ group, here ^ at
        xy = ((block_off >> 2) & 1) + (block_off & 2)
        return all_scr[(group_off >> 1) * 16 + xy * 4 + (group_off & 1) + 2 * (block_off & 1)]

    def ffn_piece(at, part):
        mask = mine ^ at
        nth = (((mask >> 1) & 1) + ((mask >> 2) & 1) * 2) * 2 + part
        return jnp.where((mask & 1) == 1, f_other[nth].astype(f32), f_ref[nth].astype(f32))

    @pl.when(block == 0)
    def _():
        for side, ref in enumerate((c_ref, c_other)):
            for n in range(16):
                all_scr[side * 16 + n] = ref[n * SLICE : (n + 1) * SLICE, :]
        vectors = total(c_ref[count:, :], c_other[count:, :])
        bias_in = jnp.zeros((1, WIDTH), f32)
        for q in range(TP):
            bias_in = jnp.where(z_here == q, vectors[6 + q : 7 + q, :], bias_in)
        for out, n in zip(vec_outs[:8], (0, 1, 2, 3, 4, 5, 10, 11)):
            out[...] = vectors[n]
        vec_outs[8][...] = bias_in[0]
        for at in range(SLOTS):
            rows = slice(at * SLICE, (at + 1) * SLICE)
            last = [piece(group, at)[:, 3 * GROUP_WIDTH :] for group in range(TP)]
            flip_scr[rows, :] = jnp.concatenate(last, axis=1).astype(f32)
            back_scr[rows, :] = ffn_piece(at, 1)
        out_scr[...] = flip_scr[...].T
        flip_scr[...] = back_scr[...].T

    rows = pl.ds(pl.multiple_of(block * SLICE, SLICE), SLICE)
    pieces = [piece(group, block) for group in range(TP)]
    for kind in range(3):
        cols = slice(kind * GROUP_WIDTH, (kind + 1) * GROUP_WIDTH)
        joined = jnp.concatenate([part[:, cols] for part in pieces], axis=1)
        qkv_out[:, kind * WIDTH : (kind + 1) * WIDTH] = joined.astype(f32)
    out_out[...] = out_scr[rows, :]
    w_back_out[...] = flip_scr[rows, :]
    w_in_out[...] = ffn_piece(block, 0)
    layer_out[...] = low_out[...]
    token_out[...] = low_tokens[...]


def add_to(out, *terms):
    out[...] = add_low(*terms)


def join_kernel(*refs):
    out, at = refs[-1], 0
    for ref in refs[:-1]:
        out[at : at + ref.shape[0]] = ref[...]
        at += ref.shape[0]


def diag_kernel(by_x, by_y, first, second):
    half = first.shape[0]
    first[...] = by_x[:half]
    second[...] = by_y[half:]


CUT = SLICE


def mix_kernel(by_x, by_y, own, to_x, to_y):
    to_x[:PIECE] = own[...]
    to_y[:PIECE] = own[...]
    for n in range(2):
        to_x[PIECE + n * (PIECE - CUT) : PIECE + (n + 1) * (PIECE - CUT)] = by_y[n * PIECE + CUT : (n + 1) * PIECE]
        to_y[PIECE + n * CUT : PIECE + (n + 1) * CUT] = by_x[n * PIECE : n * PIECE + CUT]


def last_mix_kernel(by_x, by_y, to_x, to_y):
    to_x[...] = by_y[CUT:PIECE]
    to_y[...] = by_x[:CUT]


def level_one_kernel(keep, other, first, second):
    add_to(first, keep[0, 2:], other[0, 2:])
    add_to(second, keep[1, 2:], other[1, 2:])


def middle_kernel(in_keep, in_other, back_keep, back_other, back_x, back_y, to_x, to_y):
    for n in range(2):
        out = to_y if n else to_x
        for p in range(2):
            for pair in range(2):
                add_to(out.at[2 * p + pair], in_keep[n, 2 + p, pair], in_other[n, 2 + p, pair])
    for pair in range(2):
        add_to(to_y.at[4 + pair], back_keep[0, 1, pair], back_other[0, 1, pair], back_x[1, pair])
        add_to(to_x.at[4 + pair], back_keep[1, 1, pair], back_other[1, 1, pair], back_y[1, pair])


def in_two_kernel(keep, other, by_x, by_y, first, second):
    for pair in range(2):
        add_to(first.at[pair], keep[0, 1, pair], other[0, 1, pair], by_x[2 + pair])
        add_to(second.at[pair], keep[1, 1, pair], other[1, 1, pair], by_y[2 + pair])


def in_plane_kernel(keep, other, by_x, by_y, by_xy, by_yx, near, kept):
    for q in range(TP):
        order, pair = q // 2, q % 2
        first, second = (by_x, by_xy) if order == 0 else (by_y, by_yx)
        out = near if q % 2 else kept
        add_to(out.at[q // 2], keep[order, 0, pair], other[order, 0, pair], first[pair], second[pair])


def back_plane_kernel(keep, other, by_x, by_y, mid_x, mid_y, near, kept):
    for q in range(TP):
        order, pair = q // 2, q % 2
        first, second = (by_x, mid_y) if order == 0 else (by_y, mid_x)
        out = near if q % 2 else kept
        add_to(out.at[q // 2], keep[order, 0, pair], other[order, 0, pair], first[0, pair], second[4 + pair])


def far_kernel(kept, near, far):
    add_to(far, kept[1], near[1])


def last_kernel(kept_a, near_a, far_a, kept_b, near_b, far_b, out):
    add_to(out.at[0], kept_a[0], near_a[0], far_a[...])
    add_to(out.at[1], kept_b[0], near_b[0], far_b[...])


def go_kernel(keep, other, own, send):
    add_to(own, keep[:, :GROUP_WIDTH], other[:, :GROUP_WIDTH])
    add_to(send, keep[:, GROUP_WIDTH:], other[:, GROUP_WIDTH:])


def near_kernel(keep, other, out):
    add_to(out, keep[QUARTER:], other[QUARTER:])


def tokens_kernel(keep, other, near, grad_in, out_here, tokens, again):
    add_to(tokens, keep[:QUARTER], other[:QUARTER], near[...], grad_in[...])
    again[...] = out_here[...]


TWO = 2 * SLICE


def qkv_two_kernel(la, ra, lb, rb, la_out, lb_out):
    add_to(la_out, la[TWO:], ra[TWO:])
    add_to(lb_out, lb[TWO:HELD], rb[TWO:HELD])


def qkv_three_kernel(la, ra, ra2, lb, rb, rb2, out):
    add_to(out.at[:TWO, :HALF], la[:TWO], ra[:TWO], ra2[:TWO])
    add_to(out.at[:TWO, HALF:], lb[:TWO], rb[:TWO], rb2[...])
    for n in range(2):
        rows = slice(HELD + n * VEC_ROWS, HELD + (n + 1) * VEC_ROWS)
        rows_two = slice(TWO + n * VEC_ROWS, TWO + (n + 1) * VEC_ROWS)
        add_to(out.at[TWO:, n * HALF : (n + 1) * HALF], la[rows], ra[rows], ra2[rows_two])


def qkv_four_kernel(own, other, out):
    add_to(out.at[:SLICE], own[:SLICE], other[SLICE:TWO])
    add_to(out.at[SLICE:TWO], own[SLICE:TWO], other[:SLICE])
    add_to(out.at[TWO:], own[TWO:], other[TWO:])


def mix_l_kernel(by_x, by_y, other, to_x, to_y):
    to_x[:TWO] = other[:TWO]
    to_x[TWO:] = by_y[SLICE:TWO]
    to_y[:TWO] = other[:TWO]
    to_y[TWO:] = by_x[:SLICE]


def diag_l_kernel(by_x, by_y, to_x, to_y):
    to_x[...] = by_y[SLICE:TWO]
    to_y[...] = by_x[:SLICE]


def plane_l_kernel(own, other, x_own, y_own, x_other, y_other, d_x, d_y, out):
    diag_own = (y_other[TWO:], x_other[TWO:])
    diag_other = (d_y[...], d_x[...])
    places = (
        ((own[:SLICE], own[SLICE:TWO]), (other[:SLICE], other[SLICE:TWO])),
        ((x_own[:SLICE], x_own[SLICE:TWO]), (x_other[:SLICE], x_other[SLICE:TWO])),
        ((y_own[:SLICE], y_own[SLICE:TWO]), (y_other[:SLICE], y_other[SLICE:TWO])),
        (diag_own, diag_other),
    )
    for p, (here, there) in enumerate(places):
        for slot in range(TP):
            at = (p * TP + slot) * SLICE
            out[at : at + SLICE] = (there if slot % 2 else here)[slot // 2]
    add_to(out.at[16 * SLICE :], own[TWO:], other[TWO:])


VMEM = pl.BlockSpec(memory_space=pltpu.VMEM)
SMEM = pl.BlockSpec(memory_space=pltpu.SMEM)
HBM = pl.BlockSpec(memory_space=pl.ANY)


def call(kernel, in_specs, outs, scratch, vmem_mib, name, deps=()):
    count, extra = len(in_specs), len(deps)

    def body(*refs):
        kernel(*refs[:count], *refs[count + extra :])

    run = pl.pallas_call(
        body,
        out_shape=[jax.ShapeDtypeStruct(shape, dtype) for shape, dtype in outs],
        in_specs=list(in_specs) + [HBM] * extra,
        out_specs=[VMEM] * len(outs),
        scratch_shapes=scratch,
        compiler_params=pltpu.CompilerParams(vmem_limit_bytes=vmem_mib * 1024 * 1024),
        cost_estimate=pl.CostEstimate(flops=1, bytes_accessed=1, transcendentals=0),
        name=name,
    )
    return lambda *arrays: run(*arrays, *deps)


def step(kernel, name, outs, *arrays, deps=()):
    shapes = [(shape, bf16) for shape in outs]
    result = call(kernel, [VMEM] * len(arrays), shapes, [], 12, name, deps)(*arrays)
    return result[0] if len(outs) == 1 else result


def per_device(
    tokens,
    w_qkv,
    bias_query,
    bias_value,
    w_out,
    bias_out,
    gain_attn,
    shift_attn,
    w_in,
    bias_in,
    w_back,
    bias_back,
    gain_ffn,
    shift_ffn,
    random_blocks,
    cotangent,
):
    dp_count = lax.axis_size("dp")
    d = lax.axis_index("dp")
    z = lax.axis_index("tp")
    core = d & 1
    quarter = (z & 1) + 2 * core
    mine = d & (SLOTS - 1)
    here = ((d >> 1) & 1) * 4 + ((d >> 2) & 1) * 2 + (z >> 1)
    native = (core == z // 2).astype(jnp.int32)
    info = jnp.stack([quarter, mine, z, here, native]).astype(jnp.int32)
    extra_bits = [1 << b for b in range(3, dp_count.bit_length() - 1)]

    own_tokens = place(tokens[0])
    piece = call(
        piece_kernel,
        [SMEM, HBM, VMEM, VMEM],
        [((2 * SLICE + VEC_ROWS, WIDTH), bf16)],
        [pltpu.VMEM((WIDTH, WIDTH), bf16), pltpu.SemaphoreType.DMA],
        8,
        "piece",
    )(info, w_in, w_back, bias_in)[0]
    piece_one = hop(piece, 0, 1)
    piece_two = hop(piece, 0, 2)
    random_own = random_blocks.reshape(-1)
    random_other = hop(random_own, CORE, 0)
    w_group, bias_group = call(
        group_kernel,
        [SMEM, VMEM, VMEM, VMEM],
        [((WIDTH, 3 * GROUP_WIDTH), bf16), ((1, 3 * GROUP_WIDTH), f32)],
        [],
        16,
        "group",
    )(info, w_qkv, bias_query, bias_value)
    near_tokens = hop(own_tokens, 0, 1)
    core_tokens = hop(own_tokens, CORE, 0)
    far_tokens = hop(near_tokens, CORE, 0)
    part_one = step(
        join_kernel, "pair", [(2 * PIECE, WIDTH)], piece_one, piece_two, deps=(own_tokens, w_group)
    )
    x_one = hop(part_one, X_BIT, 0)
    y_one = hop(part_one, Y_BIT, 0)
    piece_three = hop(piece_two, 0, 1)
    cot = place(cotangent[0])
    to_x, to_y = step(
        mix_kernel,
        "mix",
        [(3 * PIECE - 2 * CUT, WIDTH), (PIECE + 2 * CUT, WIDTH)],
        x_one,
        y_one,
        piece_three,
        deps=(near_tokens,),
    )
    x_three = hop(to_x, X_BIT, 0)
    y_three = hop(to_y, Y_BIT, 0)

    packed = ((PACKED, 2 * HEAD_DIM), bf16)
    double = ((2 * PACKED, 2 * HEAD_DIM), bf16)
    per_head = ((LENGTH, HEAD_DIM), bf16)
    token_slots = (own_tokens, near_tokens, core_tokens, far_tokens)
    a0, a13, a2, *heads = call(
        attention_kernel,
        [SMEM] * 3 + [VMEM] * 6,
        [packed, double, packed] + [per_head] * 9 + [((16, QUARTER), f32)],
        [pltpu.VMEM((GROUP, LENGTH, HEAD_DIM), bf16)],
        24,
        "attention",
        (to_x, core_tokens),
    )(info, random_own, random_other, *token_slots, w_group, bias_group)
    heads, lse = heads[:9], heads[9]
    a1 = hop(a13, 0, 1)
    a2 = hop(a2, CORE, 0)
    a3 = hop(a1[PACKED:], CORE, 0)
    to_x, to_y = step(
        last_mix_kernel,
        "mix_last",
        [(PIECE - CUT, WIDTH), (CUT, WIDTH)],
        x_three,
        y_three,
        deps=(a0, cot),
    )
    last_back = hop(to_x, X_BIT, 0)
    last_in = hop(to_y, Y_BIT, 0)
    held = step(
        held_kernel,
        "held",
        [(11 * PIECE, WIDTH)],
        part_one,
        x_one,
        y_one,
        piece_three,
        x_three,
        y_three,
        deps=(a2, cot),
    )
    tokens_t = call(flip_kernel, [VMEM] * 4, [((WIDTH, LENGTH), bf16)], [], 8, "flip_tokens", (a1, held))(
        *token_slots
    )[0]
    last = step(join_kernel, "last_piece", [(PIECE, WIDTH)], last_in, last_back, deps=(tokens_t,))
    quarters = ((TP - 1, WIDTH, WIDTH), bf16)
    w_in_s, w_back_s, w_out_s, bias_s = call(
        assemble_kernel,
        [SMEM] + [VMEM] * 6,
        [quarters, quarters, ((WIDTH, WIDTH), bf16), ((TP - 1, VEC_ROWS, WIDTH), bf16)],
        [],
        20,
        "assemble",
    )(info, held, hop(held, CORE, 0), last_in, last_back, hop(last, CORE, 0), w_out)

    rows = ((QUARTER, WIDTH), bf16)
    wide = ((QUARTER, TP * WIDTH), bf16)
    rows_f32 = ((QUARTER, WIDTH), f32)
    vec_rows = ((VEC_ROWS, WIDTH), f32)
    out_here, first_in, grad_second, ffn_input, grad_branch, activated, gelu_slope, attended, vectors = call(
        ffn_kernel,
        [SMEM] + [VMEM] * 19,
        [rows, rows_f32, rows_f32, rows, rows, wide, ((QUARTER, TP * WIDTH), f32), rows, vec_rows],
        [],
        20,
        "ffn",
        (tokens_t,),
    )(
        info,
        own_tokens,
        a0,
        a1,
        a2,
        a3,
        bias_out,
        gain_attn,
        shift_attn,
        bias_back,
        gain_ffn,
        shift_ffn,
        bias_in,
        cot,
        w_out_s,
        w_in,
        w_back,
        w_in_s,
        w_back_s,
        bias_s,
    )
    pairs = ((2, SLOTS // 2, 2, SLICE, WIDTH), bf16)
    halves = ((WIDTH, 2 * GROUP_WIDTH), bf16)
    flips = [pltpu.VMEM((WIDTH, QUARTER), bf16), pltpu.VMEM((WIDTH, QUARTER), bf16)]
    back_keep, back_send = call(
        weight_grads, [SMEM] + [VMEM] * 2, [pairs] * 2, flips, 12, "back_grads"
    )(info, grad_branch, activated)
    back_other = hop(back_send, CORE, 0)

    g0, g13, g2, grad_in, vectors, in_keep, in_send, go_keep, go_send = call(
        ffn_back_kernel,
        [SMEM] + [VMEM] * 13,
        [packed, double, packed, rows_f32, vec_rows] + [pairs] * 2 + [halves] * 2,
        [pltpu.VMEM((QUARTER, TP * WIDTH), bf16)] + flips,
        20,
        "ffn_back",
        (back_keep,),
    )(
        info,
        first_in,
        grad_second,
        grad_branch,
        gelu_slope,
        gain_attn,
        vectors,
        w_out_s,
        w_in,
        w_back,
        w_in_s,
        w_back_s,
        ffn_input,
        attended,
    )
    g1 = hop(g13, 0, 1)
    g2 = hop(g2, CORE, 0)
    g3 = hop(g1[PACKED:], CORE, 0)

    first_level = [(2, 2, SLICE, WIDTH)] * 2
    def hop_pair(pair, first, second):
        return hop(pair[0], first, 0), hop(pair[1], second, 0)

    back_sums = step(level_one_kernel, "back_one", first_level, back_keep, back_other, deps=(g13,))
    back_x, back_y = hop_pair(back_sums, X_BIT, Y_BIT)
    in_other = hop(in_send, CORE, 0)
    go_other = hop(go_send, CORE, 0)

    def head_back(h, deps):
        return call(
            functools.partial(attention_back_kernel, h),
            [SMEM] * 3 + [VMEM] * 8,
            [((LENGTH, 3 * HEAD_DIM), bf16), ((8, 3 * HEAD_DIM), f32)],
            [
                pltpu.VMEM((LENGTH, HEAD_DIM), bf16),
                pltpu.VMEM((LENGTH, HEAD_DIM), f32),
                pltpu.VMEM((LENGTH, HEAD_DIM), f32),
                pltpu.VMEM((LENGTH, HEAD_DIM), f32),
            ],
            12,
            f"attention_back_{h}",
            deps,
        )(info, random_own, random_other, *heads[3 * h : 3 * h + 3], lse, g0, g1, g2, g3)

    go_own, go_send = step(go_kernel, "go", [(WIDTH, GROUP_WIDTH)] * 2, go_keep, go_other)
    go_near = hop(go_send, 0, 1)
    gh0, s0 = head_back(0, (go_own, back_sums[0]))
    back_parts = [back_keep, back_other, back_x, back_y]
    to_x, to_y = step(
        middle_kernel,
        "middle",
        [(6, SLICE, WIDTH)] * 2,
        in_keep,
        in_other,
        *back_parts,
        deps=(gh0,),
    )
    mid_x, mid_y = hop(to_x, X_BIT, 0), hop(to_y, Y_BIT, 0)
    in_parts = [in_keep, in_other, mid_x, mid_y]
    z_level = [(2, SLICE, WIDTH)] * 2
    gh1, s1 = head_back(1, (to_x,))
    gh2, s2 = head_back(2, (gh1,))

    la_keep, la_send, lb_keep, lb_send = call(
        qkv_grad_kernel,
        [SMEM] + [VMEM] * 10,
        [((HELD + 2 * VEC_ROWS, HALF), bf16)] * 4,
        [pltpu.VMEM((WIDTH, 4 * GROUP_WIDTH), bf16)],
        16,
        "qkv_grads",
        (gh2,),
    )(info, tokens_t, gh0, gh1, gh2, go_own, go_near, vectors, s0, s1, s2)
    ra = hop(la_send, X_BIT, 0)
    rb = hop(lb_send, Y_BIT, 0)

    keep, send = call(
        token_grad_kernel,
        [VMEM] * 4,
        [((LENGTH // 2, WIDTH), bf16)] * 2,
        [pltpu.VMEM((LENGTH, 3 * GROUP_WIDTH), bf16)],
        16,
        "token_grad",
        (la_keep,),
    )(gh0, gh1, gh2, w_group)
    other = hop(send, CORE, 0)
    near_b, kept_b = step(
        back_plane_kernel, "back_plane", z_level, *back_parts, mid_x, mid_y, deps=(keep,)
    )
    near_b = hop(near_b, 0, 1)
    sums = step(in_two_kernel, "in_two", z_level, *in_parts, deps=(kept_b,))
    in_parts += hop_pair(sums, Y_BIT, X_BIT)
    near_low = step(near_kernel, "near", [(QUARTER, WIDTH)], keep, other, deps=(sums[0],))
    near = hop(near_low, 0, 1)
    far_b = step(far_kernel, "far_back", [(SLICE, WIDTH)], kept_b, near_b, deps=(near_low,))
    far_hop_b = hop(far_b, 0, 2)
    la2, lb2 = step(
        qkv_two_kernel,
        "qkv_two",
        [(TWO + 2 * VEC_ROWS, HALF), (TWO, HALF)],
        la_keep,
        ra,
        lb_keep,
        rb,
        deps=(far_b,),
    )
    ra2 = hop(la2, Y_BIT, 0)
    rb2 = hop(lb2, X_BIT, 0)
    rows_l = (TWO + VEC_ROWS, WIDTH)
    near_a, kept_a = step(in_plane_kernel, "in_plane", z_level, *in_parts, deps=(la2,))
    near_a = hop(near_a, 0, 1)
    partial = step(
        qkv_three_kernel, "qkv_three", [rows_l], la_keep, ra, ra2, lb_keep, rb, rb2, deps=(kept_a, far_hop_b)
    )
    far_a = step(far_kernel, "far_in", [(SLICE, WIDTH)], kept_a, near_a, deps=(partial, far_hop_b))
    far_hop_a = hop(far_a, 0, 2)
    sum_l = step(
        qkv_four_kernel, "qkv_four", [rows_l], partial, hop(partial, 0, 2), deps=(far_a, near)
    )
    for bit in extra_bits:
        sum_l = add_low(sum_l, hop(sum_l, bit, 0))

    own_l = sum_l[:TWO]
    x_own = hop(own_l, X_BIT, 0)
    y_own = hop(own_l, Y_BIT, 0)
    other_l = hop(sum_l, 0, 1)
    to_x, to_y = step(
        mix_l_kernel, "mix_l", [(TWO + SLICE, WIDTH)] * 2, x_own, y_own, other_l
    )
    x_other = hop(to_x, X_BIT, 0)
    y_other = hop(to_y, Y_BIT, 0)
    sum_f = step(
        last_kernel,
        "last",
        [(2, SLICE, WIDTH)],
        kept_a,
        near_a,
        far_hop_a,
        kept_b,
        near_b,
        far_hop_b,
        deps=(to_x,),
    )
    for bit in extra_bits:
        sum_f = add_low(sum_f, hop(sum_f, bit, 0))
    low_outs = step(
        tokens_kernel,
        "tokens",
        [(QUARTER, WIDTH)] * 2,
        keep,
        other,
        near,
        grad_in,
        out_here,
        deps=(sum_f,),
    )
    token_grads, layer_out = place(low_outs[0]), place(low_outs[1])
    f_x = hop(sum_f, X_BIT, 0)
    f_y = hop(sum_f, Y_BIT, 0)
    diag_f = step(diag_kernel, "diag_f", [(1, SLICE, WIDTH)] * 2, f_x, f_y, deps=(to_x,))
    f_d0, f_d1 = hop_pair(diag_f, Y_BIT, X_BIT)
    diag_l = step(
        diag_l_kernel, "diag_l", [(SLICE, WIDTH)] * 2, x_other, y_other, deps=(diag_f[0],)
    )
    d_x, d_y = hop_pair(diag_l, X_BIT, Y_BIT)
    f_all = step(join_kernel, "join_f", [(8, SLICE, WIDTH)], sum_f, f_x, f_y, f_d0, f_d1)
    plane = step(
        plane_l_kernel,
        "join_l",
        [(16 * SLICE + VEC_ROWS, WIDTH)],
        sum_l,
        other_l,
        x_own,
        y_own,
        x_other,
        y_other,
        d_x,
        d_y,
        deps=(f_all, token_grads, layer_out),
    )
    whole = pl.BlockSpec(memory_space=pltpu.VMEM)
    piece_rows = QUARTER // SLOTS
    by_rows = lambda rows, cols: pl.BlockSpec((rows, cols), lambda i: (i, 0))
    square = ((WIDTH, WIDTH), f32)
    grad_w_qkv, grad_w_out, grad_w_in, grad_w_back, layer_out, grad_tokens, *vec_outs = pl.pallas_call(
        final_kernel,
        grid=(SLOTS,),
        out_shape=[
            jax.ShapeDtypeStruct(shape, dtype)
            for shape, dtype in [((WIDTH, 3 * WIDTH), f32), square, square, square, rows, rows]
            + [((WIDTH,), f32)] * 9
        ],
        in_specs=[SMEM]
        + [whole] * 4
        + [by_rows(piece_rows, WIDTH)] * 2,
        out_specs=[by_rows(SLICE, 3 * WIDTH)]
        + [by_rows(SLICE, WIDTH)] * 3
        + [by_rows(piece_rows, WIDTH)] * 2
        + [pl.BlockSpec((WIDTH,), lambda i: (0,))] * 9,
        scratch_shapes=[pltpu.VMEM((32, SLICE, WIDTH), bf16)] + [pltpu.VMEM((WIDTH, WIDTH), f32)] * 3,
        compiler_params=pltpu.CompilerParams(vmem_limit_bytes=36 * 1024 * 1024),
        cost_estimate=pl.CostEstimate(flops=1, bytes_accessed=1, transcendentals=0),
        name="final",
    )(info, plane, hop(plane, CORE, 0), f_all, hop(f_all, CORE, 0), token_grads, layer_out)
    (
        grad_shift_ffn,
        grad_gain_ffn,
        grad_bias_back,
        grad_shift_attn,
        grad_gain_attn,
        grad_bias_out,
        grad_bias_query,
        grad_bias_value,
        grad_bias_in,
    ) = vec_outs
    return (
        layer_out[None],
        grad_tokens[None],
        grad_w_qkv,
        grad_bias_query,
        grad_bias_value,
        grad_w_out,
        grad_bias_out,
        grad_gain_attn,
        grad_shift_attn,
        grad_w_in,
        grad_bias_in,
        grad_w_back,
        grad_bias_back,
        grad_gain_ffn,
        grad_shift_ffn,
    )


def solution(mesh):
    in_specs = (
        P("dp", "tp", None),
        P(),
        P(),
        P(),
        P(),
        P(),
        P(),
        P(),
        P(None, "tp"),
        P("tp"),
        P("tp", None),
        P(),
        P(),
        P(),
        P("dp", None, None, None),
        P("dp", "tp", None),
    )
    out_specs = (
        P("dp", "tp", None),
        P("dp", "tp", None),
        P(),
        P(),
        P(),
        P(),
        P(),
        P(),
        P(),
        P(None, "tp"),
        P("tp"),
        P("tp", None),
        P(),
        P(),
        P(),
    )
    return jax.shard_map(
        per_device, mesh=mesh, in_specs=in_specs, out_specs=out_specs, check_vma=False
    )
```

```python
import functools

import jax
import jax.numpy as jnp
from jax import lax
from jax.experimental import pallas as pl
from jax.experimental.pallas import tpu as pltpu
from jax.sharding import PartitionSpec as P

HEADS = 12
BLOCK = 64
HEAD_DIM = 64
TP = 4
GROUP = HEADS // TP
QUARTER = 256
LENGTH = TP * QUARTER
WIDTH = HEADS * HEAD_DIM
GROUP_WIDTH = GROUP * HEAD_DIM
SLOTS = 8
SLICE = WIDTH // SLOTS
VEC_ROWS = 16
CORE, X_BIT, Y_BIT = 1, 2, 4
PLANE_MASKS = (0, X_BIT, Y_BIT, X_BIT | Y_BIT)

epsilon = 1e-05
masked_score = -1e30
score_scale = HEAD_DIM ** (-0.5)
f32 = jnp.float32
bf16 = jnp.bfloat16


def mm(left, right):
    return jnp.dot(left, right, preferred_element_type=f32)


def mm_nt(left, right):
    return lax.dot_general(left, right, (((1,), (1,)), ((), ())), preferred_element_type=f32)


def total(*terms):
    acc = terms[0].astype(f32)
    for term in terms[1:]:
        acc = acc + term.astype(f32)
    return acc


def add_low(*terms):
    return total(*terms).astype(bf16)


def hop(array, dp_mask, z_mask):
    dp_count = lax.axis_size("dp")
    pairs = [
        (d * TP + z, (d ^ dp_mask) * TP + (z ^ z_mask)) for d in range(dp_count) for z in range(TP)
    ]
    return lax.ppermute(array, ("dp", "tp"), pairs)


def place(array):
    dp_count = lax.axis_size("dp")
    pairs = []
    for d in range(dp_count):
        for z in range(TP):
            here = d * TP + z
            away = (d ^ CORE) * TP + (z ^ 2)
            pairs.append((here, here if (d & 1) == z // 2 else away))
    return lax.ppermute(array, ("dp", "tp"), pairs)


def piece_kernel(info, w_in_hbm, w_back_ref, bias_ref, piece_ref, flip_scr, sem):
    start = pl.multiple_of(info[1] * SLICE, SLICE)
    copy = pltpu.make_async_copy(
        w_in_hbm.at[pl.ds(start, SLICE), :], piece_ref.at[pl.ds(0, SLICE), :], sem
    )
    copy.start()
    flip_scr[...] = w_back_ref[...].T
    piece_ref[SLICE : 2 * SLICE, :] = flip_scr[pl.ds(start, SLICE), :]
    bias = bias_ref[...].astype(f32).reshape(1, WIDTH)
    piece_ref[2 * SLICE :, :] = jnp.broadcast_to(bias, (VEC_ROWS, WIDTH)).astype(bf16)
    copy.wait()


def group_kernel(info, w_ref, bias_query_ref, bias_value_ref, w_out, b_out):
    bias_query = bias_query_ref[...].astype(f32).reshape(1, WIDTH)
    bias_value = bias_value_ref[...].astype(f32).reshape(1, WIDTH)
    b_out[...] = jnp.zeros_like(b_out)
    for g in range(TP):

        @pl.when(info[0] == g)
        def _(g=g):
            cols = slice(g * GROUP_WIDTH, (g + 1) * GROUP_WIDTH)
            for kind in range(3):
                lo = kind * GROUP_WIDTH
                w_out[:, lo : lo + GROUP_WIDTH] = w_ref[:, kind * WIDTH :][:, cols]
            b_out[:, :GROUP_WIDTH] = bias_query[:, cols]
            b_out[:, 2 * GROUP_WIDTH :] = bias_value[:, cols]


def block_bias(quarter, native, random_refs, head, chunk):
    shape = (LENGTH // BLOCK, QUARTER)
    row = lax.broadcasted_iota(jnp.int32, shape, 0)
    lane_block = lax.broadcasted_iota(jnp.int32, shape, 1) // BLOCK
    key_block = ((row // TP) ^ quarter) * TP + (row % TP)
    base = TP * (quarter ^ chunk)
    query_block = base + lane_block
    last = LENGTH // BLOCK - 1
    allowed = (key_block == 0) | (key_block == last)
    allowed |= (query_block == 0) | (query_block == last)
    allowed |= jnp.abs(key_block - query_block) <= 1
    for pick in range(3):
        chosen = jnp.zeros(shape, jnp.int32)
        for b in range(TP):
            at = (head * (LENGTH // BLOCK) + base + b) * 3 + pick
            value = jnp.where(native == 1, random_refs[0][at], random_refs[1][at])
            chosen = jnp.where(lane_block == b, value, chosen)
        allowed |= key_block == chosen
    return jnp.where(allowed, 0.0, masked_score).astype(f32)


def biased(scores, bias):
    blocks = LENGTH // BLOCK
    spread = scores.reshape(blocks, BLOCK, QUARTER) + bias.reshape(blocks, 1, QUARTER)
    return spread.reshape(LENGTH, QUARTER)


PACKED = QUARTER + QUARTER // 2


def pack_heads(ref, row, pieces):
    end = row + QUARTER
    ref[row:end, 0:64] = pieces[0]
    ref[row:end, 64:128] = pieces[1]
    ref[end : row + PACKED, 0:64] = pieces[2][: QUARTER // 2]
    ref[end : row + PACKED, 64:128] = pieces[2][QUARTER // 2 :]


def unpack_heads(ref, row):
    end = row + QUARTER
    third = jnp.concatenate([ref[end : row + PACKED, 0:64], ref[end : row + PACKED, 64:128]], axis=0)
    return [ref[row:end, 0:64], ref[row:end, 64:128], third]


def attention_kernel(info, rnd_own, rnd_other, t0, t1, t2, t3, w_ref, b_ref, a0, a13, a2, *rest):
    heads, lse_ref, out_scr = rest[:9], rest[9], rest[10]
    quarter, native = info[0], info[4]
    for slot, t_ref in enumerate((t0, t1, t2, t3)):
        rows = pl.ds(slot * QUARTER, QUARTER)
        proj = mm(t_ref[...], w_ref[...]) + b_ref[...]
        for h in range(GROUP):
            for kind in range(3):
                lo = kind * GROUP_WIDTH + h * HEAD_DIM
                piece = proj[:, lo : lo + HEAD_DIM].astype(bf16)
                if kind == 0:
                    piece = (piece.astype(f32) * score_scale).astype(bf16)
                heads[3 * h + kind][rows, :] = piece
    for h in range(GROUP):
        q_ref, k_ref, v_ref = heads[3 * h : 3 * h + 3]
        keys = k_ref[...]
        values_t = v_ref[...].T

        def chunk_step(chunk, carry, h=h, q_ref=q_ref, keys=keys, values_t=values_t):
            rows = pl.ds(pl.multiple_of(chunk * QUARTER, QUARTER), QUARTER)
            scores = mm_nt(keys, q_ref[rows, :])
            head = quarter * GROUP + h
            scores = biased(scores, block_bias(quarter, native, (rnd_own, rnd_other), head, chunk))
            row_max = jnp.max(scores, axis=0, keepdims=True)
            probs = jnp.exp(scores - row_max)
            row_sum = jnp.sum(probs, axis=0, keepdims=True)
            out_t = mm(values_t, probs.astype(bf16)) / row_sum
            out_scr[h, rows, :] = out_t.T.astype(bf16)
            lse_ref[pl.ds(h * TP + chunk, 1), :] = row_max + jnp.log(row_sum)
            return carry

        lax.fori_loop(0, TP, chunk_step, 0, unroll=True)
    for slot, (a_ref, row) in enumerate(((a0, 0), (a13, 0), (a2, 0), (a13, PACKED))):
        rows = slice(slot * QUARTER, (slot + 1) * QUARTER)
        pack_heads(a_ref, row, [out_scr[h, rows, :] for h in range(GROUP)])


def attention_back_kernel(
    h, info, rnd_own, rnd_other, q_ref, k_ref, v_ref, lse_ref, g0, g1, g2, g3, out_ref, sums_ref, do_scr, dk_scr, dv_scr, dq_scr
):
    quarter, native = info[0], info[4]
    for slot, g_ref in enumerate((g0, g1, g2, g3)):
        do_scr[slot * QUARTER : (slot + 1) * QUARTER, :] = unpack_heads(g_ref, 0)[h]
    keys = k_ref[...]
    keys_t = keys.T
    values = v_ref[...]
    dk_scr[...] = jnp.zeros_like(dk_scr)
    dv_scr[...] = jnp.zeros_like(dv_scr)

    def chunk_step(chunk, carry):
        rows = pl.ds(pl.multiple_of(chunk * QUARTER, QUARTER), QUARTER)
        queries = q_ref[rows, :]
        grad_out = do_scr[rows, :]
        scores = mm_nt(keys, queries)
        head = quarter * GROUP + h
        scores = biased(scores, block_bias(quarter, native, (rnd_own, rnd_other), head, chunk))
        probs = jnp.exp(scores - lse_ref[pl.ds(h * TP + chunk, 1), :])
        grad_probs = mm_nt(values, grad_out)
        delta = jnp.sum(probs * grad_probs, axis=0, keepdims=True)
        grad_scores = (probs * (grad_probs - delta)).astype(bf16)
        dv_scr[...] += mm(probs.astype(bf16), grad_out)
        dk_scr[...] += mm(grad_scores, queries)
        dq_t = mm(keys_t, grad_scores) * score_scale
        dq_scr[rows, :] = dq_t.T
        return carry

    lax.fori_loop(0, TP, chunk_step, 0, unroll=True)
    for n, scr in enumerate((dq_scr, dk_scr, dv_scr)):
        out_ref[:, n * HEAD_DIM : (n + 1) * HEAD_DIM] = scr[...].astype(bf16)
    sums_ref[...] = jnp.zeros_like(sums_ref)
    sums_ref[0:1, :] = jnp.sum(out_ref[...].astype(f32), axis=0, keepdims=True)


PIECE = 2 * SLICE + VEC_ROWS


def held_kernel(own, by_x, by_y, third, third_x, third_y, out):
    for q in range(2):
        for p, ref in enumerate((own, by_x, by_y)):
            at = (4 * q + p) * PIECE
            out[at : at + PIECE] = ref[q * PIECE : (q + 1) * PIECE]
        at = (4 * q + 3) * PIECE
        out[at : at + CUT] = third_y[PIECE + q * CUT : PIECE + (q + 1) * CUT]
        out[at + CUT : at + PIECE] = third_x[PIECE + q * (PIECE - CUT) : PIECE + (q + 1) * (PIECE - CUT)]
    for p, ref in enumerate((third, third_x, third_y)):
        at = (8 + p) * PIECE
        out[at : at + PIECE] = ref[:PIECE]


def assemble_kernel(info, held, other, last_in, last_back, other_last, w_out_ref, w_in_s, w_back_s, w_out_s, bias_s):
    quarter, mine = info[0], info[1]
    for slot in range(TP):
        start = pl.multiple_of((quarter ^ slot) * GROUP_WIDTH, GROUP_WIDTH)
        w_out_s[slot * GROUP_WIDTH : (slot + 1) * GROUP_WIDTH, :] = w_out_ref[pl.ds(start, GROUP_WIDTH), :]
    for side, main in enumerate((held, other)):
        for q in range(TP - 1):
            for p in range(4):
                start = pl.multiple_of((mine ^ PLANE_MASKS[p] ^ side) * SLICE, SLICE)
                at = (4 * q + p) * PIECE
                if q == TP - 2 and p == 3:
                    left = other_last[:SLICE] if side else last_in[...]
                    right = other_last[SLICE : 2 * SLICE] if side else last_back[:SLICE]
                else:
                    left, right = main[at : at + SLICE], main[at + SLICE : at + 2 * SLICE]
                w_in_s[q, pl.ds(start, SLICE), :] = left
                w_back_s[q, pl.ds(start, SLICE), :] = right
                if p == 0 and side == 0:
                    bias_s[q] = main[at + 2 * SLICE : at + PIECE]


def row(ref):
    return ref[...].astype(f32).reshape(1, WIDTH)


def spread(h):
    centred = h - jnp.mean(h, axis=-1, keepdims=True)
    scale = lax.rsqrt(jnp.mean(centred * centred, axis=-1, keepdims=True) + epsilon)
    return centred * scale, scale


def spread_back(grad, gain, normal, scale):
    weighted = grad * gain
    mean_one = jnp.mean(weighted, axis=-1, keepdims=True)
    mean_two = jnp.mean(weighted * normal, axis=-1, keepdims=True)
    return scale * (weighted - mean_one - normal * mean_two)


def ffn_kernel(info, t_ref, a0, a1, a2, a3, *rest):
    bias_out_ref, gain_one_ref, shift_one_ref, bias_back_ref, gain_two_ref, shift_two_ref, bias_in_ref = rest[:7]
    cot_ref, w_out_s, w_in_ref, w_back_ref, w_in_s, w_back_s, bias_s = rest[7:14]
    lo_ref, first_ref, second_ref, x_ref, gb_ref, act_ref, gp_ref, att_ref, vec_ref = rest[14:]
    for slot, a_ref in enumerate((a0, a1, a2, a3)):
        for h, piece in enumerate(unpack_heads(a_ref, 0)):
            lo = slot * GROUP_WIDTH + h * HEAD_DIM
            att_ref[:, lo : lo + HEAD_DIM] = piece
    first_in = t_ref[...].astype(f32) + (mm(att_ref[...], w_out_s[...]) + row(bias_out_ref))
    first_ref[...] = first_in
    first_norm = spread(first_in)[0] * row(gain_one_ref) + row(shift_one_ref)
    x = first_norm.astype(bf16)
    x_ref[...] = x
    branch = jnp.zeros((QUARTER, WIDTH), f32)
    for q in range(TP):
        cols = slice(q * WIDTH, (q + 1) * WIDTH)
        bias_q = bias_s[q - 1, 0:1, :].astype(f32) if q else row(bias_in_ref)
        pre = mm(x, w_in_s[q - 1] if q else w_in_ref[...]) + bias_q
        inner = 0.7978845608028654 * (pre + 0.044715 * pre * pre * pre)
        tanh = jnp.tanh(inner)
        half = 0.5 * (1.0 + tanh)
        act = (pre * half).astype(bf16)
        act_ref[:, cols] = act
        slope = 0.7978845608028654 * (1.0 + 3.0 * 0.044715 * pre * pre)
        gp_ref[:, cols] = half + 0.5 * pre * (1.0 - tanh * tanh) * slope
        branch = branch + (mm_nt(act, w_back_s[q - 1]) if q else mm(act, w_back_ref[...]))
    second_in = first_norm + branch + row(bias_back_ref)
    normal_two, scale_two = spread(second_in)
    lo_ref[...] = (normal_two * row(gain_two_ref) + row(shift_two_ref)).astype(bf16)
    grad_out = cot_ref[...].astype(f32)
    grad_second = spread_back(grad_out, row(gain_two_ref), normal_two, scale_two)
    second_ref[...] = grad_second
    grad_branch = grad_second.astype(bf16)
    gb_ref[...] = grad_branch
    vec_ref[...] = jnp.zeros_like(vec_ref)
    vec_ref[0:1, :] = jnp.sum(grad_out, axis=0, keepdims=True)
    vec_ref[1:2, :] = jnp.sum(grad_out * normal_two, axis=0, keepdims=True)
    vec_ref[2:3, :] = jnp.sum(grad_branch.astype(f32), axis=0, keepdims=True)


def position_mask(position, order):
    mask = 0
    for n, bit in enumerate(order):
        if (position >> (2 - n)) & 1:
            mask |= bit
    return mask


FFN_ORDERS = ((CORE, X_BIT, Y_BIT), (CORE, Y_BIT, X_BIT))


def weight_grads(info, left, right, keep, send, flip_scr, lhs_scr):
    mine = info[1]
    flip_scr[...] = left[...].T
    for n, order in enumerate(FFN_ORDERS):
        for p in range(SLOTS):
            start = pl.multiple_of((mine ^ position_mask(p, order)) * SLICE, SLICE)
            lhs_scr[p * SLICE : (p + 1) * SLICE, :] = flip_scr[pl.ds(start, SLICE), :]
        for pair in range(2):
            q = 2 * n + pair
            product = mm(lhs_scr[...], right[:, q * WIDTH : (q + 1) * WIDTH]).astype(bf16)
            for p in range(SLOTS):
                out = send if p >= SLOTS // 2 else keep
                out[n, p % (SLOTS // 2), pair] = product[p * SLICE : (p + 1) * SLICE, :]


def ffn_back_kernel(info, first_ref, second_ref, gb_ref, gp_ref, gain_one_ref, vec_in, *rest):
    w_out_s, w_in_ref, w_back_ref, w_in_s, w_back_s, x_ref, att_ref = rest[:7]
    g0, g13, g2, gin_ref, vec_ref, keep, send, go_keep, go_send = rest[7:16]
    gpre_ref, flip_scr, lhs_scr = rest[16:]
    grad_branch = gb_ref[...]
    grad_first = second_ref[...]
    vec_ref[...] = vec_in[...]
    for q in range(TP):
        cols = slice(q * WIDTH, (q + 1) * WIDTH)
        grad_act = mm(grad_branch, w_back_s[q - 1]) if q else mm_nt(grad_branch, w_back_ref[...])
        grad_pre = (grad_act * gp_ref[:, cols]).astype(bf16)
        gpre_ref[:, cols] = grad_pre
        vec_ref[pl.ds(6 + (info[2] ^ q), 1), :] = jnp.sum(grad_pre.astype(f32), axis=0, keepdims=True)
        grad_first = grad_first + mm_nt(grad_pre, w_in_s[q - 1] if q else w_in_ref[...])
    normal_one, scale_one = spread(first_ref[...])
    vec_ref[3:4, :] = jnp.sum(grad_first, axis=0, keepdims=True)
    vec_ref[4:5, :] = jnp.sum(grad_first * normal_one, axis=0, keepdims=True)
    grad_in = spread_back(grad_first, row(gain_one_ref), normal_one, scale_one)
    gin_ref[...] = grad_in
    grad_mixed = grad_in.astype(bf16)
    vec_ref[5:6, :] = jnp.sum(grad_mixed.astype(f32), axis=0, keepdims=True)
    grad_att = mm_nt(grad_mixed, w_out_s[...]).astype(bf16)
    for slot, (g_ref, row_at) in enumerate(((g0, 0), (g13, 0), (g2, 0), (g13, PACKED))):
        lo = slot * GROUP_WIDTH
        pack_heads(
            g_ref, row_at, [grad_att[:, lo + h * HEAD_DIM : lo + (h + 1) * HEAD_DIM] for h in range(GROUP)]
        )
    weight_grads(info, x_ref, gpre_ref, keep, send, flip_scr, lhs_scr)
    product = mm(grad_mixed.T, att_ref[...]).astype(bf16)
    go_keep[...] = product[:, : 2 * GROUP_WIDTH]
    go_send[...] = product[:, 2 * GROUP_WIDTH :]


ORDER_LA = (4, 2, 1)
ORDER_LB = (2, 4, 1)


HALF = WIDTH // 2
HELD = SLOTS // 2 * SLICE


def flip_kernel(t0, t1, t2, t3, out_ref):
    for slot, t_ref in enumerate((t0, t1, t2, t3)):
        out_ref[:, slot * QUARTER : (slot + 1) * QUARTER] = t_ref[...].T


def qkv_grad_kernel(
    info, tokens_t, gh0, gh1, gh2, go_own, go_near, vec_ref, s0, s1, s2, la_keep, la_send, lb_keep, lb_send, out_scr
):
    quarter, here = info[0], info[3]
    for h, gh_ref in enumerate((gh0, gh1, gh2)):
        product = mm(tokens_t[...], gh_ref[...]).astype(bf16)
        for kind in range(3):
            lo = kind * GROUP_WIDTH + h * HEAD_DIM
            out_scr[:, lo : lo + HEAD_DIM] = product[:, kind * HEAD_DIM : (kind + 1) * HEAD_DIM]
    add_to(out_scr.at[:, 3 * GROUP_WIDTH :], go_own[...], go_near[...])
    for keep, send, order, lo in (
        (la_keep, la_send, ORDER_LA, 0),
        (lb_keep, lb_send, ORDER_LB, HALF),
    ):
        for p in range(SLOTS):
            start = pl.multiple_of((here ^ position_mask(p, order)) * SLICE, SLICE)
            out = send if p >= SLOTS // 2 else keep
            row = p % (SLOTS // 2) * SLICE
            out[row : row + SLICE, :] = out_scr[pl.ds(start, SLICE), lo : lo + HALF]
    placed = []
    for kind in (0, 2):
        cols = slice(kind * HEAD_DIM, (kind + 1) * HEAD_DIM)
        piece = jnp.concatenate([sums[0:1, cols] for sums in (s0, s1, s2)], axis=1)
        placed.append(
            jnp.concatenate([jnp.where(quarter == g, piece, 0.0) for g in range(TP)], axis=1)
        )
    vectors = jnp.concatenate([vec_ref[0:10, :]] + placed + [vec_ref[12:VEC_ROWS, :]], axis=0)
    vectors = vectors.astype(bf16)
    for out in (la_keep, la_send, lb_keep, lb_send):
        out[HELD : HELD + VEC_ROWS, :] = vectors[:, :HALF]
        out[HELD + VEC_ROWS :, :] = vectors[:, HALF:]


def token_grad_kernel(gh0, gh1, gh2, w_ref, keep_ref, send_ref, all_scr):
    for h, gh_ref in enumerate((gh0, gh1, gh2)):
        for kind in range(3):
            lo = kind * GROUP_WIDTH + h * HEAD_DIM
            all_scr[:, lo : lo + HEAD_DIM] = gh_ref[:, kind * HEAD_DIM : (kind + 1) * HEAD_DIM]
    half = LENGTH // 2
    send_ref[...] = mm_nt(all_scr[half:, :], w_ref[...]).astype(bf16)
    keep_ref[...] = mm_nt(all_scr[:half, :], w_ref[...]).astype(bf16)


AT_ONCE = 2


def final_kernel(info, c_ref, c_other, f_ref, f_other, low_tokens, low_out, *rest):
    qkv_out, out_out, w_in_out, w_back_out, layer_out, token_out = rest[:6]
    vec_outs, (all_scr, flip_scr, out_scr, back_scr) = rest[6:15], rest[15:]
    quarter, mine, z_here, here = info[0], info[1], info[2], info[3]
    block = pl.program_id(0)
    count = 16 * SLICE

    def piece(group, at):
        group_off, block_off = quarter ^ group, here ^ at
        xy = ((block_off >> 2) & 1) + (block_off & 2)
        return all_scr[(group_off >> 1) * 16 + xy * 4 + (group_off & 1) + 2 * (block_off & 1)]

    def ffn_piece(at, part):
        mask = mine ^ at
        nth = (((mask >> 1) & 1) + ((mask >> 2) & 1) * 2) * 2 + part
        return jnp.where((mask & 1) == 1, f_other[nth].astype(f32), f_ref[nth].astype(f32))

    @pl.when(block == 0)
    def _():
        for side, ref in enumerate((c_ref, c_other)):
            for n in range(16):
                all_scr[side * 16 + n] = ref[n * SLICE : (n + 1) * SLICE, :]
        vectors = total(c_ref[count:, :], c_other[count:, :])
        bias_in = jnp.zeros((1, WIDTH), f32)
        for q in range(TP):
            bias_in = jnp.where(z_here == q, vectors[6 + q : 7 + q, :], bias_in)
        for out, n in zip(vec_outs[:8], (0, 1, 2, 3, 4, 5, 10, 11)):
            out[...] = vectors[n]
        vec_outs[8][...] = bias_in[0]
        for at in range(SLOTS):
            rows = slice(at * SLICE, (at + 1) * SLICE)
            last = [piece(group, at)[:, 3 * GROUP_WIDTH :] for group in range(TP)]
            flip_scr[rows, :] = jnp.concatenate(last, axis=1).astype(f32)
            back_scr[rows, :] = ffn_piece(at, 1)
        out_scr[...] = flip_scr[...].T
        flip_scr[...] = back_scr[...].T

    for n in range(AT_ONCE):
        here_block = block * AT_ONCE + n
        rows = slice(n * SLICE, (n + 1) * SLICE)
        pieces = [piece(group, here_block) for group in range(TP)]
        for kind in range(3):
            cols = slice(kind * GROUP_WIDTH, (kind + 1) * GROUP_WIDTH)
            joined = jnp.concatenate([part[:, cols] for part in pieces], axis=1)
            qkv_out[rows, kind * WIDTH : (kind + 1) * WIDTH] = joined.astype(f32)
        w_in_out[rows, :] = ffn_piece(here_block, 0)
    rows = pl.ds(pl.multiple_of(block * AT_ONCE * SLICE, SLICE), AT_ONCE * SLICE)
    out_out[...] = out_scr[rows, :]
    w_back_out[...] = flip_scr[rows, :]
    layer_out[...] = low_out[...]
    token_out[...] = low_tokens[...]


def add_to(out, *terms):
    out[...] = add_low(*terms)


def join_kernel(*refs):
    out, at = refs[-1], 0
    for ref in refs[:-1]:
        out[at : at + ref.shape[0]] = ref[...]
        at += ref.shape[0]


def diag_kernel(by_x, by_y, first, second):
    half = first.shape[0]
    first[...] = by_x[:half]
    second[...] = by_y[half:]


CUT = SLICE


def mix_kernel(by_x, by_y, own, to_x, to_y):
    to_x[:PIECE] = own[...]
    to_y[:PIECE] = own[...]
    for n in range(2):
        to_x[PIECE + n * (PIECE - CUT) : PIECE + (n + 1) * (PIECE - CUT)] = by_y[n * PIECE + CUT : (n + 1) * PIECE]
        to_y[PIECE + n * CUT : PIECE + (n + 1) * CUT] = by_x[n * PIECE : n * PIECE + CUT]


def last_mix_kernel(by_x, by_y, to_x, to_y):
    to_x[...] = by_y[CUT:PIECE]
    to_y[...] = by_x[:CUT]


def level_one_kernel(keep, other, first, second):
    add_to(first, keep[0, 2:], other[0, 2:])
    add_to(second, keep[1, 2:], other[1, 2:])


def middle_kernel(in_keep, in_other, back_keep, back_other, back_x, back_y, to_x, to_y):
    for n in range(2):
        out = to_y if n else to_x
        for p in range(2):
            for pair in range(2):
                add_to(out.at[2 * p + pair], in_keep[n, 2 + p, pair], in_other[n, 2 + p, pair])
    for pair in range(2):
        add_to(to_y.at[4 + pair], back_keep[0, 1, pair], back_other[0, 1, pair], back_x[1, pair])
        add_to(to_x.at[4 + pair], back_keep[1, 1, pair], back_other[1, 1, pair], back_y[1, pair])


def in_two_kernel(keep, other, by_x, by_y, first, second):
    for pair in range(2):
        add_to(first.at[pair], keep[0, 1, pair], other[0, 1, pair], by_x[2 + pair])
        add_to(second.at[pair], keep[1, 1, pair], other[1, 1, pair], by_y[2 + pair])


def in_plane_kernel(keep, other, by_x, by_y, by_xy, by_yx, near, kept):
    for q in range(TP):
        order, pair = q // 2, q % 2
        first, second = (by_x, by_xy) if order == 0 else (by_y, by_yx)
        out = near if q % 2 else kept
        add_to(out.at[q // 2], keep[order, 0, pair], other[order, 0, pair], first[pair], second[pair])


def back_plane_kernel(keep, other, by_x, by_y, mid_x, mid_y, near, kept):
    for q in range(TP):
        order, pair = q // 2, q % 2
        first, second = (by_x, mid_y) if order == 0 else (by_y, mid_x)
        out = near if q % 2 else kept
        add_to(out.at[q // 2], keep[order, 0, pair], other[order, 0, pair], first[0, pair], second[4 + pair])


def far_kernel(kept, near, far):
    add_to(far, kept[1], near[1])


def last_kernel(kept_a, near_a, far_a, kept_b, near_b, far_b, out):
    add_to(out.at[0], kept_a[0], near_a[0], far_a[...])
    add_to(out.at[1], kept_b[0], near_b[0], far_b[...])


def go_kernel(keep, other, own, send):
    add_to(own, keep[:, :GROUP_WIDTH], other[:, :GROUP_WIDTH])
    add_to(send, keep[:, GROUP_WIDTH:], other[:, GROUP_WIDTH:])


def near_kernel(keep, other, out):
    add_to(out, keep[QUARTER:], other[QUARTER:])


def tokens_kernel(keep, other, near, grad_in, out_here, tokens, again):
    add_to(tokens, keep[:QUARTER], other[:QUARTER], near[...], grad_in[...])
    again[...] = out_here[...]


TWO = 2 * SLICE


def qkv_two_kernel(la, ra, lb, rb, la_out, lb_out):
    add_to(la_out, la[TWO:], ra[TWO:])
    add_to(lb_out, lb[TWO:HELD], rb[TWO:HELD])


def qkv_three_kernel(la, ra, ra2, lb, rb, rb2, out):
    add_to(out.at[:TWO, :HALF], la[:TWO], ra[:TWO], ra2[:TWO])
    add_to(out.at[:TWO, HALF:], lb[:TWO], rb[:TWO], rb2[...])
    for n in range(2):
        rows = slice(HELD + n * VEC_ROWS, HELD + (n + 1) * VEC_ROWS)
        rows_two = slice(TWO + n * VEC_ROWS, TWO + (n + 1) * VEC_ROWS)
        add_to(out.at[TWO:, n * HALF : (n + 1) * HALF], la[rows], ra[rows], ra2[rows_two])


def qkv_four_kernel(own, other, out):
    add_to(out.at[:SLICE], own[:SLICE], other[SLICE:TWO])
    add_to(out.at[SLICE:TWO], own[SLICE:TWO], other[:SLICE])
    add_to(out.at[TWO:], own[TWO:], other[TWO:])


def mix_l_kernel(by_x, by_y, other, to_x, to_y):
    to_x[:TWO] = other[:TWO]
    to_x[TWO:] = by_y[SLICE:TWO]
    to_y[:TWO] = other[:TWO]
    to_y[TWO:] = by_x[:SLICE]


def diag_l_kernel(by_x, by_y, to_x, to_y):
    to_x[...] = by_y[SLICE:TWO]
    to_y[...] = by_x[:SLICE]


def plane_l_kernel(own, other, x_own, y_own, x_other, y_other, d_x, d_y, out):
    diag_own = (y_other[TWO:], x_other[TWO:])
    diag_other = (d_y[...], d_x[...])
    places = (
        ((own[:SLICE], own[SLICE:TWO]), (other[:SLICE], other[SLICE:TWO])),
        ((x_own[:SLICE], x_own[SLICE:TWO]), (x_other[:SLICE], x_other[SLICE:TWO])),
        ((y_own[:SLICE], y_own[SLICE:TWO]), (y_other[:SLICE], y_other[SLICE:TWO])),
        (diag_own, diag_other),
    )
    for p, (here, there) in enumerate(places):
        for slot in range(TP):
            at = (p * TP + slot) * SLICE
            out[at : at + SLICE] = (there if slot % 2 else here)[slot // 2]
    add_to(out.at[16 * SLICE :], own[TWO:], other[TWO:])


VMEM = pl.BlockSpec(memory_space=pltpu.VMEM)
SMEM = pl.BlockSpec(memory_space=pltpu.SMEM)
HBM = pl.BlockSpec(memory_space=pl.ANY)


def call(kernel, in_specs, outs, scratch, vmem_mib, name, deps=()):
    count, extra = len(in_specs), len(deps)

    def body(*refs):
        kernel(*refs[:count], *refs[count + extra :])

    run = pl.pallas_call(
        body,
        out_shape=[jax.ShapeDtypeStruct(shape, dtype) for shape, dtype in outs],
        in_specs=list(in_specs) + [HBM] * extra,
        out_specs=[VMEM] * len(outs),
        scratch_shapes=scratch,
        compiler_params=pltpu.CompilerParams(vmem_limit_bytes=vmem_mib * 1024 * 1024),
        cost_estimate=pl.CostEstimate(flops=1, bytes_accessed=1, transcendentals=0),
        name=name,
    )
    return lambda *arrays: run(*arrays, *deps)


def step(kernel, name, outs, *arrays, deps=()):
    shapes = [(shape, bf16) for shape in outs]
    result = call(kernel, [VMEM] * len(arrays), shapes, [], 12, name, deps)(*arrays)
    return result[0] if len(outs) == 1 else result


def per_device(
    tokens,
    w_qkv,
    bias_query,
    bias_value,
    w_out,
    bias_out,
    gain_attn,
    shift_attn,
    w_in,
    bias_in,
    w_back,
    bias_back,
    gain_ffn,
    shift_ffn,
    random_blocks,
    cotangent,
):
    dp_count = lax.axis_size("dp")
    d = lax.axis_index("dp")
    z = lax.axis_index("tp")
    core = d & 1
    quarter = (z & 1) + 2 * core
    mine = d & (SLOTS - 1)
    here = ((d >> 1) & 1) * 4 + ((d >> 2) & 1) * 2 + (z >> 1)
    native = (core == z // 2).astype(jnp.int32)
    info = jnp.stack([quarter, mine, z, here, native]).astype(jnp.int32)
    extra_bits = [1 << b for b in range(3, dp_count.bit_length() - 1)]

    own_tokens = place(tokens[0])
    piece = call(
        piece_kernel,
        [SMEM, HBM, VMEM, VMEM],
        [((2 * SLICE + VEC_ROWS, WIDTH), bf16)],
        [pltpu.VMEM((WIDTH, WIDTH), bf16), pltpu.SemaphoreType.DMA],
        8,
        "piece",
    )(info, w_in, w_back, bias_in)[0]
    piece_one = hop(piece, 0, 1)
    piece_two = hop(piece, 0, 2)
    random_own = random_blocks.reshape(-1)
    random_other = hop(random_own, CORE, 0)
    w_group, bias_group = call(
        group_kernel,
        [SMEM, VMEM, VMEM, VMEM],
        [((WIDTH, 3 * GROUP_WIDTH), bf16), ((1, 3 * GROUP_WIDTH), f32)],
        [],
        16,
        "group",
    )(info, w_qkv, bias_query, bias_value)
    near_tokens = hop(own_tokens, 0, 1)
    core_tokens = hop(own_tokens, CORE, 0)
    far_tokens = hop(near_tokens, CORE, 0)
    part_one = step(
        join_kernel, "pair", [(2 * PIECE, WIDTH)], piece_one, piece_two, deps=(own_tokens, w_group, random_other)
    )
    x_one = hop(part_one, X_BIT, 0)
    y_one = hop(part_one, Y_BIT, 0)
    piece_three = hop(piece_two, 0, 1)
    cot = place(cotangent[0])
    to_x, to_y = step(
        mix_kernel,
        "mix",
        [(3 * PIECE - 2 * CUT, WIDTH), (PIECE + 2 * CUT, WIDTH)],
        x_one,
        y_one,
        piece_three,
        deps=(near_tokens,),
    )
    x_three = hop(to_x, X_BIT, 0)
    y_three = hop(to_y, Y_BIT, 0)

    packed = ((PACKED, 2 * HEAD_DIM), bf16)
    double = ((2 * PACKED, 2 * HEAD_DIM), bf16)
    per_head = ((LENGTH, HEAD_DIM), bf16)
    token_slots = (own_tokens, near_tokens, core_tokens, far_tokens)
    a0, a13, a2, *heads = call(
        attention_kernel,
        [SMEM] * 3 + [VMEM] * 6,
        [packed, double, packed] + [per_head] * 9 + [((16, QUARTER), f32)],
        [pltpu.VMEM((GROUP, LENGTH, HEAD_DIM), bf16)],
        24,
        "attention",
        (to_x, core_tokens),
    )(info, random_own, random_other, *token_slots, w_group, bias_group)
    heads, lse = heads[:9], heads[9]
    a1 = hop(a13, 0, 1)
    a2 = hop(a2, CORE, 0)
    a3 = hop(a1[PACKED:], CORE, 0)
    to_x, to_y = step(
        last_mix_kernel,
        "mix_last",
        [(PIECE - CUT, WIDTH), (CUT, WIDTH)],
        x_three,
        y_three,
        deps=(a0, cot),
    )
    last_back = hop(to_x, X_BIT, 0)
    last_in = hop(to_y, Y_BIT, 0)
    held = step(
        held_kernel,
        "held",
        [(11 * PIECE, WIDTH)],
        part_one,
        x_one,
        y_one,
        piece_three,
        x_three,
        y_three,
        deps=(a2, cot),
    )
    tokens_t = call(flip_kernel, [VMEM] * 4, [((WIDTH, LENGTH), bf16)], [], 8, "flip_tokens", (a1, held))(
        *token_slots
    )[0]
    last = step(join_kernel, "last_piece", [(PIECE, WIDTH)], last_in, last_back, deps=(tokens_t,))
    quarters = ((TP - 1, WIDTH, WIDTH), bf16)
    w_in_s, w_back_s, w_out_s, bias_s = call(
        assemble_kernel,
        [SMEM] + [VMEM] * 6,
        [quarters, quarters, ((WIDTH, WIDTH), bf16), ((TP - 1, VEC_ROWS, WIDTH), bf16)],
        [],
        20,
        "assemble",
    )(info, held, hop(held, CORE, 0), last_in, last_back, hop(last, CORE, 0), w_out)

    rows = ((QUARTER, WIDTH), bf16)
    wide = ((QUARTER, TP * WIDTH), bf16)
    rows_f32 = ((QUARTER, WIDTH), f32)
    vec_rows = ((VEC_ROWS, WIDTH), f32)
    out_here, first_in, grad_second, ffn_input, grad_branch, activated, gelu_slope, attended, vectors = call(
        ffn_kernel,
        [SMEM] + [VMEM] * 19,
        [rows, rows_f32, rows_f32, rows, rows, wide, ((QUARTER, TP * WIDTH), f32), rows, vec_rows],
        [],
        20,
        "ffn",
        (tokens_t,),
    )(
        info,
        own_tokens,
        a0,
        a1,
        a2,
        a3,
        bias_out,
        gain_attn,
        shift_attn,
        bias_back,
        gain_ffn,
        shift_ffn,
        bias_in,
        cot,
        w_out_s,
        w_in,
        w_back,
        w_in_s,
        w_back_s,
        bias_s,
    )
    pairs = ((2, SLOTS // 2, 2, SLICE, WIDTH), bf16)
    halves = ((WIDTH, 2 * GROUP_WIDTH), bf16)
    flips = [pltpu.VMEM((WIDTH, QUARTER), bf16), pltpu.VMEM((WIDTH, QUARTER), bf16)]
    back_keep, back_send = call(
        weight_grads, [SMEM] + [VMEM] * 2, [pairs] * 2, flips, 12, "back_grads"
    )(info, grad_branch, activated)
    back_other = hop(back_send, CORE, 0)

    g0, g13, g2, grad_in, vectors, in_keep, in_send, go_keep, go_send = call(
        ffn_back_kernel,
        [SMEM] + [VMEM] * 13,
        [packed, double, packed, rows_f32, vec_rows] + [pairs] * 2 + [halves] * 2,
        [pltpu.VMEM((QUARTER, TP * WIDTH), bf16)] + flips,
        20,
        "ffn_back",
        (back_keep,),
    )(
        info,
        first_in,
        grad_second,
        grad_branch,
        gelu_slope,
        gain_attn,
        vectors,
        w_out_s,
        w_in,
        w_back,
        w_in_s,
        w_back_s,
        ffn_input,
        attended,
    )
    g1 = hop(g13, 0, 1)
    g2 = hop(g2, CORE, 0)
    g3 = hop(g1[PACKED:], CORE, 0)

    first_level = [(2, 2, SLICE, WIDTH)] * 2
    def hop_pair(pair, first, second):
        return hop(pair[0], first, 0), hop(pair[1], second, 0)

    back_sums = step(level_one_kernel, "back_one", first_level, back_keep, back_other, deps=(g13,))
    back_x, back_y = hop_pair(back_sums, X_BIT, Y_BIT)
    in_other = hop(in_send, CORE, 0)
    go_other = hop(go_send, CORE, 0)

    def head_back(h, deps):
        return call(
            functools.partial(attention_back_kernel, h),
            [SMEM] * 3 + [VMEM] * 8,
            [((LENGTH, 3 * HEAD_DIM), bf16), ((8, 3 * HEAD_DIM), f32)],
            [
                pltpu.VMEM((LENGTH, HEAD_DIM), bf16),
                pltpu.VMEM((LENGTH, HEAD_DIM), f32),
                pltpu.VMEM((LENGTH, HEAD_DIM), f32),
                pltpu.VMEM((LENGTH, HEAD_DIM), f32),
            ],
            12,
            f"attention_back_{h}",
            deps,
        )(info, random_own, random_other, *heads[3 * h : 3 * h + 3], lse, g0, g1, g2, g3)

    go_own, go_send = step(go_kernel, "go", [(WIDTH, GROUP_WIDTH)] * 2, go_keep, go_other)
    go_near = hop(go_send, 0, 1)
    gh0, s0 = head_back(0, (go_own, back_sums[0]))
    back_parts = [back_keep, back_other, back_x, back_y]
    to_x, to_y = step(
        middle_kernel,
        "middle",
        [(6, SLICE, WIDTH)] * 2,
        in_keep,
        in_other,
        *back_parts,
        deps=(gh0,),
    )
    mid_x, mid_y = hop(to_x, X_BIT, 0), hop(to_y, Y_BIT, 0)
    in_parts = [in_keep, in_other, mid_x, mid_y]
    z_level = [(2, SLICE, WIDTH)] * 2
    gh1, s1 = head_back(1, (to_x,))
    gh2, s2 = head_back(2, (gh1,))

    la_keep, la_send, lb_keep, lb_send = call(
        qkv_grad_kernel,
        [SMEM] + [VMEM] * 10,
        [((HELD + 2 * VEC_ROWS, HALF), bf16)] * 4,
        [pltpu.VMEM((WIDTH, 4 * GROUP_WIDTH), bf16)],
        16,
        "qkv_grads",
        (gh2,),
    )(info, tokens_t, gh0, gh1, gh2, go_own, go_near, vectors, s0, s1, s2)
    ra = hop(la_send, X_BIT, 0)
    rb = hop(lb_send, Y_BIT, 0)

    keep, send = call(
        token_grad_kernel,
        [VMEM] * 4,
        [((LENGTH // 2, WIDTH), bf16)] * 2,
        [pltpu.VMEM((LENGTH, 3 * GROUP_WIDTH), bf16)],
        16,
        "token_grad",
        (la_keep,),
    )(gh0, gh1, gh2, w_group)
    other = hop(send, CORE, 0)
    near_b, kept_b = step(
        back_plane_kernel, "back_plane", z_level, *back_parts, mid_x, mid_y, deps=(keep,)
    )
    near_b = hop(near_b, 0, 1)
    sums = step(in_two_kernel, "in_two", z_level, *in_parts, deps=(kept_b,))
    in_parts += hop_pair(sums, Y_BIT, X_BIT)
    near_low = step(near_kernel, "near", [(QUARTER, WIDTH)], keep, other, deps=(sums[0],))
    near = hop(near_low, 0, 1)
    far_b = step(far_kernel, "far_back", [(SLICE, WIDTH)], kept_b, near_b, deps=(near_low,))
    far_hop_b = hop(far_b, 0, 2)
    la2, lb2 = step(
        qkv_two_kernel,
        "qkv_two",
        [(TWO + 2 * VEC_ROWS, HALF), (TWO, HALF)],
        la_keep,
        ra,
        lb_keep,
        rb,
        deps=(far_b,),
    )
    ra2 = hop(la2, Y_BIT, 0)
    rb2 = hop(lb2, X_BIT, 0)
    rows_l = (TWO + VEC_ROWS, WIDTH)
    near_a, kept_a = step(in_plane_kernel, "in_plane", z_level, *in_parts, deps=(la2,))
    near_a = hop(near_a, 0, 1)
    partial = step(
        qkv_three_kernel, "qkv_three", [rows_l], la_keep, ra, ra2, lb_keep, rb, rb2, deps=(kept_a, far_hop_b)
    )
    far_a = step(far_kernel, "far_in", [(SLICE, WIDTH)], kept_a, near_a, deps=(partial, far_hop_b))
    far_hop_a = hop(far_a, 0, 2)
    sum_l = step(
        qkv_four_kernel, "qkv_four", [rows_l], partial, hop(partial, 0, 2), deps=(far_a, near)
    )
    for bit in extra_bits:
        sum_l = add_low(sum_l, hop(sum_l, bit, 0))

    own_l = sum_l[:TWO]
    x_own = hop(own_l, X_BIT, 0)
    y_own = hop(own_l, Y_BIT, 0)
    other_l = hop(sum_l, 0, 1)
    to_x, to_y = step(
        mix_l_kernel, "mix_l", [(TWO + SLICE, WIDTH)] * 2, x_own, y_own, other_l
    )
    x_other = hop(to_x, X_BIT, 0)
    y_other = hop(to_y, Y_BIT, 0)
    sum_f = step(
        last_kernel,
        "last",
        [(2, SLICE, WIDTH)],
        kept_a,
        near_a,
        far_hop_a,
        kept_b,
        near_b,
        far_hop_b,
        deps=(to_x,),
    )
    for bit in extra_bits:
        sum_f = add_low(sum_f, hop(sum_f, bit, 0))
    low_outs = step(
        tokens_kernel,
        "tokens",
        [(QUARTER, WIDTH)] * 2,
        keep,
        other,
        near,
        grad_in,
        out_here,
        deps=(sum_f,),
    )
    token_grads, layer_out = place(low_outs[0]), place(low_outs[1])
    f_x = hop(sum_f, X_BIT, 0)
    f_y = hop(sum_f, Y_BIT, 0)
    diag_f = step(diag_kernel, "diag_f", [(1, SLICE, WIDTH)] * 2, f_x, f_y, deps=(to_x,))
    f_d0, f_d1 = hop_pair(diag_f, Y_BIT, X_BIT)
    diag_l = step(
        diag_l_kernel, "diag_l", [(SLICE, WIDTH)] * 2, x_other, y_other, deps=(diag_f[0],)
    )
    d_x, d_y = hop_pair(diag_l, X_BIT, Y_BIT)
    f_all = step(join_kernel, "join_f", [(8, SLICE, WIDTH)], sum_f, f_x, f_y, f_d0, f_d1)
    plane = step(
        plane_l_kernel,
        "join_l",
        [(16 * SLICE + VEC_ROWS, WIDTH)],
        sum_l,
        other_l,
        x_own,
        y_own,
        x_other,
        y_other,
        d_x,
        d_y,
        deps=(f_all, token_grads, layer_out),
    )
    whole = pl.BlockSpec(memory_space=pltpu.VMEM)
    piece_rows = QUARTER // SLOTS * AT_ONCE
    block_rows = SLICE * AT_ONCE
    by_rows = lambda rows, cols: pl.BlockSpec((rows, cols), lambda i: (i, 0))
    square = ((WIDTH, WIDTH), f32)
    grad_w_qkv, grad_w_out, grad_w_in, grad_w_back, layer_out, grad_tokens, *vec_outs = pl.pallas_call(
        final_kernel,
        grid=(SLOTS // AT_ONCE,),
        out_shape=[
            jax.ShapeDtypeStruct(shape, dtype)
            for shape, dtype in [((WIDTH, 3 * WIDTH), f32), square, square, square, rows, rows]
            + [((WIDTH,), f32)] * 9
        ],
        in_specs=[SMEM]
        + [whole] * 4
        + [by_rows(piece_rows, WIDTH)] * 2,
        out_specs=[by_rows(block_rows, 3 * WIDTH)]
        + [by_rows(block_rows, WIDTH)] * 3
        + [by_rows(piece_rows, WIDTH)] * 2
        + [pl.BlockSpec((WIDTH,), lambda i: (0,))] * 9,
        scratch_shapes=[pltpu.VMEM((32, SLICE, WIDTH), bf16)] + [pltpu.VMEM((WIDTH, WIDTH), f32)] * 3,
        compiler_params=pltpu.CompilerParams(vmem_limit_bytes=36 * 1024 * 1024),
        cost_estimate=pl.CostEstimate(flops=1, bytes_accessed=1, transcendentals=0),
        name="final",
    )(info, plane, hop(plane, CORE, 0), f_all, hop(f_all, CORE, 0), token_grads, layer_out)
    (
        grad_shift_ffn,
        grad_gain_ffn,
        grad_bias_back,
        grad_shift_attn,
        grad_gain_attn,
        grad_bias_out,
        grad_bias_query,
        grad_bias_value,
        grad_bias_in,
    ) = vec_outs
    return (
        layer_out[None],
        grad_tokens[None],
        grad_w_qkv,
        grad_bias_query,
        grad_bias_value,
        grad_w_out,
        grad_bias_out,
        grad_gain_attn,
        grad_shift_attn,
        grad_w_in,
        grad_bias_in,
        grad_w_back,
        grad_bias_back,
        grad_gain_ffn,
        grad_shift_ffn,
    )


def solution(mesh):
    in_specs = (
        P("dp", "tp", None),
        P(),
        P(),
        P(),
        P(),
        P(),
        P(),
        P(),
        P(None, "tp"),
        P("tp"),
        P("tp", None),
        P(),
        P(),
        P(),
        P("dp", None, None, None),
        P("dp", "tp", None),
    )
    out_specs = (
        P("dp", "tp", None),
        P("dp", "tp", None),
        P(),
        P(),
        P(),
        P(),
        P(),
        P(),
        P(),
        P(None, "tp"),
        P("tp"),
        P("tp", None),
        P(),
        P(),
        P(),
    )
    return jax.shard_map(
        per_device, mesh=mesh, in_specs=in_specs, out_specs=out_specs, check_vma=False
    )
```

```python
import functools

import jax
import jax.numpy as jnp
from jax import lax
from jax.experimental import pallas as pl
from jax.experimental.pallas import tpu as pltpu
from jax.sharding import PartitionSpec as P

HEADS = 12
BLOCK = 64
HEAD_DIM = 64
TP = 4
GROUP = HEADS // TP
QUARTER = 256
LENGTH = TP * QUARTER
WIDTH = HEADS * HEAD_DIM
GROUP_WIDTH = GROUP * HEAD_DIM
SLOTS = 8
SLICE = WIDTH // SLOTS
VEC_ROWS = 16
CORE, X_BIT, Y_BIT = 1, 2, 4
PLANE_MASKS = (0, X_BIT, Y_BIT, X_BIT | Y_BIT)

epsilon = 1e-05
masked_score = -1e30
score_scale = HEAD_DIM ** (-0.5)
f32 = jnp.float32
bf16 = jnp.bfloat16


def mm(left, right):
    return jnp.dot(left, right, preferred_element_type=f32)


def mm_nt(left, right):
    return lax.dot_general(left, right, (((1,), (1,)), ((), ())), preferred_element_type=f32)


def total(*terms):
    acc = terms[0].astype(f32)
    for term in terms[1:]:
        acc = acc + term.astype(f32)
    return acc


def add_low(*terms):
    return total(*terms).astype(bf16)


def hop(array, dp_mask, z_mask):
    dp_count = lax.axis_size("dp")
    pairs = [
        (d * TP + z, (d ^ dp_mask) * TP + (z ^ z_mask)) for d in range(dp_count) for z in range(TP)
    ]
    return lax.ppermute(array, ("dp", "tp"), pairs)


def place(array):
    dp_count = lax.axis_size("dp")
    pairs = []
    for d in range(dp_count):
        for z in range(TP):
            here = d * TP + z
            away = (d ^ CORE) * TP + (z ^ 2)
            pairs.append((here, here if (d & 1) == z // 2 else away))
    return lax.ppermute(array, ("dp", "tp"), pairs)


def piece_kernel(info, w_in_hbm, w_back_ref, bias_ref, piece_ref, flip_scr, sem):
    start = pl.multiple_of(info[1] * SLICE, SLICE)
    copy = pltpu.make_async_copy(
        w_in_hbm.at[pl.ds(start, SLICE), :], piece_ref.at[pl.ds(0, SLICE), :], sem
    )
    copy.start()
    flip_scr[...] = w_back_ref[...].T
    piece_ref[SLICE : 2 * SLICE, :] = flip_scr[pl.ds(start, SLICE), :]
    bias = bias_ref[...].astype(f32).reshape(1, WIDTH)
    piece_ref[2 * SLICE :, :] = jnp.broadcast_to(bias, (VEC_ROWS, WIDTH)).astype(bf16)
    copy.wait()


def group_kernel(info, w_ref, bias_query_ref, bias_value_ref, w_out, b_out):
    bias_query = bias_query_ref[...].astype(f32).reshape(1, WIDTH)
    bias_value = bias_value_ref[...].astype(f32).reshape(1, WIDTH)
    b_out[...] = jnp.zeros_like(b_out)
    for g in range(TP):

        @pl.when(info[0] == g)
        def _(g=g):
            cols = slice(g * GROUP_WIDTH, (g + 1) * GROUP_WIDTH)
            for kind in range(3):
                lo = kind * GROUP_WIDTH
                w_out[:, lo : lo + GROUP_WIDTH] = w_ref[:, kind * WIDTH :][:, cols]
            b_out[:, :GROUP_WIDTH] = bias_query[:, cols]
            b_out[:, 2 * GROUP_WIDTH :] = bias_value[:, cols]


def block_bias(quarter, native, random_refs, head, chunk):
    shape = (LENGTH // BLOCK, QUARTER)
    row = lax.broadcasted_iota(jnp.int32, shape, 0)
    lane_block = lax.broadcasted_iota(jnp.int32, shape, 1) // BLOCK
    key_block = ((row // TP) ^ quarter) * TP + (row % TP)
    base = TP * (quarter ^ chunk)
    query_block = base + lane_block
    last = LENGTH // BLOCK - 1
    allowed = (key_block == 0) | (key_block == last)
    allowed |= (query_block == 0) | (query_block == last)
    allowed |= jnp.abs(key_block - query_block) <= 1
    for pick in range(3):
        chosen = jnp.zeros(shape, jnp.int32)
        for b in range(TP):
            at = (head * (LENGTH // BLOCK) + base + b) * 3 + pick
            value = jnp.where(native == 1, random_refs[0][at], random_refs[1][at])
            chosen = jnp.where(lane_block == b, value, chosen)
        allowed |= key_block == chosen
    return jnp.where(allowed, 0.0, masked_score).astype(f32)


def biased(scores, bias):
    blocks = LENGTH // BLOCK
    spread = scores.reshape(blocks, BLOCK, QUARTER) + bias.reshape(blocks, 1, QUARTER)
    return spread.reshape(LENGTH, QUARTER)


PACKED = QUARTER + QUARTER // 2


def pack_heads(ref, row, pieces):
    end = row + QUARTER
    ref[row:end, 0:64] = pieces[0]
    ref[row:end, 64:128] = pieces[1]
    ref[end : row + PACKED, 0:64] = pieces[2][: QUARTER // 2]
    ref[end : row + PACKED, 64:128] = pieces[2][QUARTER // 2 :]


def unpack_heads(ref, row):
    end = row + QUARTER
    third = jnp.concatenate([ref[end : row + PACKED, 0:64], ref[end : row + PACKED, 64:128]], axis=0)
    return [ref[row:end, 0:64], ref[row:end, 64:128], third]


def attention_kernel(info, rnd_own, rnd_other, t0, t1, t2, t3, w_ref, b_ref, a0, a13, a2, *rest):
    heads, lse_ref, outs = rest[:9], rest[9], rest[10]
    ones = jnp.ones((8, LENGTH), bf16)
    quarter, native = info[0], info[4]
    for slot, t_ref in enumerate((t0, t1, t2, t3)):
        rows = pl.ds(slot * QUARTER, QUARTER)
        proj = mm(t_ref[...], w_ref[...]) + b_ref[...]
        for h in range(GROUP):
            for kind in range(3):
                lo = kind * GROUP_WIDTH + h * HEAD_DIM
                piece = proj[:, lo : lo + HEAD_DIM].astype(bf16)
                if kind == 0:
                    piece = (piece.astype(f32) * score_scale).astype(bf16)
                heads[3 * h + kind][rows, :] = piece
    for h in range(GROUP):
        q_ref, k_ref, v_ref = heads[3 * h : 3 * h + 3]
        keys = k_ref[...]
        values_t = jnp.concatenate([v_ref[...].T, ones], axis=0)

        def chunk_step(chunk, carry, h=h, q_ref=q_ref, keys=keys, values_t=values_t):
            rows = pl.ds(pl.multiple_of(chunk * QUARTER, QUARTER), QUARTER)
            scores = mm_nt(keys, q_ref[rows, :])
            head = quarter * GROUP + h
            scores = biased(scores, block_bias(quarter, native, (rnd_own, rnd_other), head, chunk))
            row_max = jnp.max(scores, axis=0, keepdims=True)
            probs = jnp.exp(scores - row_max)
            out_t = mm(values_t, probs.astype(bf16))
            row_sum = out_t[HEAD_DIM : HEAD_DIM + 1]
            out_t = out_t[:HEAD_DIM] / row_sum
            outs[h, rows, :] = out_t.T.astype(bf16)
            lse_ref[pl.ds(h * TP + chunk, 1), :] = row_max + jnp.log(row_sum)
            return carry

        lax.fori_loop(0, TP, chunk_step, 0, unroll=True)
    for slot, (a_ref, row) in enumerate(((a0, 0), (a13, 0), (a2, 0), (a13, PACKED))):
        rows = slice(slot * QUARTER, (slot + 1) * QUARTER)
        pack_heads(a_ref, row, [outs[h, rows, :] for h in range(GROUP)])


def attention_back_kernel(
    h, info, rnd_own, rnd_other, q_ref, k_ref, v_ref, lse_ref, g0, g1, g2, g3, out_ref, sums_ref, do_scr, dk_scr, dv_scr, dq_scr
):
    quarter, native = info[0], info[4]
    for slot, g_ref in enumerate((g0, g1, g2, g3)):
        do_scr[slot * QUARTER : (slot + 1) * QUARTER, :] = unpack_heads(g_ref, 0)[h]
    keys = k_ref[...]
    keys_t = keys.T
    values = v_ref[...]
    dk_scr[...] = jnp.zeros_like(dk_scr)
    dv_scr[...] = jnp.zeros_like(dv_scr)

    def chunk_step(chunk, carry):
        rows = pl.ds(pl.multiple_of(chunk * QUARTER, QUARTER), QUARTER)
        queries = q_ref[rows, :]
        grad_out = do_scr[rows, :]
        scores = mm_nt(keys, queries)
        head = quarter * GROUP + h
        bias = block_bias(quarter, native, (rnd_own, rnd_other), head, chunk)
        probs = jnp.exp(biased(scores, bias - lse_ref[pl.ds(h * TP + chunk, 1), :]))
        grad_probs = mm_nt(values, grad_out)
        delta = jnp.sum(probs * grad_probs, axis=0, keepdims=True)
        grad_scores = (probs * (grad_probs - delta)).astype(bf16)
        dv_scr[...] += mm(probs.astype(bf16), grad_out)
        dk_scr[...] += mm(grad_scores, queries)
        dq_t = mm(keys_t, grad_scores) * score_scale
        dq_scr[rows, :] = dq_t.T
        return carry

    lax.fori_loop(0, TP, chunk_step, 0, unroll=True)
    for n, scr in enumerate((dq_scr, dk_scr, dv_scr)):
        out_ref[:, n * HEAD_DIM : (n + 1) * HEAD_DIM] = scr[...].astype(bf16)
    sums_ref[...] = jnp.zeros_like(sums_ref)
    sums_ref[0:1, :] = jnp.sum(out_ref[...].astype(f32), axis=0, keepdims=True)


PIECE = 2 * SLICE + VEC_ROWS
ROOT = 0.7978845608028654
CUBE = 0.044715 * ROOT


BOTH = 2 * SLICE


def held_kernel(p1, p2, p3, x1, y1, x2, y2, x3, y3, out):
    for q, (own, by_x, by_y) in enumerate(((p1, x1, y1), (p2, x2, y2), (p3, x3, y3))):
        for p, ref in enumerate((own, by_x, by_y)):
            out[(4 * q + p) * BOTH : (4 * q + p + 1) * BOTH] = ref[:BOTH]
    for q, (by_x, by_y) in enumerate(((x2, y2), (x3, y3))):
        at = (4 * q + 3) * BOTH
        out[at : at + SLICE] = by_y[BOTH:]
        out[at + SLICE : at + BOTH] = by_x[BOTH:]


def assemble_kernel(info, held, other, last_in, last_back, other_last, p1, p2, p3, w_out_ref, *outs):
    w_in_s, w_back_s, w_out_s, bias_s = outs
    quarter, mine = info[0], info[1]
    for slot in range(TP):
        start = pl.multiple_of((quarter ^ slot) * GROUP_WIDTH, GROUP_WIDTH)
        w_out_s[slot * GROUP_WIDTH : (slot + 1) * GROUP_WIDTH, :] = w_out_ref[pl.ds(start, GROUP_WIDTH), :]
    for side, main in enumerate((held, other)):
        for q in range(TP - 1):
            for p in range(4):
                start = pl.multiple_of((mine ^ PLANE_MASKS[p] ^ side) * SLICE, SLICE)
                at = (4 * q + p) * BOTH
                if q == TP - 2 and p == 3:
                    left = other_last[:SLICE] if side else last_in[...]
                    right = other_last[SLICE:] if side else last_back[...]
                else:
                    left, right = main[at : at + SLICE], main[at + SLICE : at + BOTH]
                w_in_s[q, pl.ds(start, SLICE), :] = left
                w_back_s[q, pl.ds(start, SLICE), :] = right
    for q, ref in enumerate((p1, p2, p3)):
        bias_s[q] = ref[BOTH:PIECE]


def row(ref):
    return ref[...].astype(f32).reshape(1, WIDTH)


def spread(h):
    centred = h - jnp.mean(h, axis=-1, keepdims=True)
    scale = lax.rsqrt(jnp.mean(centred * centred, axis=-1, keepdims=True) + epsilon)
    return centred * scale, scale


def spread_back(grad, gain, normal, scale):
    weighted = grad * gain
    mean_one = jnp.mean(weighted, axis=-1, keepdims=True)
    mean_two = jnp.mean(weighted * normal, axis=-1, keepdims=True)
    return scale * (weighted - mean_one - normal * mean_two)


def ffn_kernel(info, t_ref, a0, a1, a2, a3, *rest):
    bias_out_ref, gain_one_ref, shift_one_ref, bias_back_ref, gain_two_ref, shift_two_ref, bias_in_ref = rest[:7]
    w_out_s, w_in_ref, w_back_ref, w_in_s, w_back_s, bias_s = rest[7:13]
    lo_ref, first_ref, second_ref, x_ref, act_ref, gp_ref, att_ref = rest[13:]
    for slot, a_ref in enumerate((a0, a1, a2, a3)):
        for h, piece in enumerate(unpack_heads(a_ref, 0)):
            lo = slot * GROUP_WIDTH + h * HEAD_DIM
            att_ref[:, lo : lo + HEAD_DIM] = piece
    first_in = t_ref[...].astype(f32) + (mm(att_ref[...], w_out_s[...]) + row(bias_out_ref))
    first_ref[...] = first_in
    first_norm = spread(first_in)[0] * row(gain_one_ref) + row(shift_one_ref)
    x = first_norm.astype(bf16)
    x_ref[...] = x
    branch = jnp.zeros((QUARTER, WIDTH), f32)
    for q in range(TP):
        cols = slice(q * WIDTH, (q + 1) * WIDTH)
        bias_q = bias_s[q - 1, 0:1, :].astype(f32) if q else row(bias_in_ref)
        pre = mm(x, w_in_s[q - 1] if q else w_in_ref[...]) + bias_q
        square = pre * pre
        half = 0.5 + 0.5 * jnp.tanh(pre * (ROOT + CUBE * square))
        wide_act = pre * half
        act = wide_act.astype(bf16)
        act_ref[:, cols] = act
        gp_ref[:, cols] = half + wide_act * (1.0 - half) * (2.0 * ROOT + 6.0 * CUBE * square)
        branch = branch + (mm_nt(act, w_back_s[q - 1]) if q else mm(act, w_back_ref[...]))
    second_in = first_norm + branch + row(bias_back_ref)
    second_ref[...] = second_in
    lo_ref[...] = (spread(second_in)[0] * row(gain_two_ref) + row(shift_two_ref)).astype(bf16)


def norm_back_kernel(second_in_ref, cot_ref, gain_two_ref, second_ref, gb_ref, vec_ref):
    normal_two, scale_two = spread(second_in_ref[...])
    grad_out = cot_ref[...].astype(f32)
    grad_second = spread_back(grad_out, row(gain_two_ref), normal_two, scale_two)
    second_ref[...] = grad_second
    grad_branch = grad_second.astype(bf16)
    gb_ref[...] = grad_branch
    vec_ref[...] = jnp.zeros_like(vec_ref)
    vec_ref[0:1, :] = jnp.sum(grad_out, axis=0, keepdims=True)
    vec_ref[1:2, :] = jnp.sum(grad_out * normal_two, axis=0, keepdims=True)
    vec_ref[2:3, :] = jnp.sum(grad_branch.astype(f32), axis=0, keepdims=True)


def position_mask(position, order):
    mask = 0
    for n, bit in enumerate(order):
        if (position >> (2 - n)) & 1:
            mask |= bit
    return mask


FFN_ORDERS = ((CORE, X_BIT, Y_BIT), (CORE, Y_BIT, X_BIT))


def weight_grads(info, left, right, keep, send, flip_scr, lhs_scr):
    mine = info[1]
    flip_scr[...] = left[...].T
    for n, order in enumerate(FFN_ORDERS):
        for p in range(SLOTS):
            start = pl.multiple_of((mine ^ position_mask(p, order)) * SLICE, SLICE)
            lhs_scr[p * SLICE : (p + 1) * SLICE, :] = flip_scr[pl.ds(start, SLICE), :]
        for pair in range(2):
            q = 2 * n + pair
            product = mm(lhs_scr[...], right[:, q * WIDTH : (q + 1) * WIDTH]).astype(bf16)
            for p in range(SLOTS):
                out = send if p >= SLOTS // 2 else keep
                out[n, p % (SLOTS // 2), pair] = product[p * SLICE : (p + 1) * SLICE, :]


def ffn_back_kernel(info, first_ref, second_ref, gb_ref, gp_ref, gain_one_ref, vec_in, *rest):
    w_out_s, w_in_ref, w_back_ref, w_in_s, w_back_s, x_ref, att_ref = rest[:7]
    g0, g13, g2, gin_ref, vec_ref, keep, send, go_keep, go_send = rest[7:16]
    gpre_ref, flip_scr, lhs_scr = rest[16:]
    grad_branch = gb_ref[...]
    grad_first = second_ref[...]
    vec_ref[...] = vec_in[...]
    for q in range(TP):
        cols = slice(q * WIDTH, (q + 1) * WIDTH)
        grad_act = mm(grad_branch, w_back_s[q - 1]) if q else mm_nt(grad_branch, w_back_ref[...])
        grad_pre = (grad_act * gp_ref[:, cols]).astype(bf16)
        gpre_ref[:, cols] = grad_pre
        vec_ref[pl.ds(6 + (info[2] ^ q), 1), :] = jnp.sum(grad_pre.astype(f32), axis=0, keepdims=True)
        grad_first = grad_first + mm_nt(grad_pre, w_in_s[q - 1] if q else w_in_ref[...])
    normal_one, scale_one = spread(first_ref[...])
    vec_ref[3:4, :] = jnp.sum(grad_first, axis=0, keepdims=True)
    vec_ref[4:5, :] = jnp.sum(grad_first * normal_one, axis=0, keepdims=True)
    grad_in = spread_back(grad_first, row(gain_one_ref), normal_one, scale_one)
    gin_ref[...] = grad_in
    grad_mixed = grad_in.astype(bf16)
    vec_ref[5:6, :] = jnp.sum(grad_mixed.astype(f32), axis=0, keepdims=True)
    grad_att = mm_nt(grad_mixed, w_out_s[...]).astype(bf16)
    for slot, (g_ref, row_at) in enumerate(((g0, 0), (g13, 0), (g2, 0), (g13, PACKED))):
        lo = slot * GROUP_WIDTH
        pack_heads(
            g_ref, row_at, [grad_att[:, lo + h * HEAD_DIM : lo + (h + 1) * HEAD_DIM] for h in range(GROUP)]
        )
    weight_grads(info, x_ref, gpre_ref, keep, send, flip_scr, lhs_scr)
    product = mm(grad_mixed.T, att_ref[...]).astype(bf16)
    go_keep[...] = product[:, : 2 * GROUP_WIDTH]
    go_send[...] = product[:, 2 * GROUP_WIDTH :]


ORDER_LA = (4, 2, 1)
ORDER_LB = (2, 4, 1)


HALF = WIDTH // 2
HELD = SLOTS // 2 * SLICE


def flip_kernel(t0, t1, t2, t3, out_ref):
    for slot, t_ref in enumerate((t0, t1, t2, t3)):
        out_ref[:, slot * QUARTER : (slot + 1) * QUARTER] = t_ref[...].T


def qkv_grad_kernel(
    info, tokens_t, gh0, gh1, gh2, go_own, go_near, vec_ref, s0, s1, s2, la_keep, la_send, lb_keep, lb_send, out_scr
):
    quarter, here = info[0], info[3]
    for h, gh_ref in enumerate((gh0, gh1, gh2)):
        product = mm(tokens_t[...], gh_ref[...]).astype(bf16)
        for kind in range(3):
            lo = kind * GROUP_WIDTH + h * HEAD_DIM
            out_scr[:, lo : lo + HEAD_DIM] = product[:, kind * HEAD_DIM : (kind + 1) * HEAD_DIM]
    add_to(out_scr.at[:, 3 * GROUP_WIDTH :], go_own[...], go_near[...])
    for keep, send, order, lo in (
        (la_keep, la_send, ORDER_LA, 0),
        (lb_keep, lb_send, ORDER_LB, HALF),
    ):
        for p in range(SLOTS):
            start = pl.multiple_of((here ^ position_mask(p, order)) * SLICE, SLICE)
            out = send if p >= SLOTS // 2 else keep
            row = p % (SLOTS // 2) * SLICE
            out[row : row + SLICE, :] = out_scr[pl.ds(start, SLICE), lo : lo + HALF]
    placed = []
    for kind in (0, 2):
        cols = slice(kind * HEAD_DIM, (kind + 1) * HEAD_DIM)
        piece = jnp.concatenate([sums[0:1, cols] for sums in (s0, s1, s2)], axis=1)
        placed.append(
            jnp.concatenate([jnp.where(quarter == g, piece, 0.0) for g in range(TP)], axis=1)
        )
    vectors = jnp.concatenate([vec_ref[0:10, :]] + placed + [vec_ref[12:VEC_ROWS, :]], axis=0)
    vectors = vectors.astype(bf16)
    for out in (la_keep, la_send, lb_keep, lb_send):
        out[HELD : HELD + VEC_ROWS, :] = vectors[:, :HALF]
        out[HELD + VEC_ROWS :, :] = vectors[:, HALF:]


def token_grad_kernel(gh0, gh1, gh2, w_ref, keep_ref, send_ref, all_scr):
    for h, gh_ref in enumerate((gh0, gh1, gh2)):
        for kind in range(3):
            lo = kind * GROUP_WIDTH + h * HEAD_DIM
            all_scr[:, lo : lo + HEAD_DIM] = gh_ref[:, kind * HEAD_DIM : (kind + 1) * HEAD_DIM]
    half = LENGTH // 2
    send_ref[...] = mm_nt(all_scr[half:, :], w_ref[...]).astype(bf16)
    keep_ref[...] = mm_nt(all_scr[:half, :], w_ref[...]).astype(bf16)


FFN_AT = 16 * SLICE + VEC_ROWS
AT_ONCE = 2


def final_kernel(info, c_ref, c_other, low_tokens, low_out, *rest):
    qkv_out, out_out, w_in_out, w_back_out, layer_out, token_out = rest[:6]
    vec_outs, (flip_scr, out_scr, back_scr) = rest[6:15], rest[15:]
    quarter, mine, z_here, here = info[0], info[1], info[2], info[3]
    step_now = pl.program_id(0)
    vec_rows = slice(16 * SLICE, FFN_AT)

    def blocks_of(core):
        def piece(group, at, cols):
            ref = c_ref if (group >> 1) == core else c_other
            group_off, block_off = quarter ^ group, here ^ at
            xy = ((block_off >> 2) & 1) + (block_off & 2)
            nth = xy * 4 + (group_off & 1) + 2 * (block_off & 1)
            return ref[pl.ds(pl.multiple_of(nth * SLICE, SLICE), SLICE), cols]

        def ffn_piece(at, odd, part):
            ref = c_ref if odd == core else c_other
            mask = mine ^ at
            nth = (((mask >> 1) & 1) + ((mask >> 2) & 1) * 2) * 2 + part
            return ref[pl.ds(pl.multiple_of(FFN_AT + nth * SLICE, VEC_ROWS), SLICE), :].astype(f32)

        @pl.when(step_now == 0)
        def _():
            cols = slice(3 * GROUP_WIDTH, 4 * GROUP_WIDTH)
            for at in range(SLOTS):
                rows = slice(at * SLICE, (at + 1) * SLICE)
                last = [piece(group, at, cols) for group in range(TP)]
                flip_scr[rows, :] = jnp.concatenate(last, axis=1).astype(f32)
                back_scr[rows, :] = ffn_piece(at, at & 1, 1)
            out_scr[...] = flip_scr[...].T
            flip_scr[...] = back_scr[...].T

        for n in range(AT_ONCE):
            at = step_now * AT_ONCE + n
            rows = slice(n * SLICE, (n + 1) * SLICE)
            for kind in range(3):
                cols = slice(kind * GROUP_WIDTH, (kind + 1) * GROUP_WIDTH)
                joined = jnp.concatenate([piece(group, at, cols) for group in range(TP)], axis=1)
                qkv_out[rows, kind * WIDTH : (kind + 1) * WIDTH] = joined.astype(f32)
            w_in_out[rows, :] = ffn_piece(at, n & 1, 0)

    for core in range(2):
        pl.when((mine & 1) == core)(functools.partial(blocks_of, core))

    @pl.when(step_now == 0)
    def _():
        vectors = total(c_ref[vec_rows, :], c_other[vec_rows, :])
        bias_in = jnp.zeros((1, WIDTH), f32)
        for q in range(TP):
            bias_in = jnp.where(z_here == q, vectors[6 + q : 7 + q, :], bias_in)
        for out, n in zip(vec_outs[:8], (0, 1, 2, 3, 4, 5, 10, 11)):
            out[...] = vectors[n]
        vec_outs[8][...] = bias_in[0]

    rows = pl.ds(pl.multiple_of(step_now * AT_ONCE * SLICE, SLICE), AT_ONCE * SLICE)
    out_out[...] = out_scr[rows, :]
    w_back_out[...] = flip_scr[rows, :]
    layer_out[...] = low_out[...]
    token_out[...] = low_tokens[...]


def add_to(out, *terms):
    out[...] = add_low(*terms)


def join_kernel(*refs):
    out, at = refs[-1], 0
    for ref in refs[:-1]:
        out[at : at + ref.shape[0]] = ref[...]
        at += ref.shape[0]


def diag_kernel(by_x, by_y, first, second):
    half = first.shape[0]
    first[...] = by_x[:half]
    second[...] = by_y[half:]


def trim_kernel(piece, out):
    out[...] = piece[:BOTH]


def mix_kernel(by_x, by_y, own, to_x, to_y):
    to_x[:BOTH] = own[:BOTH]
    to_x[BOTH:] = by_y[SLICE:BOTH]
    to_y[:BOTH] = own[:BOTH]
    to_y[BOTH:] = by_x[:SLICE]


def last_mix_kernel(by_x, by_y, to_x, to_y):
    to_x[...] = by_y[SLICE:BOTH]
    to_y[...] = by_x[:SLICE]


def level_one_kernel(keep, other, first, second):
    add_to(first, keep[0, 2:], other[0, 2:])
    add_to(second, keep[1, 2:], other[1, 2:])


def middle_kernel(in_keep, in_other, back_keep, back_other, back_x, back_y, to_x, to_y):
    for n in range(2):
        out = to_y if n else to_x
        for p in range(2):
            for pair in range(2):
                add_to(out.at[2 * p + pair], in_keep[n, 2 + p, pair], in_other[n, 2 + p, pair])
    for pair in range(2):
        add_to(to_y.at[4 + pair], back_keep[0, 1, pair], back_other[0, 1, pair], back_x[1, pair])
        add_to(to_x.at[4 + pair], back_keep[1, 1, pair], back_other[1, 1, pair], back_y[1, pair])


def in_two_kernel(keep, other, by_x, by_y, first, second):
    for pair in range(2):
        add_to(first.at[pair], keep[0, 1, pair], other[0, 1, pair], by_x[2 + pair])
        add_to(second.at[pair], keep[1, 1, pair], other[1, 1, pair], by_y[2 + pair])


def in_plane_kernel(keep, other, by_x, by_y, by_xy, by_yx, near, kept):
    for q in range(TP):
        order, pair = q // 2, q % 2
        first, second = (by_x, by_xy) if order == 0 else (by_y, by_yx)
        out = near if q % 2 else kept
        add_to(out.at[q // 2], keep[order, 0, pair], other[order, 0, pair], first[pair], second[pair])


def back_plane_kernel(keep, other, by_x, by_y, mid_x, mid_y, near, kept):
    for q in range(TP):
        order, pair = q // 2, q % 2
        first, second = (by_x, mid_y) if order == 0 else (by_y, mid_x)
        out = near if q % 2 else kept
        add_to(out.at[q // 2], keep[order, 0, pair], other[order, 0, pair], first[0, pair], second[4 + pair])


def far_kernel(kept, near, far):
    add_to(far, kept[1], near[1])


def last_kernel(kept_a, near_a, far_a, kept_b, near_b, far_b, out):
    add_to(out.at[0], kept_a[0], near_a[0], far_a[...])
    add_to(out.at[1], kept_b[0], near_b[0], far_b[...])


def go_kernel(keep, other, own, send):
    add_to(own, keep[:, :GROUP_WIDTH], other[:, :GROUP_WIDTH])
    add_to(send, keep[:, GROUP_WIDTH:], other[:, GROUP_WIDTH:])


def near_kernel(keep, other, out):
    add_to(out, keep[QUARTER:], other[QUARTER:])


def tokens_kernel(keep, other, near, grad_in, out_here, tokens, again):
    add_to(tokens, keep[:QUARTER], other[:QUARTER], near[...], grad_in[...])
    again[...] = out_here[...]


TWO = 2 * SLICE


def qkv_two_kernel(la, ra, lb, rb, la_out, lb_out):
    add_to(la_out, la[TWO:], ra[TWO:])
    add_to(lb_out, lb[TWO:HELD], rb[TWO:HELD])


def qkv_three_kernel(la, ra, ra2, lb, rb, rb2, out):
    add_to(out.at[:TWO, :HALF], la[:TWO], ra[:TWO], ra2[:TWO])
    add_to(out.at[:TWO, HALF:], lb[:TWO], rb[:TWO], rb2[...])
    for n in range(2):
        rows = slice(HELD + n * VEC_ROWS, HELD + (n + 1) * VEC_ROWS)
        rows_two = slice(TWO + n * VEC_ROWS, TWO + (n + 1) * VEC_ROWS)
        add_to(out.at[TWO:, n * HALF : (n + 1) * HALF], la[rows], ra[rows], ra2[rows_two])


def qkv_four_kernel(own, other, out):
    add_to(out.at[:SLICE], own[:SLICE], other[SLICE:TWO])
    add_to(out.at[SLICE:TWO], own[SLICE:TWO], other[:SLICE])
    add_to(out.at[TWO:], own[TWO:], other[TWO:])


def mix_l_kernel(by_x, by_y, other, to_x, to_y):
    to_x[:TWO] = other[:TWO]
    to_x[TWO:] = by_y[SLICE:TWO]
    to_y[:TWO] = other[:TWO]
    to_y[TWO:] = by_x[:SLICE]


def diag_kernel(l_x, l_y, f_x, f_y, to_x, to_y):
    to_x[:SLICE] = l_y[SLICE:TWO]
    to_x[SLICE:] = f_y[1]
    to_y[:SLICE] = l_x[:SLICE]
    to_y[SLICE:] = f_x[0]


def plane_l_kernel(own, other, x_own, y_own, x_other, y_other, f_own, f_x, f_y, d_x, d_y, out):
    diag_own = (y_other[TWO:], x_other[TWO:])
    diag_other = (d_y[:SLICE], d_x[:SLICE])
    places = (
        ((own[:SLICE], own[SLICE:TWO]), (other[:SLICE], other[SLICE:TWO])),
        ((x_own[:SLICE], x_own[SLICE:TWO]), (x_other[:SLICE], x_other[SLICE:TWO])),
        ((y_own[:SLICE], y_own[SLICE:TWO]), (y_other[:SLICE], y_other[SLICE:TWO])),
        (diag_own, diag_other),
    )
    for p, (here, there) in enumerate(places):
        for slot in range(TP):
            at = (p * TP + slot) * SLICE
            out[at : at + SLICE] = (there if slot % 2 else here)[slot // 2]
    add_to(out.at[16 * SLICE : FFN_AT], own[TWO:], other[TWO:])
    for n, (left, right) in enumerate(
        ((f_own[0], f_own[1]), (f_x[0], f_x[1]), (f_y[0], f_y[1]), (d_y[SLICE:], d_x[SLICE:]))
    ):
        out[FFN_AT + 2 * n * SLICE : FFN_AT + (2 * n + 1) * SLICE] = left
        out[FFN_AT + (2 * n + 1) * SLICE : FFN_AT + (2 * n + 2) * SLICE] = right


VMEM = pl.BlockSpec(memory_space=pltpu.VMEM)
SMEM = pl.BlockSpec(memory_space=pltpu.SMEM)
HBM = pl.BlockSpec(memory_space=pl.ANY)


def call(kernel, in_specs, outs, scratch, vmem_mib, name, deps=()):
    count, extra = len(in_specs), len(deps)

    def body(*refs):
        kernel(*refs[:count], *refs[count + extra :])

    run = pl.pallas_call(
        body,
        out_shape=[jax.ShapeDtypeStruct(shape, dtype) for shape, dtype in outs],
        in_specs=list(in_specs) + [HBM] * extra,
        out_specs=[VMEM] * len(outs),
        scratch_shapes=scratch,
        compiler_params=pltpu.CompilerParams(vmem_limit_bytes=vmem_mib * 1024 * 1024),
        cost_estimate=pl.CostEstimate(flops=1, bytes_accessed=1, transcendentals=0),
        name=name,
    )
    return lambda *arrays: run(*arrays, *deps)


def step(kernel, name, outs, *arrays, deps=()):
    shapes = [(shape, bf16) for shape in outs]
    result = call(kernel, [VMEM] * len(arrays), shapes, [], 12, name, deps)(*arrays)
    return result[0] if len(outs) == 1 else result


def per_device(
    tokens,
    w_qkv,
    bias_query,
    bias_value,
    w_out,
    bias_out,
    gain_attn,
    shift_attn,
    w_in,
    bias_in,
    w_back,
    bias_back,
    gain_ffn,
    shift_ffn,
    random_blocks,
    cotangent,
):
    dp_count = lax.axis_size("dp")
    d = lax.axis_index("dp")
    z = lax.axis_index("tp")
    core = d & 1
    quarter = (z & 1) + 2 * core
    mine = d & (SLOTS - 1)
    here = ((d >> 1) & 1) * 4 + ((d >> 2) & 1) * 2 + (z >> 1)
    native = (core == z // 2).astype(jnp.int32)
    info = jnp.stack([quarter, mine, z, here, native]).astype(jnp.int32)
    extra_bits = [1 << b for b in range(3, dp_count.bit_length() - 1)]

    own_tokens = place(tokens[0])
    piece = call(
        piece_kernel,
        [SMEM, HBM, VMEM, VMEM],
        [((2 * SLICE + VEC_ROWS, WIDTH), bf16)],
        [pltpu.VMEM((WIDTH, WIDTH), bf16), pltpu.SemaphoreType.DMA],
        8,
        "piece",
    )(info, w_in, w_back, bias_in)[0]
    piece_one = hop(piece, 0, 1)
    again = step(join_kernel, "again", [(PIECE, WIDTH)], piece, deps=(own_tokens,))
    piece_two = hop(again, 0, 2)
    random_own = random_blocks.reshape(-1)
    random_other = hop(random_own, CORE, 0)
    w_group, bias_group = call(
        group_kernel,
        [SMEM, VMEM, VMEM, VMEM],
        [((WIDTH, 3 * GROUP_WIDTH), bf16), ((1, 3 * GROUP_WIDTH), f32)],
        [],
        16,
        "group",
    )(info, w_qkv, bias_query, bias_value)
    near_tokens = hop(own_tokens, 0, 1)
    core_tokens = hop(own_tokens, CORE, 0)
    far_tokens = hop(near_tokens, CORE, 0)
    trimmed = step(trim_kernel, "trim", [(BOTH, WIDTH)], piece_one, deps=(w_group, random_other))
    x_one = hop(trimmed, X_BIT, 0)
    y_one = hop(trimmed, Y_BIT, 0)
    piece_three = hop(piece_two, 0, 1)
    cot = place(cotangent[0])
    mixed = [(BOTH + SLICE, WIDTH)] * 2
    to_x, to_y = step(mix_kernel, "mix_two", mixed, x_one, y_one, piece_two, deps=(near_tokens,))
    x_two = hop(to_x, X_BIT, 0)
    y_two = hop(to_y, Y_BIT, 0)

    packed = ((PACKED, 2 * HEAD_DIM), bf16)
    double = ((2 * PACKED, 2 * HEAD_DIM), bf16)
    per_head = ((LENGTH, HEAD_DIM), bf16)
    token_slots = (own_tokens, near_tokens, core_tokens, far_tokens)
    a0, a13, a2, *heads = call(
        attention_kernel,
        [SMEM] * 3 + [VMEM] * 6,
        [packed, double, packed] + [per_head] * 9 + [((16, QUARTER), f32)],
        [pltpu.VMEM((GROUP, LENGTH, HEAD_DIM), bf16)],
        24,
        "attention",
        (to_x,),
    )(info, random_own, random_other, *token_slots, w_group, bias_group)
    heads, lse = heads[:9], heads[9]
    a1 = hop(a13, 0, 1)
    a2 = hop(a2, CORE, 0)
    a3 = hop(a1[PACKED:], CORE, 0)
    to_x, to_y = step(mix_kernel, "mix_three", mixed, x_two, y_two, piece_three, deps=(a0,))
    x_three = hop(to_x, X_BIT, 0)
    y_three = hop(to_y, Y_BIT, 0)
    tokens_t = call(flip_kernel, [VMEM] * 4, [((WIDTH, LENGTH), bf16)], [], 8, "flip_tokens", (a1, to_x))(
        *token_slots
    )[0]
    to_x, to_y = step(
        last_mix_kernel, "mix_last", [(SLICE, WIDTH)] * 2, x_three, y_three, deps=(tokens_t,)
    )
    last_back = hop(to_x, X_BIT, 0)
    last_in = hop(to_y, Y_BIT, 0)
    pieces = (piece_one, piece_two, piece_three)
    held = step(
        held_kernel,
        "held",
        [(11 * BOTH, WIDTH)],
        *pieces,
        x_one,
        y_one,
        x_two,
        y_two,
        x_three,
        y_three,
        deps=(to_x,),
    )
    last = step(join_kernel, "last_piece", [(BOTH, WIDTH)], last_in, last_back, deps=(held,))
    quarters = ((TP - 1, WIDTH, WIDTH), bf16)
    w_in_s, w_back_s, w_out_s, bias_s = call(
        assemble_kernel,
        [SMEM] + [VMEM] * 9,
        [quarters, quarters, ((WIDTH, WIDTH), bf16), ((TP - 1, VEC_ROWS, WIDTH), bf16)],
        [],
        12,
        "assemble",
    )(info, held, hop(held, CORE, 0), last_in, last_back, hop(last, CORE, 0), *pieces, w_out)

    rows = ((QUARTER, WIDTH), bf16)
    wide = ((QUARTER, TP * WIDTH), bf16)
    rows_f32 = ((QUARTER, WIDTH), f32)
    vec_rows = ((VEC_ROWS, WIDTH), f32)
    out_here, first_in, second_in, ffn_input, activated, gelu_slope, attended = call(
        ffn_kernel,
        [SMEM] + [VMEM] * 18,
        [rows, rows_f32, rows_f32, rows, wide, ((QUARTER, TP * WIDTH), f32), rows],
        [],
        14,
        "ffn",
        (tokens_t,),
    )(
        info,
        own_tokens,
        a0,
        a1,
        a2,
        a3,
        bias_out,
        gain_attn,
        shift_attn,
        bias_back,
        gain_ffn,
        shift_ffn,
        bias_in,
        w_out_s,
        w_in,
        w_back,
        w_in_s,
        w_back_s,
        bias_s,
    )
    grad_second, grad_branch, vectors = call(
        norm_back_kernel, [VMEM] * 3, [rows_f32, rows, vec_rows], [], 10, "norm_back"
    )(second_in, cot, gain_ffn)
    pairs = ((2, SLOTS // 2, 2, SLICE, WIDTH), bf16)
    halves = ((WIDTH, 2 * GROUP_WIDTH), bf16)
    flips = [pltpu.VMEM((WIDTH, QUARTER), bf16), pltpu.VMEM((WIDTH, QUARTER), bf16)]
    back_keep, back_send = call(
        weight_grads, [SMEM] + [VMEM] * 2, [pairs] * 2, flips, 8, "back_grads"
    )(info, grad_branch, activated)
    back_other = hop(back_send, CORE, 0)

    g0, g13, g2, grad_in, vectors, in_keep, in_send, go_keep, go_send = call(
        ffn_back_kernel,
        [SMEM] + [VMEM] * 13,
        [packed, double, packed, rows_f32, vec_rows] + [pairs] * 2 + [halves] * 2,
        [pltpu.VMEM((QUARTER, TP * WIDTH), bf16)] + flips,
        12,
        "ffn_back",
        (back_keep,),
    )(
        info,
        first_in,
        grad_second,
        grad_branch,
        gelu_slope,
        gain_attn,
        vectors,
        w_out_s,
        w_in,
        w_back,
        w_in_s,
        w_back_s,
        ffn_input,
        attended,
    )
    g1 = hop(g13, 0, 1)
    g2 = hop(g2, CORE, 0)
    g3 = hop(g1[PACKED:], CORE, 0)

    first_level = [(2, 2, SLICE, WIDTH)] * 2
    def hop_pair(pair, first, second):
        return hop(pair[0], first, 0), hop(pair[1], second, 0)

    back_sums = step(level_one_kernel, "back_one", first_level, back_keep, back_other, deps=(g13,))
    back_x, back_y = hop_pair(back_sums, X_BIT, Y_BIT)
    in_other = hop(in_send, CORE, 0)
    go_other = hop(go_send, CORE, 0)

    def head_back(h, deps):
        return call(
            functools.partial(attention_back_kernel, h),
            [SMEM] * 3 + [VMEM] * 8,
            [((LENGTH, 3 * HEAD_DIM), bf16), ((8, 3 * HEAD_DIM), f32)],
            [
                pltpu.VMEM((LENGTH, HEAD_DIM), bf16),
                pltpu.VMEM((LENGTH, HEAD_DIM), f32),
                pltpu.VMEM((LENGTH, HEAD_DIM), f32),
                pltpu.VMEM((LENGTH, HEAD_DIM), f32),
            ],
            12,
            f"attention_back_{h}",
            deps,
        )(info, random_own, random_other, *heads[3 * h : 3 * h + 3], lse, g0, g1, g2, g3)

    go_own, go_send = step(go_kernel, "go", [(WIDTH, GROUP_WIDTH)] * 2, go_keep, go_other)
    go_near = hop(go_send, 0, 1)
    gh0, s0 = head_back(0, (go_own, back_sums[0]))
    back_parts = [back_keep, back_other, back_x, back_y]
    to_x, to_y = step(
        middle_kernel,
        "middle",
        [(6, SLICE, WIDTH)] * 2,
        in_keep,
        in_other,
        *back_parts,
        deps=(gh0,),
    )
    mid_x, mid_y = hop(to_x, X_BIT, 0), hop(to_y, Y_BIT, 0)
    in_parts = [in_keep, in_other, mid_x, mid_y]
    z_level = [(2, SLICE, WIDTH)] * 2
    gh1, s1 = head_back(1, (to_x,))
    gh2, s2 = head_back(2, (gh1,))

    la_keep, la_send, lb_keep, lb_send = call(
        qkv_grad_kernel,
        [SMEM] + [VMEM] * 10,
        [((HELD + 2 * VEC_ROWS, HALF), bf16)] * 4,
        [pltpu.VMEM((WIDTH, 4 * GROUP_WIDTH), bf16)],
        16,
        "qkv_grads",
        (gh2,),
    )(info, tokens_t, gh0, gh1, gh2, go_own, go_near, vectors, s0, s1, s2)
    ra = hop(la_send, X_BIT, 0)
    rb = hop(lb_send, Y_BIT, 0)

    keep, send = call(
        token_grad_kernel,
        [VMEM] * 4,
        [((LENGTH // 2, WIDTH), bf16)] * 2,
        [pltpu.VMEM((LENGTH, 3 * GROUP_WIDTH), bf16)],
        16,
        "token_grad",
        (la_keep,),
    )(gh0, gh1, gh2, w_group)
    other = hop(send, CORE, 0)
    near_b, kept_b = step(
        back_plane_kernel, "back_plane", z_level, *back_parts, mid_x, mid_y, deps=(keep,)
    )
    near_b = hop(near_b, 0, 1)
    sums = step(in_two_kernel, "in_two", z_level, *in_parts, deps=(kept_b,))
    in_parts += hop_pair(sums, Y_BIT, X_BIT)
    near_low = step(near_kernel, "near", [(QUARTER, WIDTH)], keep, other, deps=(sums[0],))
    near = hop(near_low, 0, 1)
    far_b = step(far_kernel, "far_back", [(SLICE, WIDTH)], kept_b, near_b, deps=(near_low,))
    far_hop_b = hop(far_b, 0, 2)
    la2, lb2 = step(
        qkv_two_kernel,
        "qkv_two",
        [(TWO + 2 * VEC_ROWS, HALF), (TWO, HALF)],
        la_keep,
        ra,
        lb_keep,
        rb,
        deps=(far_b,),
    )
    ra2 = hop(la2, Y_BIT, 0)
    rb2 = hop(lb2, X_BIT, 0)
    rows_l = (TWO + VEC_ROWS, WIDTH)
    near_a, kept_a = step(in_plane_kernel, "in_plane", z_level, *in_parts, deps=(la2,))
    near_a = hop(near_a, 0, 1)
    partial = step(
        qkv_three_kernel, "qkv_three", [rows_l], la_keep, ra, ra2, lb_keep, rb, rb2, deps=(kept_a, far_hop_b)
    )
    far_a = step(far_kernel, "far_in", [(SLICE, WIDTH)], kept_a, near_a, deps=(partial, far_hop_b))
    far_hop_a = hop(far_a, 0, 2)
    sum_l = step(
        qkv_four_kernel, "qkv_four", [rows_l], partial, hop(partial, 0, 2), deps=(far_a, near)
    )
    for bit in extra_bits:
        sum_l = add_low(sum_l, hop(sum_l, bit, 0))

    own_l = sum_l[:TWO]
    x_own = hop(own_l, X_BIT, 0)
    y_own = hop(own_l, Y_BIT, 0)
    other_l = hop(sum_l, 0, 1)
    to_x, to_y = step(
        mix_l_kernel, "mix_l", [(TWO + SLICE, WIDTH)] * 2, x_own, y_own, other_l
    )
    x_other = hop(to_x, X_BIT, 0)
    y_other = hop(to_y, Y_BIT, 0)
    sum_f = step(
        last_kernel,
        "last",
        [(2, SLICE, WIDTH)],
        kept_a,
        near_a,
        far_hop_a,
        kept_b,
        near_b,
        far_hop_b,
        deps=(to_x,),
    )
    for bit in extra_bits:
        sum_f = add_low(sum_f, hop(sum_f, bit, 0))
    low_outs = step(
        tokens_kernel,
        "tokens",
        [(QUARTER, WIDTH)] * 2,
        keep,
        other,
        near,
        grad_in,
        out_here,
        deps=(sum_f,),
    )
    token_grads, layer_out = place(low_outs[0]), place(low_outs[1])
    f_x = hop(sum_f, X_BIT, 0)
    f_y = hop(sum_f, Y_BIT, 0)
    diag = step(diag_kernel, "diag", [(TWO, WIDTH)] * 2, x_other, y_other, f_x, f_y)
    d_x, d_y = hop_pair(diag, X_BIT, Y_BIT)
    plane = step(
        plane_l_kernel,
        "plane",
        [(FFN_AT + SLOTS * SLICE, WIDTH)],
        sum_l,
        other_l,
        x_own,
        y_own,
        x_other,
        y_other,
        sum_f,
        f_x,
        f_y,
        d_x,
        d_y,
        deps=(token_grads, layer_out),
    )
    whole = pl.BlockSpec(memory_space=pltpu.VMEM)
    piece_rows = QUARTER // SLOTS * AT_ONCE
    block_rows = SLICE * AT_ONCE
    by_rows = lambda rows, cols: pl.BlockSpec((rows, cols), lambda i: (i, 0))
    square = ((WIDTH, WIDTH), f32)
    grad_w_qkv, grad_w_out, grad_w_in, grad_w_back, layer_out, grad_tokens, *vec_outs = pl.pallas_call(
        final_kernel,
        grid=(SLOTS // AT_ONCE,),
        out_shape=[
            jax.ShapeDtypeStruct(shape, dtype)
            for shape, dtype in [((WIDTH, 3 * WIDTH), f32), square, square, square, rows, rows]
            + [((WIDTH,), f32)] * 9
        ],
        in_specs=[SMEM]
        + [whole] * 2
        + [by_rows(piece_rows, WIDTH)] * 2,
        out_specs=[by_rows(block_rows, 3 * WIDTH)]
        + [by_rows(block_rows, WIDTH)] * 3
        + [by_rows(piece_rows, WIDTH)] * 2
        + [pl.BlockSpec((WIDTH,), lambda i: (0,))] * 9,
        scratch_shapes=[pltpu.VMEM((WIDTH, WIDTH), f32)] * 3,
        compiler_params=pltpu.CompilerParams(vmem_limit_bytes=36 * 1024 * 1024),
        cost_estimate=pl.CostEstimate(flops=1, bytes_accessed=1, transcendentals=0),
        name="final",
    )(info, plane, hop(plane, CORE, 0), token_grads, layer_out)
    (
        grad_shift_ffn,
        grad_gain_ffn,
        grad_bias_back,
        grad_shift_attn,
        grad_gain_attn,
        grad_bias_out,
        grad_bias_query,
        grad_bias_value,
        grad_bias_in,
    ) = vec_outs
    return (
        layer_out[None],
        grad_tokens[None],
        grad_w_qkv,
        grad_bias_query,
        grad_bias_value,
        grad_w_out,
        grad_bias_out,
        grad_gain_attn,
        grad_shift_attn,
        grad_w_in,
        grad_bias_in,
        grad_w_back,
        grad_bias_back,
        grad_gain_ffn,
        grad_shift_ffn,
    )


def solution(mesh):
    in_specs = (
        P("dp", "tp", None),
        P(),
        P(),
        P(),
        P(),
        P(),
        P(),
        P(),
        P(None, "tp"),
        P("tp"),
        P("tp", None),
        P(),
        P(),
        P(),
        P("dp", None, None, None),
        P("dp", "tp", None),
    )
    out_specs = (
        P("dp", "tp", None),
        P("dp", "tp", None),
        P(),
        P(),
        P(),
        P(),
        P(),
        P(),
        P(),
        P(None, "tp"),
        P("tp"),
        P("tp", None),
        P(),
        P(),
        P(),
    )
    return jax.shard_map(
        per_device, mesh=mesh, in_specs=in_specs, out_specs=out_specs, check_vma=False
    )
```

```python
import functools

import jax
import jax.numpy as jnp
from jax import lax
from jax.experimental import pallas as pl
from jax.experimental.pallas import tpu as pltpu
from jax.sharding import PartitionSpec as P

HEADS = 12
BLOCK = 64
HEAD_DIM = 64
TP = 4
GROUP = HEADS // TP
QUARTER = 256
LENGTH = TP * QUARTER
WIDTH = HEADS * HEAD_DIM
GROUP_WIDTH = GROUP * HEAD_DIM
SLOTS = 8
SLICE = WIDTH // SLOTS
VEC_ROWS = 16
CORE, X_BIT, Y_BIT = 1, 2, 4
PLANE_MASKS = (0, X_BIT, Y_BIT, X_BIT | Y_BIT)

epsilon = 1e-05
masked_score = -1e30
score_scale = HEAD_DIM ** (-0.5)
f32 = jnp.float32
bf16 = jnp.bfloat16


def mm(left, right):
    return jnp.dot(left, right, preferred_element_type=f32)


def mm_nt(left, right):
    return lax.dot_general(left, right, (((1,), (1,)), ((), ())), preferred_element_type=f32)


def total(*terms):
    acc = terms[0].astype(f32)
    for term in terms[1:]:
        acc = acc + term.astype(f32)
    return acc


def add_low(*terms):
    return total(*terms).astype(bf16)


def hop(array, dp_mask, z_mask):
    dp_count = lax.axis_size("dp")
    pairs = [
        (d * TP + z, (d ^ dp_mask) * TP + (z ^ z_mask)) for d in range(dp_count) for z in range(TP)
    ]
    return lax.ppermute(array, ("dp", "tp"), pairs)


def place(array):
    dp_count = lax.axis_size("dp")
    pairs = []
    for d in range(dp_count):
        for z in range(TP):
            here = d * TP + z
            away = (d ^ CORE) * TP + (z ^ 2)
            pairs.append((here, here if (d & 1) == z // 2 else away))
    return lax.ppermute(array, ("dp", "tp"), pairs)


def piece_kernel(info, w_in_hbm, w_back_ref, bias_ref, piece_ref, flip_scr, sem):
    start = pl.multiple_of(info[1] * SLICE, SLICE)
    copy = pltpu.make_async_copy(
        w_in_hbm.at[pl.ds(start, SLICE), :], piece_ref.at[pl.ds(0, SLICE), :], sem
    )
    copy.start()
    flip_scr[...] = w_back_ref[...].T
    piece_ref[SLICE : 2 * SLICE, :] = flip_scr[pl.ds(start, SLICE), :]
    bias = bias_ref[...].astype(f32).reshape(1, WIDTH)
    piece_ref[2 * SLICE :, :] = jnp.broadcast_to(bias, (VEC_ROWS, WIDTH)).astype(bf16)
    copy.wait()


def group_kernel(info, w_ref, bias_query_ref, bias_value_ref, w_out, b_out):
    bias_query = bias_query_ref[...].astype(f32).reshape(1, WIDTH)
    bias_value = bias_value_ref[...].astype(f32).reshape(1, WIDTH)
    b_out[...] = jnp.zeros_like(b_out)
    for g in range(TP):

        @pl.when(info[0] == g)
        def _(g=g):
            cols = slice(g * GROUP_WIDTH, (g + 1) * GROUP_WIDTH)
            for kind in range(3):
                lo = kind * GROUP_WIDTH
                w_out[:, lo : lo + GROUP_WIDTH] = w_ref[:, kind * WIDTH :][:, cols]
            b_out[:, :GROUP_WIDTH] = bias_query[:, cols]
            b_out[:, 2 * GROUP_WIDTH :] = bias_value[:, cols]


def block_bias(quarter, native, random_refs, head, chunk):
    shape = (LENGTH // BLOCK, QUARTER)
    row = lax.broadcasted_iota(jnp.int32, shape, 0)
    lane_block = lax.broadcasted_iota(jnp.int32, shape, 1) // BLOCK
    key_block = ((row // TP) ^ quarter) * TP + (row % TP)
    base = TP * (quarter ^ chunk)
    query_block = base + lane_block
    last = LENGTH // BLOCK - 1
    allowed = (key_block == 0) | (key_block == last)
    allowed |= (query_block == 0) | (query_block == last)
    allowed |= jnp.abs(key_block - query_block) <= 1
    for pick in range(3):
        chosen = jnp.zeros(shape, jnp.int32)
        for b in range(TP):
            at = (head * (LENGTH // BLOCK) + base + b) * 3 + pick
            value = jnp.where(native == 1, random_refs[0][at], random_refs[1][at])
            chosen = jnp.where(lane_block == b, value, chosen)
        allowed |= key_block == chosen
    return jnp.where(allowed, 0.0, masked_score).astype(f32)


def biased(scores, bias):
    blocks = LENGTH // BLOCK
    spread = scores.reshape(blocks, BLOCK, QUARTER) + bias.reshape(blocks, 1, QUARTER)
    return spread.reshape(LENGTH, QUARTER)


PACKED = QUARTER + QUARTER // 2


def pack_heads(ref, row, pieces):
    end = row + QUARTER
    ref[row:end, 0:64] = pieces[0]
    ref[row:end, 64:128] = pieces[1]
    ref[end : row + PACKED, 0:64] = pieces[2][: QUARTER // 2]
    ref[end : row + PACKED, 64:128] = pieces[2][QUARTER // 2 :]


def unpack_heads(ref, row):
    end = row + QUARTER
    third = jnp.concatenate([ref[end : row + PACKED, 0:64], ref[end : row + PACKED, 64:128]], axis=0)
    return [ref[row:end, 0:64], ref[row:end, 64:128], third]


def attention_kernel(info, rnd_own, rnd_other, t0, t1, t2, t3, w_ref, b_ref, a0, a13, a2, *rest):
    heads, lse_ref, outs = rest[:9], rest[9], rest[10]
    ones = jnp.ones((8, LENGTH), bf16)
    quarter, native = info[0], info[4]
    for slot, t_ref in enumerate((t0, t1, t2, t3)):
        rows = pl.ds(slot * QUARTER, QUARTER)
        proj = mm(t_ref[...], w_ref[...]) + b_ref[...]
        for h in range(GROUP):
            for kind in range(3):
                lo = kind * GROUP_WIDTH + h * HEAD_DIM
                piece = proj[:, lo : lo + HEAD_DIM].astype(bf16)
                if kind == 0:
                    piece = (piece.astype(f32) * score_scale).astype(bf16)
                heads[3 * h + kind][rows, :] = piece
    for h in range(GROUP):
        q_ref, k_ref, v_ref = heads[3 * h : 3 * h + 3]
        keys = k_ref[...]
        values_t = jnp.concatenate([v_ref[...].T, ones], axis=0)

        def chunk_step(chunk, carry, h=h, q_ref=q_ref, keys=keys, values_t=values_t):
            rows = pl.ds(pl.multiple_of(chunk * QUARTER, QUARTER), QUARTER)
            scores = mm_nt(keys, q_ref[rows, :])
            head = quarter * GROUP + h
            scores = biased(scores, block_bias(quarter, native, (rnd_own, rnd_other), head, chunk))
            row_max = jnp.max(scores, axis=0, keepdims=True)
            probs = jnp.exp(scores - row_max)
            out_t = mm(values_t, probs.astype(bf16))
            row_sum = out_t[HEAD_DIM : HEAD_DIM + 1]
            out_t = out_t[:HEAD_DIM] / row_sum
            outs[h, rows, :] = out_t.T.astype(bf16)
            lse_ref[pl.ds(h * TP + chunk, 1), :] = row_max + jnp.log(row_sum)
            return carry

        lax.fori_loop(0, TP, chunk_step, 0, unroll=True)
    for slot, (a_ref, row) in enumerate(((a0, 0), (a13, 0), (a2, 0), (a13, PACKED))):
        rows = slice(slot * QUARTER, (slot + 1) * QUARTER)
        pack_heads(a_ref, row, [outs[h, rows, :] for h in range(GROUP)])


def attention_back_kernel(
    h, info, rnd_own, rnd_other, q_ref, k_ref, v_ref, lse_ref, g0, g1, g2, g3, out_ref, sums_ref, do_scr, dk_scr, dv_scr, dq_scr
):
    quarter, native = info[0], info[4]
    for slot, g_ref in enumerate((g0, g1, g2, g3)):
        do_scr[slot * QUARTER : (slot + 1) * QUARTER, :] = unpack_heads(g_ref, 0)[h]
    keys = k_ref[...]
    keys_t = keys.T
    values = v_ref[...]
    dk_scr[...] = jnp.zeros_like(dk_scr)
    dv_scr[...] = jnp.zeros_like(dv_scr)

    def chunk_step(chunk, carry):
        rows = pl.ds(pl.multiple_of(chunk * QUARTER, QUARTER), QUARTER)
        queries = q_ref[rows, :]
        grad_out = do_scr[rows, :]
        scores = mm_nt(keys, queries)
        head = quarter * GROUP + h
        bias = block_bias(quarter, native, (rnd_own, rnd_other), head, chunk)
        probs = jnp.exp(biased(scores, bias - lse_ref[pl.ds(h * TP + chunk, 1), :]))
        grad_probs = mm_nt(values, grad_out)
        delta = jnp.sum(probs * grad_probs, axis=0, keepdims=True)
        grad_scores = (probs * (grad_probs - delta)).astype(bf16)
        dv_scr[...] += mm(probs.astype(bf16), grad_out)
        dk_scr[...] += mm(grad_scores, queries)
        dq_t = mm(keys_t, grad_scores) * score_scale
        dq_scr[rows, :] = dq_t.T
        return carry

    lax.fori_loop(0, TP, chunk_step, 0, unroll=True)
    for n, scr in enumerate((dq_scr, dk_scr, dv_scr)):
        out_ref[:, n * HEAD_DIM : (n + 1) * HEAD_DIM] = scr[...].astype(bf16)
    sums_ref[...] = jnp.zeros_like(sums_ref)
    sums_ref[0:1, :] = jnp.sum(out_ref[...].astype(f32), axis=0, keepdims=True)


PIECE = 2 * SLICE + VEC_ROWS
ROOT = 0.7978845608028654
CUBE = 0.044715 * ROOT


BOTH = 2 * SLICE


def held_kernel(p1, p2, p3, x1, y1, x2, y2, x3, y3, out):
    for q, (own, by_x, by_y) in enumerate(((p1, x1, y1), (p2, x2, y2), (p3, x3, y3))):
        for p, ref in enumerate((own, by_x, by_y)):
            out[(4 * q + p) * BOTH : (4 * q + p + 1) * BOTH] = ref[:BOTH]
    for q, (by_x, by_y) in enumerate(((x2, y2), (x3, y3))):
        at = (4 * q + 3) * BOTH
        out[at : at + SLICE] = by_y[BOTH:]
        out[at + SLICE : at + BOTH] = by_x[BOTH:]


def assemble_kernel(info, held, other, last_in, last_back, other_last, p1, p2, p3, w_out_ref, *outs):
    w_in_s, w_back_s, w_out_s, bias_s = outs
    quarter, mine = info[0], info[1]
    for slot in range(TP):
        start = pl.multiple_of((quarter ^ slot) * GROUP_WIDTH, GROUP_WIDTH)
        w_out_s[slot * GROUP_WIDTH : (slot + 1) * GROUP_WIDTH, :] = w_out_ref[pl.ds(start, GROUP_WIDTH), :]
    for side, main in enumerate((held, other)):
        for q in range(TP - 1):
            for p in range(4):
                start = pl.multiple_of((mine ^ PLANE_MASKS[p] ^ side) * SLICE, SLICE)
                at = (4 * q + p) * BOTH
                if q == TP - 2 and p == 3:
                    left = other_last[:SLICE] if side else last_in[...]
                    right = other_last[SLICE:] if side else last_back[...]
                else:
                    left, right = main[at : at + SLICE], main[at + SLICE : at + BOTH]
                w_in_s[q, pl.ds(start, SLICE), :] = left
                w_back_s[q, pl.ds(start, SLICE), :] = right
    for q, ref in enumerate((p1, p2, p3)):
        bias_s[q] = ref[BOTH:PIECE]


def wait_all(copies):
    for copy in copies:
        copy.wait()


def row(ref):
    return ref[...].astype(f32).reshape(1, WIDTH)


def spread(h):
    centred = h - jnp.mean(h, axis=-1, keepdims=True)
    scale = lax.rsqrt(jnp.mean(centred * centred, axis=-1, keepdims=True) + epsilon)
    return centred * scale, scale


def spread_back(grad, gain, normal, scale):
    weighted = grad * gain
    mean_one = jnp.mean(weighted, axis=-1, keepdims=True)
    mean_two = jnp.mean(weighted * normal, axis=-1, keepdims=True)
    return scale * (weighted - mean_one - normal * mean_two)


def ffn_kernel(info, t_ref, a0, a1, a2, a3, *rest):
    bias_out_ref, gain_one_ref, shift_one_ref, bias_back_ref, gain_two_ref, shift_two_ref, bias_in_ref = rest[:7]
    w_out_s, w_in_ref, w_back_ref, w_in_s, w_back_s, bias_s = rest[7:13]
    lo_ref, first_ref, second_ref, x_ref, act_ref, gp_ref, att_ref = rest[13:]
    for slot, a_ref in enumerate((a0, a1, a2, a3)):
        for h, piece in enumerate(unpack_heads(a_ref, 0)):
            lo = slot * GROUP_WIDTH + h * HEAD_DIM
            att_ref[:, lo : lo + HEAD_DIM] = piece
    first_in = t_ref[...].astype(f32) + (mm(att_ref[...], w_out_s[...]) + row(bias_out_ref))
    first_ref[...] = first_in
    first_norm = spread(first_in)[0] * row(gain_one_ref) + row(shift_one_ref)
    x = first_norm.astype(bf16)
    x_ref[...] = x
    branch = jnp.zeros((QUARTER, WIDTH), f32)
    for q in range(TP):
        cols = slice(q * WIDTH, (q + 1) * WIDTH)
        bias_q = bias_s[q - 1, 0:1, :].astype(f32) if q else row(bias_in_ref)
        pre = mm(x, w_in_s[q - 1] if q else w_in_ref[...]) + bias_q
        square = pre * pre
        half = 0.5 + 0.5 * jnp.tanh(pre * (ROOT + CUBE * square))
        wide_act = pre * half
        act = wide_act.astype(bf16)
        act_ref[:, cols] = act
        gp_ref[:, cols] = half + wide_act * (1.0 - half) * (2.0 * ROOT + 6.0 * CUBE * square)
        branch = branch + (mm_nt(act, w_back_s[q - 1]) if q else mm(act, w_back_ref[...]))
    second_in = first_norm + branch + row(bias_back_ref)
    second_ref[...] = second_in
    lo_ref[...] = (spread(second_in)[0] * row(gain_two_ref) + row(shift_two_ref)).astype(bf16)


def norm_back_kernel(second_in_ref, cot_ref, gain_two_ref, second_ref, gb_ref, vec_ref):
    normal_two, scale_two = spread(second_in_ref[...])
    grad_out = cot_ref[...].astype(f32)
    grad_second = spread_back(grad_out, row(gain_two_ref), normal_two, scale_two)
    second_ref[...] = grad_second
    grad_branch = grad_second.astype(bf16)
    gb_ref[...] = grad_branch
    vec_ref[...] = jnp.zeros_like(vec_ref)
    vec_ref[0:1, :] = jnp.sum(grad_out, axis=0, keepdims=True)
    vec_ref[1:2, :] = jnp.sum(grad_out * normal_two, axis=0, keepdims=True)
    vec_ref[2:3, :] = jnp.sum(grad_branch.astype(f32), axis=0, keepdims=True)


def position_mask(position, order):
    mask = 0
    for n, bit in enumerate(order):
        if (position >> (2 - n)) & 1:
            mask |= bit
    return mask


FFN_ORDERS = ((CORE, X_BIT, Y_BIT), (CORE, Y_BIT, X_BIT))


def weight_grads(info, left, right, keep, send, flip_scr, lhs_scr):
    mine = info[1]
    flip_scr[...] = left[...].T
    for n, order in enumerate(FFN_ORDERS):
        for p in range(SLOTS):
            start = pl.multiple_of((mine ^ position_mask(p, order)) * SLICE, SLICE)
            lhs_scr[p * SLICE : (p + 1) * SLICE, :] = flip_scr[pl.ds(start, SLICE), :]
        for pair in range(2):
            q = 2 * n + pair
            product = mm(lhs_scr[...], right[:, q * WIDTH : (q + 1) * WIDTH]).astype(bf16)
            for p in range(SLOTS):
                out = send if p >= SLOTS // 2 else keep
                out[n, p % (SLOTS // 2), pair] = product[p * SLICE : (p + 1) * SLICE, :]


def ffn_back_kernel(info, first_ref, second_ref, gb_ref, gp_ref, gain_one_ref, vec_in, *rest):
    w_out_s, w_in_ref, w_back_ref, w_in_s, w_back_s, x_ref, att_ref = rest[:7]
    g0, g13, g2, gin_ref, vec_ref, keep, send, go_keep, go_send = rest[7:16]
    gpre_ref, flip_scr, lhs_scr = rest[16:]
    grad_branch = gb_ref[...]
    grad_first = second_ref[...]
    vec_ref[...] = vec_in[...]
    for q in range(TP):
        cols = slice(q * WIDTH, (q + 1) * WIDTH)
        grad_act = mm(grad_branch, w_back_s[q - 1]) if q else mm_nt(grad_branch, w_back_ref[...])
        grad_pre = (grad_act * gp_ref[:, cols]).astype(bf16)
        gpre_ref[:, cols] = grad_pre
        vec_ref[pl.ds(6 + (info[2] ^ q), 1), :] = jnp.sum(grad_pre.astype(f32), axis=0, keepdims=True)
        grad_first = grad_first + mm_nt(grad_pre, w_in_s[q - 1] if q else w_in_ref[...])
    normal_one, scale_one = spread(first_ref[...])
    vec_ref[3:4, :] = jnp.sum(grad_first, axis=0, keepdims=True)
    vec_ref[4:5, :] = jnp.sum(grad_first * normal_one, axis=0, keepdims=True)
    grad_in = spread_back(grad_first, row(gain_one_ref), normal_one, scale_one)
    gin_ref[...] = grad_in
    grad_mixed = grad_in.astype(bf16)
    vec_ref[5:6, :] = jnp.sum(grad_mixed.astype(f32), axis=0, keepdims=True)
    grad_att = mm_nt(grad_mixed, w_out_s[...]).astype(bf16)
    for slot, (g_ref, row_at) in enumerate(((g0, 0), (g13, 0), (g2, 0), (g13, PACKED))):
        lo = slot * GROUP_WIDTH
        pack_heads(
            g_ref, row_at, [grad_att[:, lo + h * HEAD_DIM : lo + (h + 1) * HEAD_DIM] for h in range(GROUP)]
        )
    weight_grads(info, x_ref, gpre_ref, keep, send, flip_scr, lhs_scr)
    product = mm(grad_mixed.T, att_ref[...]).astype(bf16)
    go_keep[...] = product[:, : 2 * GROUP_WIDTH]
    go_send[...] = product[:, 2 * GROUP_WIDTH :]


ORDER_LA = (4, 2, 1)
ORDER_LB = (2, 4, 1)


HALF = WIDTH // 2
HELD = SLOTS // 2 * SLICE


def flip_kernel(t0, t1, t2, t3, out_ref):
    for slot, t_ref in enumerate((t0, t1, t2, t3)):
        out_ref[:, slot * QUARTER : (slot + 1) * QUARTER] = t_ref[...].T


def qkv_grad_kernel(
    info, tokens_t, gh0, gh1, gh2, go_own, go_near, vec_ref, s0, s1, s2, la_keep, la_send, lb_keep, lb_send, out_scr
):
    quarter, here = info[0], info[3]
    for h, gh_ref in enumerate((gh0, gh1, gh2)):
        product = mm(tokens_t[...], gh_ref[...]).astype(bf16)
        for kind in range(3):
            lo = kind * GROUP_WIDTH + h * HEAD_DIM
            out_scr[:, lo : lo + HEAD_DIM] = product[:, kind * HEAD_DIM : (kind + 1) * HEAD_DIM]
    add_to(out_scr.at[:, 3 * GROUP_WIDTH :], go_own[...], go_near[...])
    for keep, send, order, lo in (
        (la_keep, la_send, ORDER_LA, 0),
        (lb_keep, lb_send, ORDER_LB, HALF),
    ):
        for p in range(SLOTS):
            start = pl.multiple_of((here ^ position_mask(p, order)) * SLICE, SLICE)
            out = send if p >= SLOTS // 2 else keep
            row = p % (SLOTS // 2) * SLICE
            out[row : row + SLICE, :] = out_scr[pl.ds(start, SLICE), lo : lo + HALF]
    placed = []
    for kind in (0, 2):
        cols = slice(kind * HEAD_DIM, (kind + 1) * HEAD_DIM)
        piece = jnp.concatenate([sums[0:1, cols] for sums in (s0, s1, s2)], axis=1)
        placed.append(
            jnp.concatenate([jnp.where(quarter == g, piece, 0.0) for g in range(TP)], axis=1)
        )
    vectors = jnp.concatenate([vec_ref[0:10, :]] + placed + [vec_ref[12:VEC_ROWS, :]], axis=0)
    vectors = vectors.astype(bf16)
    for out in (la_keep, la_send, lb_keep, lb_send):
        out[HELD : HELD + VEC_ROWS, :] = vectors[:, :HALF]
        out[HELD + VEC_ROWS :, :] = vectors[:, HALF:]


def token_grad_kernel(gh0, gh1, gh2, w_ref, keep_ref, send_ref, all_scr):
    for h, gh_ref in enumerate((gh0, gh1, gh2)):
        for kind in range(3):
            lo = kind * GROUP_WIDTH + h * HEAD_DIM
            all_scr[:, lo : lo + HEAD_DIM] = gh_ref[:, kind * HEAD_DIM : (kind + 1) * HEAD_DIM]
    half = LENGTH // 2
    send_ref[...] = mm_nt(all_scr[half:, :], w_ref[...]).astype(bf16)
    keep_ref[...] = mm_nt(all_scr[:half, :], w_ref[...]).astype(bf16)


FFN_AT = 16 * SLICE + VEC_ROWS
HALF_GROUPS = TP // 2 * GROUP_WIDTH


def write_half(info, side, plane, qkv_hbm, out_hbm, w_in_hbm, qkv_scr, out_scr, w_in_scr, sems):
    quarter, mine, here = info[0], info[1], info[3]
    core = (quarter >> 1) ^ side
    first_col = core * HALF_GROUPS
    copies = []

    def send(source, target):
        copies.append(pltpu.make_async_copy(source, target, sems.at[len(copies)]))
        copies[-1].start()

    def piece(at, cols):
        block_off = here ^ at
        xy = ((block_off >> 2) & 1) + (block_off & 2)
        parts = []
        for group in range(2):
            nth = xy * 4 + ((quarter & 1) ^ group) + 2 * (block_off & 1)
            parts.append(plane[pl.ds(pl.multiple_of(nth * SLICE, SLICE), SLICE), cols])
        return jnp.concatenate(parts, axis=1).astype(f32)

    for chunk in range(SLOTS // 2):
        rows = pl.ds(2 * chunk * SLICE, 2 * SLICE)
        for kind in range(3):
            cols = pl.ds(kind * HALF_GROUPS, HALF_GROUPS)
            for at in (2 * chunk, 2 * chunk + 1):
                qkv_scr[at * SLICE : (at + 1) * SLICE, kind * HALF_GROUPS : (kind + 1) * HALF_GROUPS] = piece(
                    at, slice(kind * GROUP_WIDTH, (kind + 1) * GROUP_WIDTH)
                )
            to = pl.ds(pl.multiple_of(kind * WIDTH + first_col, 128), HALF_GROUPS)
            send(qkv_scr.at[rows, cols], qkv_hbm.at[rows, to])
        at = 2 * chunk + core
        mask = mine ^ at
        nth = (((mask >> 1) & 1) + ((mask >> 2) & 1) * 2) * 2
        start = pl.multiple_of(FFN_AT + nth * SLICE, VEC_ROWS)
        here_rows = pl.ds(chunk * SLICE, SLICE)
        w_in_scr[here_rows, :] = plane[pl.ds(start, SLICE), :].astype(f32)
        send(w_in_scr.at[here_rows, :], w_in_hbm.at[pl.ds(pl.multiple_of(at * SLICE, SLICE), SLICE), :])
    cols = slice(3 * GROUP_WIDTH, 4 * GROUP_WIDTH)
    out_scr[...] = jnp.concatenate([piece(at, cols) for at in range(SLOTS)], axis=0).T
    send(out_scr, out_hbm.at[pl.ds(pl.multiple_of(first_col, HALF_GROUPS), HALF_GROUPS), :])
    return copies


def first_half_kernel(info, plane, low_tokens, low_out, qkv_hbm, out_hbm, w_in_hbm, layer_out, token_out, *scratch):
    whole = [
        pltpu.make_async_copy(low_out, layer_out, scratch[4].at[0]),
        pltpu.make_async_copy(low_tokens, token_out, scratch[4].at[1]),
    ]
    for copy in whole:
        copy.start()
    wait_all(write_half(info, 0, plane, qkv_hbm, out_hbm, w_in_hbm, *scratch[:4]) + whole)


def second_half_kernel(info, plane, other, _qkv, _out, _w_in, qkv_hbm, out_hbm, w_in_hbm, w_back_hbm, *rest):
    vec_outs, scratch = rest[:9], rest[9:]
    mine, z_here = info[1], info[2]
    flip_scr, back_scr, sem = scratch[4:]
    for core in range(2):

        @pl.when((mine & 1) == core)
        def _(core=core):
            for at in range(SLOTS):
                mask = mine ^ at
                nth = (((mask >> 1) & 1) + ((mask >> 2) & 1) * 2) * 2 + 1
                start = pl.multiple_of(FFN_AT + nth * SLICE, VEC_ROWS)
                ref = plane if (at & 1) == core else other
                flip_scr[at * SLICE : (at + 1) * SLICE, :] = ref[pl.ds(start, SLICE), :].astype(f32)

    back_scr[...] = flip_scr[...].T
    back_copy = pltpu.make_async_copy(back_scr, w_back_hbm, sem)
    back_copy.start()
    copies = write_half(info, 1, other, qkv_hbm, out_hbm, w_in_hbm, *scratch[:4])
    vec_rows = slice(16 * SLICE, FFN_AT)
    vectors = total(plane[vec_rows, :], other[vec_rows, :])
    bias_in = jnp.zeros((1, WIDTH), f32)
    for q in range(TP):
        bias_in = jnp.where(z_here == q, vectors[6 + q : 7 + q, :], bias_in)
    for out, n in zip(vec_outs[:8], (0, 1, 2, 3, 4, 5, 10, 11)):
        out[...] = vectors[n]
    vec_outs[8][...] = bias_in[0]
    wait_all(copies + [back_copy])


def add_to(out, *terms):
    out[...] = add_low(*terms)


def join_kernel(*refs):
    out, at = refs[-1], 0
    for ref in refs[:-1]:
        out[at : at + ref.shape[0]] = ref[...]
        at += ref.shape[0]


def diag_kernel(by_x, by_y, first, second):
    half = first.shape[0]
    first[...] = by_x[:half]
    second[...] = by_y[half:]


def trim_kernel(piece, out):
    out[...] = piece[:BOTH]


def mix_kernel(by_x, by_y, own, to_x, to_y):
    to_x[:BOTH] = own[:BOTH]
    to_x[BOTH:] = by_y[SLICE:BOTH]
    to_y[:BOTH] = own[:BOTH]
    to_y[BOTH:] = by_x[:SLICE]


def last_mix_kernel(by_x, by_y, to_x, to_y):
    to_x[...] = by_y[SLICE:BOTH]
    to_y[...] = by_x[:SLICE]


def level_one_kernel(keep, other, first, second):
    add_to(first, keep[0, 2:], other[0, 2:])
    add_to(second, keep[1, 2:], other[1, 2:])


def middle_kernel(in_keep, in_other, back_keep, back_other, back_x, back_y, to_x, to_y):
    for n in range(2):
        out = to_y if n else to_x
        for p in range(2):
            for pair in range(2):
                add_to(out.at[2 * p + pair], in_keep[n, 2 + p, pair], in_other[n, 2 + p, pair])
    for pair in range(2):
        add_to(to_y.at[4 + pair], back_keep[0, 1, pair], back_other[0, 1, pair], back_x[1, pair])
        add_to(to_x.at[4 + pair], back_keep[1, 1, pair], back_other[1, 1, pair], back_y[1, pair])


def in_two_kernel(keep, other, by_x, by_y, first, second):
    for pair in range(2):
        add_to(first.at[pair], keep[0, 1, pair], other[0, 1, pair], by_x[2 + pair])
        add_to(second.at[pair], keep[1, 1, pair], other[1, 1, pair], by_y[2 + pair])


def in_plane_kernel(keep, other, by_x, by_y, by_xy, by_yx, near, kept):
    for q in range(TP):
        order, pair = q // 2, q % 2
        first, second = (by_x, by_xy) if order == 0 else (by_y, by_yx)
        out = near if q % 2 else kept
        add_to(out.at[q // 2], keep[order, 0, pair], other[order, 0, pair], first[pair], second[pair])


def back_plane_kernel(keep, other, by_x, by_y, mid_x, mid_y, near, kept):
    for q in range(TP):
        order, pair = q // 2, q % 2
        first, second = (by_x, mid_y) if order == 0 else (by_y, mid_x)
        out = near if q % 2 else kept
        add_to(out.at[q // 2], keep[order, 0, pair], other[order, 0, pair], first[0, pair], second[4 + pair])


def far_kernel(kept, near, far):
    add_to(far, kept[1], near[1])


def last_kernel(kept_a, near_a, far_a, kept_b, near_b, far_b, out):
    add_to(out.at[0], kept_a[0], near_a[0], far_a[...])
    add_to(out.at[1], kept_b[0], near_b[0], far_b[...])


def go_kernel(keep, other, own, send):
    add_to(own, keep[:, :GROUP_WIDTH], other[:, :GROUP_WIDTH])
    add_to(send, keep[:, GROUP_WIDTH:], other[:, GROUP_WIDTH:])


def near_kernel(keep, other, out):
    add_to(out, keep[QUARTER:], other[QUARTER:])


def tokens_kernel(keep, other, near, grad_in, out_here, tokens, again):
    add_to(tokens, keep[:QUARTER], other[:QUARTER], near[...], grad_in[...])
    again[...] = out_here[...]


TWO = 2 * SLICE


def qkv_two_kernel(la, ra, lb, rb, la_out, lb_out):
    add_to(la_out, la[TWO:], ra[TWO:])
    add_to(lb_out, lb[TWO:HELD], rb[TWO:HELD])


def qkv_three_kernel(la, ra, ra2, lb, rb, rb2, out):
    add_to(out.at[:TWO, :HALF], la[:TWO], ra[:TWO], ra2[:TWO])
    add_to(out.at[:TWO, HALF:], lb[:TWO], rb[:TWO], rb2[...])
    for n in range(2):
        rows = slice(HELD + n * VEC_ROWS, HELD + (n + 1) * VEC_ROWS)
        rows_two = slice(TWO + n * VEC_ROWS, TWO + (n + 1) * VEC_ROWS)
        add_to(out.at[TWO:, n * HALF : (n + 1) * HALF], la[rows], ra[rows], ra2[rows_two])


def qkv_four_kernel(own, other, out):
    add_to(out.at[:SLICE], own[:SLICE], other[SLICE:TWO])
    add_to(out.at[SLICE:TWO], own[SLICE:TWO], other[:SLICE])
    add_to(out.at[TWO:], own[TWO:], other[TWO:])


def mix_l_kernel(by_x, by_y, other, to_x, to_y):
    to_x[:TWO] = other[:TWO]
    to_x[TWO:] = by_y[SLICE:TWO]
    to_y[:TWO] = other[:TWO]
    to_y[TWO:] = by_x[:SLICE]


def diag_kernel(l_x, l_y, f_x, f_y, to_x, to_y):
    to_x[:SLICE] = l_y[SLICE:TWO]
    to_x[SLICE:] = f_y[1]
    to_y[:SLICE] = l_x[:SLICE]
    to_y[SLICE:] = f_x[0]


def plane_l_kernel(own, other, x_own, y_own, x_other, y_other, f_own, f_x, f_y, d_x, d_y, out):
    diag_own = (y_other[TWO:], x_other[TWO:])
    diag_other = (d_y[:SLICE], d_x[:SLICE])
    places = (
        ((own[:SLICE], own[SLICE:TWO]), (other[:SLICE], other[SLICE:TWO])),
        ((x_own[:SLICE], x_own[SLICE:TWO]), (x_other[:SLICE], x_other[SLICE:TWO])),
        ((y_own[:SLICE], y_own[SLICE:TWO]), (y_other[:SLICE], y_other[SLICE:TWO])),
        (diag_own, diag_other),
    )
    for p, (here, there) in enumerate(places):
        for slot in range(TP):
            at = (p * TP + slot) * SLICE
            out[at : at + SLICE] = (there if slot % 2 else here)[slot // 2]
    add_to(out.at[16 * SLICE : FFN_AT], own[TWO:], other[TWO:])
    for n, (left, right) in enumerate(
        ((f_own[0], f_own[1]), (f_x[0], f_x[1]), (f_y[0], f_y[1]), (d_y[SLICE:], d_x[SLICE:]))
    ):
        out[FFN_AT + 2 * n * SLICE : FFN_AT + (2 * n + 1) * SLICE] = left
        out[FFN_AT + (2 * n + 1) * SLICE : FFN_AT + (2 * n + 2) * SLICE] = right


VMEM = pl.BlockSpec(memory_space=pltpu.VMEM)
SMEM = pl.BlockSpec(memory_space=pltpu.SMEM)
HBM = pl.BlockSpec(memory_space=pl.ANY)


def call(kernel, in_specs, outs, scratch, vmem_mib, name, deps=()):
    count, extra = len(in_specs), len(deps)

    def body(*refs):
        kernel(*refs[:count], *refs[count + extra :])

    run = pl.pallas_call(
        body,
        out_shape=[jax.ShapeDtypeStruct(shape, dtype) for shape, dtype in outs],
        in_specs=list(in_specs) + [HBM] * extra,
        out_specs=[VMEM] * len(outs),
        scratch_shapes=scratch,
        compiler_params=pltpu.CompilerParams(vmem_limit_bytes=vmem_mib * 1024 * 1024),
        cost_estimate=pl.CostEstimate(flops=1, bytes_accessed=1, transcendentals=0),
        name=name,
    )
    return lambda *arrays: run(*arrays, *deps)


def step(kernel, name, outs, *arrays, deps=()):
    shapes = [(shape, bf16) for shape in outs]
    result = call(kernel, [VMEM] * len(arrays), shapes, [], 12, name, deps)(*arrays)
    return result[0] if len(outs) == 1 else result


def per_device(
    tokens,
    w_qkv,
    bias_query,
    bias_value,
    w_out,
    bias_out,
    gain_attn,
    shift_attn,
    w_in,
    bias_in,
    w_back,
    bias_back,
    gain_ffn,
    shift_ffn,
    random_blocks,
    cotangent,
):
    dp_count = lax.axis_size("dp")
    d = lax.axis_index("dp")
    z = lax.axis_index("tp")
    core = d & 1
    quarter = (z & 1) + 2 * core
    mine = d & (SLOTS - 1)
    here = ((d >> 1) & 1) * 4 + ((d >> 2) & 1) * 2 + (z >> 1)
    native = (core == z // 2).astype(jnp.int32)
    info = jnp.stack([quarter, mine, z, here, native]).astype(jnp.int32)
    extra_bits = [1 << b for b in range(3, dp_count.bit_length() - 1)]

    own_tokens = place(tokens[0])
    piece = call(
        piece_kernel,
        [SMEM, HBM, VMEM, VMEM],
        [((2 * SLICE + VEC_ROWS, WIDTH), bf16)],
        [pltpu.VMEM((WIDTH, WIDTH), bf16), pltpu.SemaphoreType.DMA],
        8,
        "piece",
    )(info, w_in, w_back, bias_in)[0]
    piece_one = hop(piece, 0, 1)
    again = step(join_kernel, "again", [(PIECE, WIDTH)], piece, deps=(own_tokens,))
    piece_two = hop(again, 0, 2)
    random_own = random_blocks.reshape(-1)
    random_other = hop(random_own, CORE, 0)
    w_group, bias_group = call(
        group_kernel,
        [SMEM, VMEM, VMEM, VMEM],
        [((WIDTH, 3 * GROUP_WIDTH), bf16), ((1, 3 * GROUP_WIDTH), f32)],
        [],
        16,
        "group",
    )(info, w_qkv, bias_query, bias_value)
    near_tokens = hop(own_tokens, 0, 1)
    core_tokens = hop(own_tokens, CORE, 0)
    far_tokens = hop(near_tokens, CORE, 0)
    trimmed = step(trim_kernel, "trim", [(BOTH, WIDTH)], piece_one, deps=(w_group, random_other))
    x_one = hop(trimmed, X_BIT, 0)
    y_one = hop(trimmed, Y_BIT, 0)
    piece_three = hop(piece_two, 0, 1)
    cot = place(cotangent[0])
    mixed = [(BOTH + SLICE, WIDTH)] * 2
    to_x, to_y = step(mix_kernel, "mix_two", mixed, x_one, y_one, piece_two, deps=(near_tokens,))
    x_two = hop(to_x, X_BIT, 0)
    y_two = hop(to_y, Y_BIT, 0)

    packed = ((PACKED, 2 * HEAD_DIM), bf16)
    double = ((2 * PACKED, 2 * HEAD_DIM), bf16)
    per_head = ((LENGTH, HEAD_DIM), bf16)
    token_slots = (own_tokens, near_tokens, core_tokens, far_tokens)
    a0, a13, a2, *heads = call(
        attention_kernel,
        [SMEM] * 3 + [VMEM] * 6,
        [packed, double, packed] + [per_head] * 9 + [((16, QUARTER), f32)],
        [pltpu.VMEM((GROUP, LENGTH, HEAD_DIM), bf16)],
        24,
        "attention",
        (to_x,),
    )(info, random_own, random_other, *token_slots, w_group, bias_group)
    heads, lse = heads[:9], heads[9]
    a1 = hop(a13, 0, 1)
    a2 = hop(a2, CORE, 0)
    a3 = hop(a1[PACKED:], CORE, 0)
    to_x, to_y = step(mix_kernel, "mix_three", mixed, x_two, y_two, piece_three, deps=(a0,))
    x_three = hop(to_x, X_BIT, 0)
    y_three = hop(to_y, Y_BIT, 0)
    tokens_t = call(flip_kernel, [VMEM] * 4, [((WIDTH, LENGTH), bf16)], [], 8, "flip_tokens", (a1, to_x))(
        *token_slots
    )[0]
    to_x, to_y = step(
        last_mix_kernel, "mix_last", [(SLICE, WIDTH)] * 2, x_three, y_three, deps=(tokens_t,)
    )
    last_back = hop(to_x, X_BIT, 0)
    last_in = hop(to_y, Y_BIT, 0)
    pieces = (piece_one, piece_two, piece_three)
    held = step(
        held_kernel,
        "held",
        [(11 * BOTH, WIDTH)],
        *pieces,
        x_one,
        y_one,
        x_two,
        y_two,
        x_three,
        y_three,
        deps=(to_x,),
    )
    last = step(join_kernel, "last_piece", [(BOTH, WIDTH)], last_in, last_back, deps=(held,))
    quarters = ((TP - 1, WIDTH, WIDTH), bf16)
    w_in_s, w_back_s, w_out_s, bias_s = call(
        assemble_kernel,
        [SMEM] + [VMEM] * 9,
        [quarters, quarters, ((WIDTH, WIDTH), bf16), ((TP - 1, VEC_ROWS, WIDTH), bf16)],
        [],
        12,
        "assemble",
    )(info, held, hop(held, CORE, 0), last_in, last_back, hop(last, CORE, 0), *pieces, w_out)

    rows = ((QUARTER, WIDTH), bf16)
    wide = ((QUARTER, TP * WIDTH), bf16)
    rows_f32 = ((QUARTER, WIDTH), f32)
    vec_rows = ((VEC_ROWS, WIDTH), f32)
    out_here, first_in, second_in, ffn_input, activated, gelu_slope, attended = call(
        ffn_kernel,
        [SMEM] + [VMEM] * 18,
        [rows, rows_f32, rows_f32, rows, wide, ((QUARTER, TP * WIDTH), f32), rows],
        [],
        14,
        "ffn",
        (tokens_t,),
    )(
        info,
        own_tokens,
        a0,
        a1,
        a2,
        a3,
        bias_out,
        gain_attn,
        shift_attn,
        bias_back,
        gain_ffn,
        shift_ffn,
        bias_in,
        w_out_s,
        w_in,
        w_back,
        w_in_s,
        w_back_s,
        bias_s,
    )
    grad_second, grad_branch, vectors = call(
        norm_back_kernel, [VMEM] * 3, [rows_f32, rows, vec_rows], [], 10, "norm_back"
    )(second_in, cot, gain_ffn)
    pairs = ((2, SLOTS // 2, 2, SLICE, WIDTH), bf16)
    halves = ((WIDTH, 2 * GROUP_WIDTH), bf16)
    flips = [pltpu.VMEM((WIDTH, QUARTER), bf16), pltpu.VMEM((WIDTH, QUARTER), bf16)]
    back_keep, back_send = call(
        weight_grads, [SMEM] + [VMEM] * 2, [pairs] * 2, flips, 8, "back_grads"
    )(info, grad_branch, activated)
    back_other = hop(back_send, CORE, 0)

    g0, g13, g2, grad_in, vectors, in_keep, in_send, go_keep, go_send = call(
        ffn_back_kernel,
        [SMEM] + [VMEM] * 13,
        [packed, double, packed, rows_f32, vec_rows] + [pairs] * 2 + [halves] * 2,
        [pltpu.VMEM((QUARTER, TP * WIDTH), bf16)] + flips,
        12,
        "ffn_back",
        (back_keep,),
    )(
        info,
        first_in,
        grad_second,
        grad_branch,
        gelu_slope,
        gain_attn,
        vectors,
        w_out_s,
        w_in,
        w_back,
        w_in_s,
        w_back_s,
        ffn_input,
        attended,
    )
    g1 = hop(g13, 0, 1)
    g2 = hop(g2, CORE, 0)
    g3 = hop(g1[PACKED:], CORE, 0)

    first_level = [(2, 2, SLICE, WIDTH)] * 2
    def hop_pair(pair, first, second):
        return hop(pair[0], first, 0), hop(pair[1], second, 0)

    back_sums = step(level_one_kernel, "back_one", first_level, back_keep, back_other, deps=(g13,))
    back_x, back_y = hop_pair(back_sums, X_BIT, Y_BIT)
    in_other = hop(in_send, CORE, 0)
    go_other = hop(go_send, CORE, 0)

    def head_back(h, deps):
        return call(
            functools.partial(attention_back_kernel, h),
            [SMEM] * 3 + [VMEM] * 8,
            [((LENGTH, 3 * HEAD_DIM), bf16), ((8, 3 * HEAD_DIM), f32)],
            [
                pltpu.VMEM((LENGTH, HEAD_DIM), bf16),
                pltpu.VMEM((LENGTH, HEAD_DIM), f32),
                pltpu.VMEM((LENGTH, HEAD_DIM), f32),
                pltpu.VMEM((LENGTH, HEAD_DIM), f32),
            ],
            12,
            f"attention_back_{h}",
            deps,
        )(info, random_own, random_other, *heads[3 * h : 3 * h + 3], lse, g0, g1, g2, g3)

    go_own, go_send = step(go_kernel, "go", [(WIDTH, GROUP_WIDTH)] * 2, go_keep, go_other)
    go_near = hop(go_send, 0, 1)
    gh0, s0 = head_back(0, (go_own, back_sums[0]))
    back_parts = [back_keep, back_other, back_x, back_y]
    to_x, to_y = step(
        middle_kernel,
        "middle",
        [(6, SLICE, WIDTH)] * 2,
        in_keep,
        in_other,
        *back_parts,
        deps=(gh0,),
    )
    mid_x, mid_y = hop(to_x, X_BIT, 0), hop(to_y, Y_BIT, 0)
    in_parts = [in_keep, in_other, mid_x, mid_y]
    z_level = [(2, SLICE, WIDTH)] * 2
    gh1, s1 = head_back(1, (to_x,))
    gh2, s2 = head_back(2, (gh1,))

    la_keep, la_send, lb_keep, lb_send = call(
        qkv_grad_kernel,
        [SMEM] + [VMEM] * 10,
        [((HELD + 2 * VEC_ROWS, HALF), bf16)] * 4,
        [pltpu.VMEM((WIDTH, 4 * GROUP_WIDTH), bf16)],
        16,
        "qkv_grads",
        (gh2,),
    )(info, tokens_t, gh0, gh1, gh2, go_own, go_near, vectors, s0, s1, s2)
    ra = hop(la_send, X_BIT, 0)
    rb = hop(lb_send, Y_BIT, 0)

    keep, send = call(
        token_grad_kernel,
        [VMEM] * 4,
        [((LENGTH // 2, WIDTH), bf16)] * 2,
        [pltpu.VMEM((LENGTH, 3 * GROUP_WIDTH), bf16)],
        16,
        "token_grad",
        (la_keep,),
    )(gh0, gh1, gh2, w_group)
    other = hop(send, CORE, 0)
    near_b, kept_b = step(
        back_plane_kernel, "back_plane", z_level, *back_parts, mid_x, mid_y, deps=(keep,)
    )
    near_b = hop(near_b, 0, 1)
    sums = step(in_two_kernel, "in_two", z_level, *in_parts, deps=(kept_b,))
    in_parts += hop_pair(sums, Y_BIT, X_BIT)
    near_low = step(near_kernel, "near", [(QUARTER, WIDTH)], keep, other, deps=(sums[0],))
    near = hop(near_low, 0, 1)
    far_b = step(far_kernel, "far_back", [(SLICE, WIDTH)], kept_b, near_b, deps=(near_low,))
    far_hop_b = hop(far_b, 0, 2)
    la2, lb2 = step(
        qkv_two_kernel,
        "qkv_two",
        [(TWO + 2 * VEC_ROWS, HALF), (TWO, HALF)],
        la_keep,
        ra,
        lb_keep,
        rb,
        deps=(far_b,),
    )
    ra2 = hop(la2, Y_BIT, 0)
    rb2 = hop(lb2, X_BIT, 0)
    rows_l = (TWO + VEC_ROWS, WIDTH)
    near_a, kept_a = step(in_plane_kernel, "in_plane", z_level, *in_parts, deps=(la2,))
    near_a = hop(near_a, 0, 1)
    partial = step(
        qkv_three_kernel, "qkv_three", [rows_l], la_keep, ra, ra2, lb_keep, rb, rb2, deps=(kept_a, far_hop_b)
    )
    far_a = step(far_kernel, "far_in", [(SLICE, WIDTH)], kept_a, near_a, deps=(partial, far_hop_b))
    far_hop_a = hop(far_a, 0, 2)
    sum_l = step(
        qkv_four_kernel, "qkv_four", [rows_l], partial, hop(partial, 0, 2), deps=(far_a, near)
    )
    for bit in extra_bits:
        sum_l = add_low(sum_l, hop(sum_l, bit, 0))

    own_l = sum_l[:TWO]
    x_own = hop(own_l, X_BIT, 0)
    y_own = hop(own_l, Y_BIT, 0)
    other_l = hop(sum_l, 0, 1)
    to_x, to_y = step(
        mix_l_kernel, "mix_l", [(TWO + SLICE, WIDTH)] * 2, x_own, y_own, other_l
    )
    x_other = hop(to_x, X_BIT, 0)
    y_other = hop(to_y, Y_BIT, 0)
    sum_f = step(
        last_kernel,
        "last",
        [(2, SLICE, WIDTH)],
        kept_a,
        near_a,
        far_hop_a,
        kept_b,
        near_b,
        far_hop_b,
        deps=(to_x,),
    )
    for bit in extra_bits:
        sum_f = add_low(sum_f, hop(sum_f, bit, 0))
    low_outs = step(
        tokens_kernel,
        "tokens",
        [(QUARTER, WIDTH)] * 2,
        keep,
        other,
        near,
        grad_in,
        out_here,
        deps=(sum_f,),
    )
    token_grads, layer_out = place(low_outs[0]), place(low_outs[1])
    f_x = hop(sum_f, X_BIT, 0)
    f_y = hop(sum_f, Y_BIT, 0)
    diag = step(diag_kernel, "diag", [(TWO, WIDTH)] * 2, x_other, y_other, f_x, f_y)
    d_x, d_y = hop_pair(diag, X_BIT, Y_BIT)
    plane = step(
        plane_l_kernel,
        "plane",
        [(FFN_AT + SLOTS * SLICE, WIDTH)],
        sum_l,
        other_l,
        x_own,
        y_own,
        x_other,
        y_other,
        sum_f,
        f_x,
        f_y,
        d_x,
        d_y,
        deps=(token_grads, layer_out),
    )
    square = ((WIDTH, WIDTH), f32)
    halves_out = [((WIDTH, 3 * WIDTH), f32), square, square]
    half_scratch = [
        pltpu.VMEM((WIDTH, 3 * HALF_GROUPS), f32),
        pltpu.VMEM((HALF_GROUPS, WIDTH), f32),
        pltpu.VMEM((WIDTH // 2, WIDTH), f32),
        pltpu.SemaphoreType.DMA((2 * SLOTS + 1,)),
    ]
    as_shape = lambda outs: [jax.ShapeDtypeStruct(shape, dtype) for shape, dtype in outs]
    cheap = pl.CostEstimate(flops=1, bytes_accessed=1, transcendentals=0)
    *half_written, layer_out, grad_tokens = pl.pallas_call(
        first_half_kernel,
        out_shape=as_shape(halves_out + [rows, rows]),
        in_specs=[SMEM] + [VMEM] * 3,
        out_specs=[HBM] * 5,
        scratch_shapes=half_scratch + [pltpu.SemaphoreType.DMA((2,))],
        compiler_params=pltpu.CompilerParams(vmem_limit_bytes=16 * 1024 * 1024),
        cost_estimate=cheap,
        name="first_half",
    )(info, plane, token_grads, layer_out)
    grad_w_qkv, grad_w_out, grad_w_in, grad_w_back, *vec_outs = pl.pallas_call(
        second_half_kernel,
        out_shape=as_shape(halves_out + [square] + [((WIDTH,), f32)] * 9),
        in_specs=[SMEM, VMEM, VMEM] + [HBM] * 3,
        out_specs=[HBM] * 4 + [VMEM] * 9,
        scratch_shapes=half_scratch + [pltpu.VMEM((WIDTH, WIDTH), f32)] * 2 + [pltpu.SemaphoreType.DMA],
        input_output_aliases={3: 0, 4: 1, 5: 2},
        compiler_params=pltpu.CompilerParams(vmem_limit_bytes=24 * 1024 * 1024),
        cost_estimate=cheap,
        name="second_half",
    )(info, plane, hop(plane, CORE, 0), *half_written)
    (
        grad_shift_ffn,
        grad_gain_ffn,
        grad_bias_back,
        grad_shift_attn,
        grad_gain_attn,
        grad_bias_out,
        grad_bias_query,
        grad_bias_value,
        grad_bias_in,
    ) = vec_outs
    return (
        layer_out[None],
        grad_tokens[None],
        grad_w_qkv,
        grad_bias_query,
        grad_bias_value,
        grad_w_out,
        grad_bias_out,
        grad_gain_attn,
        grad_shift_attn,
        grad_w_in,
        grad_bias_in,
        grad_w_back,
        grad_bias_back,
        grad_gain_ffn,
        grad_shift_ffn,
    )


def solution(mesh):
    in_specs = (
        P("dp", "tp", None),
        P(),
        P(),
        P(),
        P(),
        P(),
        P(),
        P(),
        P(None, "tp"),
        P("tp"),
        P("tp", None),
        P(),
        P(),
        P(),
        P("dp", None, None, None),
        P("dp", "tp", None),
    )
    out_specs = (
        P("dp", "tp", None),
        P("dp", "tp", None),
        P(),
        P(),
        P(),
        P(),
        P(),
        P(),
        P(),
        P(None, "tp"),
        P("tp"),
        P("tp", None),
        P(),
        P(),
        P(),
    )
    return jax.shard_map(
        per_device, mesh=mesh, in_specs=in_specs, out_specs=out_specs, check_vma=False
    )
```

```python
import functools

import jax
import jax.numpy as jnp
from jax import lax
from jax.experimental import pallas as pl
from jax.experimental.pallas import tpu as pltpu
from jax.sharding import PartitionSpec as P

HEADS = 12
BLOCK = 64
HEAD_DIM = 64
TP = 4
GROUP = HEADS // TP
QUARTER = 256
LENGTH = TP * QUARTER
WIDTH = HEADS * HEAD_DIM
GROUP_WIDTH = GROUP * HEAD_DIM
SLOTS = 8
SLICE = WIDTH // SLOTS
VEC_ROWS = 16
CORE, X_BIT, Y_BIT = 1, 2, 4
PLANE_MASKS = (0, X_BIT, Y_BIT, X_BIT | Y_BIT)

epsilon = 1e-05
masked_score = -1e30
score_scale = HEAD_DIM ** (-0.5)
f32 = jnp.float32
bf16 = jnp.bfloat16


def mm(left, right):
    return jnp.dot(left, right, preferred_element_type=f32)


def mm_nt(left, right):
    return lax.dot_general(left, right, (((1,), (1,)), ((), ())), preferred_element_type=f32)


def total(*terms):
    acc = terms[0].astype(f32)
    for term in terms[1:]:
        acc = acc + term.astype(f32)
    return acc


def add_low(*terms):
    return total(*terms).astype(bf16)


def hop(array, dp_mask, z_mask):
    dp_count = lax.axis_size("dp")
    pairs = [
        (d * TP + z, (d ^ dp_mask) * TP + (z ^ z_mask)) for d in range(dp_count) for z in range(TP)
    ]
    return lax.ppermute(array, ("dp", "tp"), pairs)


def place(array):
    dp_count = lax.axis_size("dp")
    pairs = []
    for d in range(dp_count):
        for z in range(TP):
            here = d * TP + z
            away = (d ^ CORE) * TP + (z ^ 2)
            pairs.append((here, here if (d & 1) == z // 2 else away))
    return lax.ppermute(array, ("dp", "tp"), pairs)


def piece_kernel(info, w_in_hbm, w_back_ref, bias_ref, piece_ref, flip_scr, sem):
    start = pl.multiple_of(info[1] * SLICE, SLICE)
    copy = pltpu.make_async_copy(
        w_in_hbm.at[pl.ds(start, SLICE), :], piece_ref.at[pl.ds(0, SLICE), :], sem
    )
    copy.start()
    flip_scr[...] = w_back_ref[...].T
    piece_ref[SLICE : 2 * SLICE, :] = flip_scr[pl.ds(start, SLICE), :]
    bias = bias_ref[...].astype(f32).reshape(1, WIDTH)
    piece_ref[2 * SLICE :, :] = jnp.broadcast_to(bias, (VEC_ROWS, WIDTH)).astype(bf16)
    copy.wait()


def group_kernel(info, w_ref, bias_query_ref, bias_value_ref, w_out, b_out):
    bias_query = bias_query_ref[...].astype(f32).reshape(1, WIDTH)
    bias_value = bias_value_ref[...].astype(f32).reshape(1, WIDTH)
    b_out[...] = jnp.zeros_like(b_out)
    for g in range(TP):

        @pl.when(info[0] == g)
        def _(g=g):
            cols = slice(g * GROUP_WIDTH, (g + 1) * GROUP_WIDTH)
            for kind in range(3):
                lo = kind * GROUP_WIDTH
                w_out[:, lo : lo + GROUP_WIDTH] = w_ref[:, kind * WIDTH :][:, cols]
            b_out[:, :GROUP_WIDTH] = bias_query[:, cols]
            b_out[:, 2 * GROUP_WIDTH :] = bias_value[:, cols]


def block_bias(quarter, native, random_refs, head, chunk):
    shape = (LENGTH // BLOCK, QUARTER)
    row = lax.broadcasted_iota(jnp.int32, shape, 0)
    lane_block = lax.broadcasted_iota(jnp.int32, shape, 1) // BLOCK
    key_block = ((row // TP) ^ quarter) * TP + (row % TP)
    base = TP * (quarter ^ chunk)
    query_block = base + lane_block
    last = LENGTH // BLOCK - 1
    allowed = (key_block == 0) | (key_block == last)
    allowed |= (query_block == 0) | (query_block == last)
    allowed |= jnp.abs(key_block - query_block) <= 1
    for pick in range(3):
        chosen = jnp.zeros(shape, jnp.int32)
        for b in range(TP):
            at = (head * (LENGTH // BLOCK) + base + b) * 3 + pick
            value = jnp.where(native == 1, random_refs[0][at], random_refs[1][at])
            chosen = jnp.where(lane_block == b, value, chosen)
        allowed |= key_block == chosen
    return jnp.where(allowed, 0.0, masked_score).astype(f32)


def biased(scores, bias):
    blocks = LENGTH // BLOCK
    spread = scores.reshape(blocks, BLOCK, QUARTER) + bias.reshape(blocks, 1, QUARTER)
    return spread.reshape(LENGTH, QUARTER)


PACKED = QUARTER + QUARTER // 2


def pack_heads(ref, row, pieces):
    end = row + QUARTER
    ref[row:end, 0:64] = pieces[0]
    ref[row:end, 64:128] = pieces[1]
    ref[end : row + PACKED, 0:64] = pieces[2][: QUARTER // 2]
    ref[end : row + PACKED, 64:128] = pieces[2][QUARTER // 2 :]


def unpack_heads(ref, row):
    end = row + QUARTER
    third = jnp.concatenate([ref[end : row + PACKED, 0:64], ref[end : row + PACKED, 64:128]], axis=0)
    return [ref[row:end, 0:64], ref[row:end, 64:128], third]


def attention_kernel(info, rnd_own, rnd_other, t0, t1, t2, t3, w_ref, b_ref, a0, a13, a2, *rest):
    heads, lse_ref, outs = rest[:9], rest[9], rest[10]
    ones = jnp.ones((8, LENGTH), bf16)
    quarter, native = info[0], info[4]
    for slot, t_ref in enumerate((t0, t1, t2, t3)):
        rows = pl.ds(slot * QUARTER, QUARTER)
        proj = mm(t_ref[...], w_ref[...]) + b_ref[...]
        for h in range(GROUP):
            for kind in range(3):
                lo = kind * GROUP_WIDTH + h * HEAD_DIM
                piece = proj[:, lo : lo + HEAD_DIM].astype(bf16)
                if kind == 0:
                    piece = (piece.astype(f32) * score_scale).astype(bf16)
                heads[3 * h + kind][rows, :] = piece
    for h in range(GROUP):
        q_ref, k_ref, v_ref = heads[3 * h : 3 * h + 3]
        keys = k_ref[...]
        values_t = jnp.concatenate([v_ref[...].T, ones], axis=0)

        def chunk_step(chunk, carry, h=h, q_ref=q_ref, keys=keys, values_t=values_t):
            rows = pl.ds(pl.multiple_of(chunk * QUARTER, QUARTER), QUARTER)
            scores = mm_nt(keys, q_ref[rows, :])
            head = quarter * GROUP + h
            scores = biased(scores, block_bias(quarter, native, (rnd_own, rnd_other), head, chunk))
            row_max = jnp.max(scores, axis=0, keepdims=True)
            probs = jnp.exp(scores - row_max)
            out_t = mm(values_t, probs.astype(bf16))
            row_sum = out_t[HEAD_DIM : HEAD_DIM + 1]
            out_t = out_t[:HEAD_DIM] / row_sum
            outs[h, rows, :] = out_t.T.astype(bf16)
            lse_ref[pl.ds(h * TP + chunk, 1), :] = row_max + jnp.log(row_sum)
            return carry

        lax.fori_loop(0, TP, chunk_step, 0, unroll=True)
    for slot, (a_ref, row) in enumerate(((a0, 0), (a13, 0), (a2, 0), (a13, PACKED))):
        rows = slice(slot * QUARTER, (slot + 1) * QUARTER)
        pack_heads(a_ref, row, [outs[h, rows, :] for h in range(GROUP)])


def attention_back_kernel(
    h, info, rnd_own, rnd_other, q_ref, k_ref, v_ref, lse_ref, g0, g1, g2, g3, out_ref, sums_ref, do_scr, dk_scr, dv_scr, dq_scr
):
    quarter, native = info[0], info[4]
    for slot, g_ref in enumerate((g0, g1, g2, g3)):
        do_scr[slot * QUARTER : (slot + 1) * QUARTER, :] = unpack_heads(g_ref, 0)[h]
    keys = k_ref[...]
    keys_t = keys.T
    values = v_ref[...]
    dk_scr[...] = jnp.zeros_like(dk_scr)
    dv_scr[...] = jnp.zeros_like(dv_scr)

    def chunk_step(chunk, carry):
        rows = pl.ds(pl.multiple_of(chunk * QUARTER, QUARTER), QUARTER)
        queries = q_ref[rows, :]
        grad_out = do_scr[rows, :]
        scores = mm_nt(keys, queries)
        head = quarter * GROUP + h
        bias = block_bias(quarter, native, (rnd_own, rnd_other), head, chunk)
        probs = jnp.exp(biased(scores, bias - lse_ref[pl.ds(h * TP + chunk, 1), :]))
        grad_probs = mm_nt(values, grad_out)
        delta = jnp.sum(probs * grad_probs, axis=0, keepdims=True)
        grad_scores = (probs * (grad_probs - delta)).astype(bf16)
        dv_scr[...] += mm(probs.astype(bf16), grad_out)
        dk_scr[...] += mm(grad_scores, queries)
        dq_t = mm(keys_t, grad_scores) * score_scale
        dq_scr[rows, :] = dq_t.T
        return carry

    lax.fori_loop(0, TP, chunk_step, 0, unroll=True)
    for n, scr in enumerate((dq_scr, dk_scr, dv_scr)):
        out_ref[:, n * HEAD_DIM : (n + 1) * HEAD_DIM] = scr[...].astype(bf16)
    sums_ref[...] = jnp.zeros_like(sums_ref)
    sums_ref[0:1, :] = jnp.sum(out_ref[...].astype(f32), axis=0, keepdims=True)


PIECE = 2 * SLICE + VEC_ROWS
ROOT = 0.7978845608028654
CUBE = 0.044715 * ROOT


def held_kernel(own, by_x, by_y, third, third_x, third_y, out):
    for q in range(2):
        for p, ref in enumerate((own, by_x, by_y)):
            at = (4 * q + p) * PIECE
            out[at : at + PIECE] = ref[q * PIECE : (q + 1) * PIECE]
        at = (4 * q + 3) * PIECE
        out[at : at + CUT] = third_y[PIECE + q * CUT : PIECE + (q + 1) * CUT]
        out[at + CUT : at + PIECE] = third_x[PIECE + q * (PIECE - CUT) : PIECE + (q + 1) * (PIECE - CUT)]
    for p, ref in enumerate((third, third_x, third_y)):
        at = (8 + p) * PIECE
        out[at : at + PIECE] = ref[:PIECE]


def assemble_kernel(info, held, other, last_in, last_back, other_last, w_out_ref, w_in_s, w_back_s, w_out_s, bias_s):
    quarter, mine = info[0], info[1]
    for slot in range(TP):
        start = pl.multiple_of((quarter ^ slot) * GROUP_WIDTH, GROUP_WIDTH)
        w_out_s[slot * GROUP_WIDTH : (slot + 1) * GROUP_WIDTH, :] = w_out_ref[pl.ds(start, GROUP_WIDTH), :]
    for side, main in enumerate((held, other)):
        for q in range(TP - 1):
            for p in range(4):
                start = pl.multiple_of((mine ^ PLANE_MASKS[p] ^ side) * SLICE, SLICE)
                at = (4 * q + p) * PIECE
                if q == TP - 2 and p == 3:
                    left = other_last[:SLICE] if side else last_in[...]
                    right = other_last[SLICE : 2 * SLICE] if side else last_back[:SLICE]
                else:
                    left, right = main[at : at + SLICE], main[at + SLICE : at + 2 * SLICE]
                w_in_s[q, pl.ds(start, SLICE), :] = left
                w_back_s[q, pl.ds(start, SLICE), :] = right
                if p == 0 and side == 0:
                    bias_s[q] = main[at + 2 * SLICE : at + PIECE]


def wait_all(copies):
    for copy in copies:
        copy.wait()


def row(ref):
    return ref[...].astype(f32).reshape(1, WIDTH)


def spread(h):
    centred = h - jnp.mean(h, axis=-1, keepdims=True)
    scale = lax.rsqrt(jnp.mean(centred * centred, axis=-1, keepdims=True) + epsilon)
    return centred * scale, scale


def spread_back(grad, gain, normal, scale):
    weighted = grad * gain
    mean_one = jnp.mean(weighted, axis=-1, keepdims=True)
    mean_two = jnp.mean(weighted * normal, axis=-1, keepdims=True)
    return scale * (weighted - mean_one - normal * mean_two)


def ffn_kernel(info, t_ref, a0, a1, a2, a3, *rest):
    bias_out_ref, gain_one_ref, shift_one_ref, bias_back_ref, gain_two_ref, shift_two_ref, bias_in_ref = rest[:7]
    cot_ref, w_out_s, w_in_ref, w_back_ref, w_in_s, w_back_s, bias_s = rest[7:14]
    lo_ref, first_ref, second_ref, x_ref, gb_ref, act_ref, gp_ref, att_ref, vec_ref = rest[14:]
    for slot, a_ref in enumerate((a0, a1, a2, a3)):
        for h, piece in enumerate(unpack_heads(a_ref, 0)):
            lo = slot * GROUP_WIDTH + h * HEAD_DIM
            att_ref[:, lo : lo + HEAD_DIM] = piece
    first_in = t_ref[...].astype(f32) + (mm(att_ref[...], w_out_s[...]) + row(bias_out_ref))
    first_ref[...] = first_in
    first_norm = spread(first_in)[0] * row(gain_one_ref) + row(shift_one_ref)
    x = first_norm.astype(bf16)
    x_ref[...] = x
    branch = jnp.zeros((QUARTER, WIDTH), f32)
    for q in range(TP):
        cols = slice(q * WIDTH, (q + 1) * WIDTH)
        bias_q = bias_s[q - 1, 0:1, :].astype(f32) if q else row(bias_in_ref)
        pre = mm(x, w_in_s[q - 1] if q else w_in_ref[...]) + bias_q
        square = pre * pre
        half = 0.5 + 0.5 * jnp.tanh(pre * (ROOT + CUBE * square))
        wide_act = pre * half
        act = wide_act.astype(bf16)
        act_ref[:, cols] = act
        gp_ref[:, cols] = half + wide_act * (1.0 - half) * (2.0 * ROOT + 6.0 * CUBE * square)
        branch = branch + (mm_nt(act, w_back_s[q - 1]) if q else mm(act, w_back_ref[...]))
    second_in = first_norm + branch + row(bias_back_ref)
    normal_two, scale_two = spread(second_in)
    lo_ref[...] = (normal_two * row(gain_two_ref) + row(shift_two_ref)).astype(bf16)
    grad_out = cot_ref[...].astype(f32)
    grad_second = spread_back(grad_out, row(gain_two_ref), normal_two, scale_two)
    second_ref[...] = grad_second
    grad_branch = grad_second.astype(bf16)
    gb_ref[...] = grad_branch
    vec_ref[...] = jnp.zeros_like(vec_ref)
    vec_ref[0:1, :] = jnp.sum(grad_out, axis=0, keepdims=True)
    vec_ref[1:2, :] = jnp.sum(grad_out * normal_two, axis=0, keepdims=True)
    vec_ref[2:3, :] = jnp.sum(grad_branch.astype(f32), axis=0, keepdims=True)


def position_mask(position, order):
    mask = 0
    for n, bit in enumerate(order):
        if (position >> (2 - n)) & 1:
            mask |= bit
    return mask


FFN_ORDERS = ((CORE, X_BIT, Y_BIT), (CORE, Y_BIT, X_BIT))


def weight_grads(info, left, right, keep, send, flip_scr, lhs_scr):
    mine = info[1]
    flip_scr[...] = left[...].T
    for n, order in enumerate(FFN_ORDERS):
        for p in range(SLOTS):
            start = pl.multiple_of((mine ^ position_mask(p, order)) * SLICE, SLICE)
            lhs_scr[p * SLICE : (p + 1) * SLICE, :] = flip_scr[pl.ds(start, SLICE), :]
        for pair in range(2):
            q = 2 * n + pair
            product = mm(lhs_scr[...], right[:, q * WIDTH : (q + 1) * WIDTH]).astype(bf16)
            for p in range(SLOTS):
                out = send if p >= SLOTS // 2 else keep
                out[n, p % (SLOTS // 2), pair] = product[p * SLICE : (p + 1) * SLICE, :]


def ffn_back_kernel(info, first_ref, second_ref, gb_ref, gp_ref, gain_one_ref, vec_in, *rest):
    w_out_s, w_in_ref, w_back_ref, w_in_s, w_back_s, x_ref, att_ref = rest[:7]
    g0, g13, g2, gin_ref, vec_ref, keep, send, go_keep, go_send = rest[7:16]
    gpre_ref, flip_scr, lhs_scr = rest[16:]
    grad_branch = gb_ref[...]
    grad_first = second_ref[...]
    vec_ref[...] = vec_in[...]
    for q in range(TP):
        cols = slice(q * WIDTH, (q + 1) * WIDTH)
        grad_act = mm(grad_branch, w_back_s[q - 1]) if q else mm_nt(grad_branch, w_back_ref[...])
        grad_pre = (grad_act * gp_ref[:, cols]).astype(bf16)
        gpre_ref[:, cols] = grad_pre
        vec_ref[pl.ds(6 + (info[2] ^ q), 1), :] = jnp.sum(grad_pre.astype(f32), axis=0, keepdims=True)
        grad_first = grad_first + mm_nt(grad_pre, w_in_s[q - 1] if q else w_in_ref[...])
    normal_one, scale_one = spread(first_ref[...])
    vec_ref[3:4, :] = jnp.sum(grad_first, axis=0, keepdims=True)
    vec_ref[4:5, :] = jnp.sum(grad_first * normal_one, axis=0, keepdims=True)
    grad_in = spread_back(grad_first, row(gain_one_ref), normal_one, scale_one)
    gin_ref[...] = grad_in
    grad_mixed = grad_in.astype(bf16)
    vec_ref[5:6, :] = jnp.sum(grad_mixed.astype(f32), axis=0, keepdims=True)
    grad_att = mm_nt(grad_mixed, w_out_s[...]).astype(bf16)
    for slot, (g_ref, row_at) in enumerate(((g0, 0), (g13, 0), (g2, 0), (g13, PACKED))):
        lo = slot * GROUP_WIDTH
        pack_heads(
            g_ref, row_at, [grad_att[:, lo + h * HEAD_DIM : lo + (h + 1) * HEAD_DIM] for h in range(GROUP)]
        )
    weight_grads(info, x_ref, gpre_ref, keep, send, flip_scr, lhs_scr)
    product = mm(grad_mixed.T, att_ref[...]).astype(bf16)
    go_keep[...] = product[:, : 2 * GROUP_WIDTH]
    go_send[...] = product[:, 2 * GROUP_WIDTH :]


ORDER_LA = (4, 2, 1)
ORDER_LB = (2, 4, 1)


HALF = WIDTH // 2
HELD = SLOTS // 2 * SLICE


def flip_kernel(t0, t1, t2, t3, out_ref):
    for slot, t_ref in enumerate((t0, t1, t2, t3)):
        out_ref[:, slot * QUARTER : (slot + 1) * QUARTER] = t_ref[...].T


def qkv_grad_kernel(
    info, tokens_t, gh0, gh1, gh2, go_own, go_near, vec_ref, s0, s1, s2, la_keep, la_send, lb_keep, lb_send, out_scr
):
    quarter, here = info[0], info[3]
    for h, gh_ref in enumerate((gh0, gh1, gh2)):
        product = mm(tokens_t[...], gh_ref[...]).astype(bf16)
        for kind in range(3):
            lo = kind * GROUP_WIDTH + h * HEAD_DIM
            out_scr[:, lo : lo + HEAD_DIM] = product[:, kind * HEAD_DIM : (kind + 1) * HEAD_DIM]
    add_to(out_scr.at[:, 3 * GROUP_WIDTH :], go_own[...], go_near[...])
    for keep, send, order, lo in (
        (la_keep, la_send, ORDER_LA, 0),
        (lb_keep, lb_send, ORDER_LB, HALF),
    ):
        for p in range(SLOTS):
            start = pl.multiple_of((here ^ position_mask(p, order)) * SLICE, SLICE)
            out = send if p >= SLOTS // 2 else keep
            row = p % (SLOTS // 2) * SLICE
            out[row : row + SLICE, :] = out_scr[pl.ds(start, SLICE), lo : lo + HALF]
    placed = []
    for kind in (0, 2):
        cols = slice(kind * HEAD_DIM, (kind + 1) * HEAD_DIM)
        piece = jnp.concatenate([sums[0:1, cols] for sums in (s0, s1, s2)], axis=1)
        placed.append(
            jnp.concatenate([jnp.where(quarter == g, piece, 0.0) for g in range(TP)], axis=1)
        )
    vectors = jnp.concatenate([vec_ref[0:10, :]] + placed + [vec_ref[12:VEC_ROWS, :]], axis=0)
    vectors = vectors.astype(bf16)
    for out in (la_keep, la_send, lb_keep, lb_send):
        out[HELD : HELD + VEC_ROWS, :] = vectors[:, :HALF]
        out[HELD + VEC_ROWS :, :] = vectors[:, HALF:]


def token_grad_kernel(gh0, gh1, gh2, w_ref, keep_ref, send_ref, all_scr):
    for h, gh_ref in enumerate((gh0, gh1, gh2)):
        for kind in range(3):
            lo = kind * GROUP_WIDTH + h * HEAD_DIM
            all_scr[:, lo : lo + HEAD_DIM] = gh_ref[:, kind * HEAD_DIM : (kind + 1) * HEAD_DIM]
    half = LENGTH // 2
    send_ref[...] = mm_nt(all_scr[half:, :], w_ref[...]).astype(bf16)
    keep_ref[...] = mm_nt(all_scr[:half, :], w_ref[...]).astype(bf16)


FFN_AT = 16 * SLICE + VEC_ROWS
HALF_GROUPS = TP // 2 * GROUP_WIDTH


def write_half(info, side, plane, qkv_hbm, out_hbm, w_in_hbm, qkv_scr, out_scr, w_in_scr, sems):
    quarter, mine, here = info[0], info[1], info[3]
    core = (quarter >> 1) ^ side
    first_col = core * HALF_GROUPS
    copies = []

    def send(source, target):
        copies.append(pltpu.make_async_copy(source, target, sems.at[len(copies)]))
        copies[-1].start()

    def piece(at, cols):
        block_off = here ^ at
        xy = ((block_off >> 2) & 1) + (block_off & 2)
        parts = []
        for group in range(2):
            nth = xy * 4 + ((quarter & 1) ^ group) + 2 * (block_off & 1)
            parts.append(plane[pl.ds(pl.multiple_of(nth * SLICE, SLICE), SLICE), cols])
        return jnp.concatenate(parts, axis=1).astype(f32)

    for chunk in range(SLOTS // 2):
        rows = pl.ds(2 * chunk * SLICE, 2 * SLICE)
        for kind in range(3):
            cols = pl.ds(kind * HALF_GROUPS, HALF_GROUPS)
            for at in (2 * chunk, 2 * chunk + 1):
                qkv_scr[at * SLICE : (at + 1) * SLICE, kind * HALF_GROUPS : (kind + 1) * HALF_GROUPS] = piece(
                    at, slice(kind * GROUP_WIDTH, (kind + 1) * GROUP_WIDTH)
                )
            to = pl.ds(pl.multiple_of(kind * WIDTH + first_col, 128), HALF_GROUPS)
            send(qkv_scr.at[rows, cols], qkv_hbm.at[rows, to])
        at = 2 * chunk + core
        mask = mine ^ at
        nth = (((mask >> 1) & 1) + ((mask >> 2) & 1) * 2) * 2
        start = pl.multiple_of(FFN_AT + nth * SLICE, VEC_ROWS)
        here_rows = pl.ds(chunk * SLICE, SLICE)
        w_in_scr[here_rows, :] = plane[pl.ds(start, SLICE), :].astype(f32)
        send(w_in_scr.at[here_rows, :], w_in_hbm.at[pl.ds(pl.multiple_of(at * SLICE, SLICE), SLICE), :])
    cols = slice(3 * GROUP_WIDTH, 4 * GROUP_WIDTH)
    out_scr[...] = jnp.concatenate([piece(at, cols) for at in range(SLOTS)], axis=0).T
    send(out_scr, out_hbm.at[pl.ds(pl.multiple_of(first_col, HALF_GROUPS), HALF_GROUPS), :])
    return copies


def first_half_kernel(info, plane, low_tokens, low_out, qkv_hbm, out_hbm, w_in_hbm, layer_out, token_out, *scratch):
    whole = [
        pltpu.make_async_copy(low_out, layer_out, scratch[4].at[0]),
        pltpu.make_async_copy(low_tokens, token_out, scratch[4].at[1]),
    ]
    for copy in whole:
        copy.start()
    wait_all(write_half(info, 0, plane, qkv_hbm, out_hbm, w_in_hbm, *scratch[:4]) + whole)


def second_half_kernel(info, plane, other, _qkv, _out, _w_in, qkv_hbm, out_hbm, w_in_hbm, w_back_hbm, *rest):
    vec_outs, scratch = rest[:9], rest[9:]
    mine, z_here = info[1], info[2]
    flip_scr, back_scr, sem = scratch[4:]
    for core in range(2):

        @pl.when((mine & 1) == core)
        def _(core=core):
            for at in range(SLOTS):
                mask = mine ^ at
                nth = (((mask >> 1) & 1) + ((mask >> 2) & 1) * 2) * 2 + 1
                start = pl.multiple_of(FFN_AT + nth * SLICE, VEC_ROWS)
                ref = plane if (at & 1) == core else other
                flip_scr[at * SLICE : (at + 1) * SLICE, :] = ref[pl.ds(start, SLICE), :].astype(f32)

    back_scr[...] = flip_scr[...].T
    back_copy = pltpu.make_async_copy(back_scr, w_back_hbm, sem)
    back_copy.start()
    copies = write_half(info, 1, other, qkv_hbm, out_hbm, w_in_hbm, *scratch[:4])
    vec_rows = slice(16 * SLICE, FFN_AT)
    vectors = total(plane[vec_rows, :], other[vec_rows, :])
    bias_in = jnp.zeros((1, WIDTH), f32)
    for q in range(TP):
        bias_in = jnp.where(z_here == q, vectors[6 + q : 7 + q, :], bias_in)
    for out, n in zip(vec_outs[:8], (0, 1, 2, 3, 4, 5, 10, 11)):
        out[...] = vectors[n]
    vec_outs[8][...] = bias_in[0]
    wait_all(copies + [back_copy])


def add_to(out, *terms):
    out[...] = add_low(*terms)


def join_kernel(*refs):
    out, at = refs[-1], 0
    for ref in refs[:-1]:
        out[at : at + ref.shape[0]] = ref[...]
        at += ref.shape[0]


def diag_kernel(by_x, by_y, first, second):
    half = first.shape[0]
    first[...] = by_x[:half]
    second[...] = by_y[half:]


CUT = SLICE


def mix_kernel(by_x, by_y, own, to_x, to_y):
    to_x[:PIECE] = own[...]
    to_y[:PIECE] = own[...]
    for n in range(2):
        to_x[PIECE + n * (PIECE - CUT) : PIECE + (n + 1) * (PIECE - CUT)] = by_y[n * PIECE + CUT : (n + 1) * PIECE]
        to_y[PIECE + n * CUT : PIECE + (n + 1) * CUT] = by_x[n * PIECE : n * PIECE + CUT]


def last_mix_kernel(by_x, by_y, to_x, to_y):
    to_x[...] = by_y[CUT:PIECE]
    to_y[...] = by_x[:CUT]


def level_one_kernel(keep, other, first, second):
    add_to(first, keep[0, 2:], other[0, 2:])
    add_to(second, keep[1, 2:], other[1, 2:])


def middle_kernel(in_keep, in_other, back_keep, back_other, back_x, back_y, to_x, to_y):
    for n in range(2):
        out = to_y if n else to_x
        for p in range(2):
            for pair in range(2):
                add_to(out.at[2 * p + pair], in_keep[n, 2 + p, pair], in_other[n, 2 + p, pair])
    for pair in range(2):
        add_to(to_y.at[4 + pair], back_keep[0, 1, pair], back_other[0, 1, pair], back_x[1, pair])
        add_to(to_x.at[4 + pair], back_keep[1, 1, pair], back_other[1, 1, pair], back_y[1, pair])


def in_two_kernel(keep, other, by_x, by_y, first, second):
    for pair in range(2):
        add_to(first.at[pair], keep[0, 1, pair], other[0, 1, pair], by_x[2 + pair])
        add_to(second.at[pair], keep[1, 1, pair], other[1, 1, pair], by_y[2 + pair])


def in_plane_kernel(keep, other, by_x, by_y, by_xy, by_yx, near, kept):
    for q in range(TP):
        order, pair = q // 2, q % 2
        first, second = (by_x, by_xy) if order == 0 else (by_y, by_yx)
        out = near if q % 2 else kept
        add_to(out.at[q // 2], keep[order, 0, pair], other[order, 0, pair], first[pair], second[pair])


def back_plane_kernel(keep, other, by_x, by_y, mid_x, mid_y, near, kept):
    for q in range(TP):
        order, pair = q // 2, q % 2
        first, second = (by_x, mid_y) if order == 0 else (by_y, mid_x)
        out = near if q % 2 else kept
        add_to(out.at[q // 2], keep[order, 0, pair], other[order, 0, pair], first[0, pair], second[4 + pair])


def far_kernel(kept, near, far):
    add_to(far, kept[1], near[1])


def last_kernel(kept_a, near_a, far_a, kept_b, near_b, far_b, out):
    add_to(out.at[0], kept_a[0], near_a[0], far_a[...])
    add_to(out.at[1], kept_b[0], near_b[0], far_b[...])


def go_kernel(keep, other, own, send):
    add_to(own, keep[:, :GROUP_WIDTH], other[:, :GROUP_WIDTH])
    add_to(send, keep[:, GROUP_WIDTH:], other[:, GROUP_WIDTH:])


def near_kernel(keep, other, out):
    add_to(out, keep[QUARTER:], other[QUARTER:])


def tokens_kernel(keep, other, near, grad_in, out_here, tokens, again):
    add_to(tokens, keep[:QUARTER], other[:QUARTER], near[...], grad_in[...])
    again[...] = out_here[...]


TWO = 2 * SLICE


def qkv_two_kernel(la, ra, lb, rb, la_out, lb_out):
    add_to(la_out, la[TWO:], ra[TWO:])
    add_to(lb_out, lb[TWO:HELD], rb[TWO:HELD])


def qkv_three_kernel(la, ra, ra2, lb, rb, rb2, out):
    add_to(out.at[:TWO, :HALF], la[:TWO], ra[:TWO], ra2[:TWO])
    add_to(out.at[:TWO, HALF:], lb[:TWO], rb[:TWO], rb2[...])
    for n in range(2):
        rows = slice(HELD + n * VEC_ROWS, HELD + (n + 1) * VEC_ROWS)
        rows_two = slice(TWO + n * VEC_ROWS, TWO + (n + 1) * VEC_ROWS)
        add_to(out.at[TWO:, n * HALF : (n + 1) * HALF], la[rows], ra[rows], ra2[rows_two])


def qkv_four_kernel(own, other, out):
    add_to(out.at[:SLICE], own[:SLICE], other[SLICE:TWO])
    add_to(out.at[SLICE:TWO], own[SLICE:TWO], other[:SLICE])
    add_to(out.at[TWO:], own[TWO:], other[TWO:])


def mix_l_kernel(by_x, by_y, other, to_x, to_y):
    to_x[:TWO] = other[:TWO]
    to_x[TWO:] = by_y[SLICE:TWO]
    to_y[:TWO] = other[:TWO]
    to_y[TWO:] = by_x[:SLICE]


def diag_kernel(l_x, l_y, f_x, f_y, to_x, to_y):
    to_x[:SLICE] = l_y[SLICE:TWO]
    to_x[SLICE:] = f_y[1]
    to_y[:SLICE] = l_x[:SLICE]
    to_y[SLICE:] = f_x[0]


def plane_l_kernel(own, other, x_own, y_own, x_other, y_other, f_own, f_x, f_y, d_x, d_y, out):
    diag_own = (y_other[TWO:], x_other[TWO:])
    diag_other = (d_y[:SLICE], d_x[:SLICE])
    places = (
        ((own[:SLICE], own[SLICE:TWO]), (other[:SLICE], other[SLICE:TWO])),
        ((x_own[:SLICE], x_own[SLICE:TWO]), (x_other[:SLICE], x_other[SLICE:TWO])),
        ((y_own[:SLICE], y_own[SLICE:TWO]), (y_other[:SLICE], y_other[SLICE:TWO])),
        (diag_own, diag_other),
    )
    for p, (here, there) in enumerate(places):
        for slot in range(TP):
            at = (p * TP + slot) * SLICE
            out[at : at + SLICE] = (there if slot % 2 else here)[slot // 2]
    add_to(out.at[16 * SLICE : FFN_AT], own[TWO:], other[TWO:])
    for n, (left, right) in enumerate(
        ((f_own[0], f_own[1]), (f_x[0], f_x[1]), (f_y[0], f_y[1]), (d_y[SLICE:], d_x[SLICE:]))
    ):
        out[FFN_AT + 2 * n * SLICE : FFN_AT + (2 * n + 1) * SLICE] = left
        out[FFN_AT + (2 * n + 1) * SLICE : FFN_AT + (2 * n + 2) * SLICE] = right


VMEM = pl.BlockSpec(memory_space=pltpu.VMEM)
SMEM = pl.BlockSpec(memory_space=pltpu.SMEM)
HBM = pl.BlockSpec(memory_space=pl.ANY)


def call(kernel, in_specs, outs, scratch, vmem_mib, name, deps=()):
    count, extra = len(in_specs), len(deps)

    def body(*refs):
        kernel(*refs[:count], *refs[count + extra :])

    run = pl.pallas_call(
        body,
        out_shape=[jax.ShapeDtypeStruct(shape, dtype) for shape, dtype in outs],
        in_specs=list(in_specs) + [HBM] * extra,
        out_specs=[VMEM] * len(outs),
        scratch_shapes=scratch,
        compiler_params=pltpu.CompilerParams(vmem_limit_bytes=vmem_mib * 1024 * 1024),
        cost_estimate=pl.CostEstimate(flops=1, bytes_accessed=1, transcendentals=0),
        name=name,
    )
    return lambda *arrays: run(*arrays, *deps)


def step(kernel, name, outs, *arrays, deps=()):
    shapes = [(shape, bf16) for shape in outs]
    result = call(kernel, [VMEM] * len(arrays), shapes, [], 12, name, deps)(*arrays)
    return result[0] if len(outs) == 1 else result


def per_device(
    tokens,
    w_qkv,
    bias_query,
    bias_value,
    w_out,
    bias_out,
    gain_attn,
    shift_attn,
    w_in,
    bias_in,
    w_back,
    bias_back,
    gain_ffn,
    shift_ffn,
    random_blocks,
    cotangent,
):
    dp_count = lax.axis_size("dp")
    d = lax.axis_index("dp")
    z = lax.axis_index("tp")
    core = d & 1
    quarter = (z & 1) + 2 * core
    mine = d & (SLOTS - 1)
    here = ((d >> 1) & 1) * 4 + ((d >> 2) & 1) * 2 + (z >> 1)
    native = (core == z // 2).astype(jnp.int32)
    info = jnp.stack([quarter, mine, z, here, native]).astype(jnp.int32)
    extra_bits = [1 << b for b in range(3, dp_count.bit_length() - 1)]

    own_tokens = place(tokens[0])
    piece = call(
        piece_kernel,
        [SMEM, HBM, VMEM, VMEM],
        [((2 * SLICE + VEC_ROWS, WIDTH), bf16)],
        [pltpu.VMEM((WIDTH, WIDTH), bf16), pltpu.SemaphoreType.DMA],
        8,
        "piece",
    )(info, w_in, w_back, bias_in)[0]
    piece_one = hop(piece, 0, 1)
    piece_two = hop(piece, 0, 2)
    random_own = random_blocks.reshape(-1)
    random_other = hop(random_own, CORE, 0)
    w_group, bias_group = call(
        group_kernel,
        [SMEM, VMEM, VMEM, VMEM],
        [((WIDTH, 3 * GROUP_WIDTH), bf16), ((1, 3 * GROUP_WIDTH), f32)],
        [],
        16,
        "group",
    )(info, w_qkv, bias_query, bias_value)
    near_tokens = hop(own_tokens, 0, 1)
    core_tokens = hop(own_tokens, CORE, 0)
    far_tokens = hop(near_tokens, CORE, 0)
    part_one = step(
        join_kernel, "pair", [(2 * PIECE, WIDTH)], piece_one, piece_two, deps=(own_tokens, w_group, random_other)
    )
    x_one = hop(part_one, X_BIT, 0)
    y_one = hop(part_one, Y_BIT, 0)
    piece_three = hop(piece_two, 0, 1)
    cot = place(cotangent[0])
    to_x, to_y = step(
        mix_kernel,
        "mix",
        [(3 * PIECE - 2 * CUT, WIDTH), (PIECE + 2 * CUT, WIDTH)],
        x_one,
        y_one,
        piece_three,
        deps=(near_tokens,),
    )
    x_three = hop(to_x, X_BIT, 0)
    y_three = hop(to_y, Y_BIT, 0)

    packed = ((PACKED, 2 * HEAD_DIM), bf16)
    double = ((2 * PACKED, 2 * HEAD_DIM), bf16)
    per_head = ((LENGTH, HEAD_DIM), bf16)
    token_slots = (own_tokens, near_tokens, core_tokens, far_tokens)
    a0, a13, a2, *heads = call(
        attention_kernel,
        [SMEM] * 3 + [VMEM] * 6,
        [packed, double, packed] + [per_head] * 9 + [((16, QUARTER), f32)],
        [pltpu.VMEM((GROUP, LENGTH, HEAD_DIM), bf16)],
        24,
        "attention",
        (to_x, core_tokens),
    )(info, random_own, random_other, *token_slots, w_group, bias_group)
    heads, lse = heads[:9], heads[9]
    a1 = hop(a13, 0, 1)
    a2 = hop(a2, CORE, 0)
    a3 = hop(a1[PACKED:], CORE, 0)
    to_x, to_y = step(
        last_mix_kernel,
        "mix_last",
        [(PIECE - CUT, WIDTH), (CUT, WIDTH)],
        x_three,
        y_three,
        deps=(a0, cot),
    )
    last_back = hop(to_x, X_BIT, 0)
    last_in = hop(to_y, Y_BIT, 0)
    held = step(
        held_kernel,
        "held",
        [(11 * PIECE, WIDTH)],
        part_one,
        x_one,
        y_one,
        piece_three,
        x_three,
        y_three,
        deps=(a2, cot),
    )
    tokens_t = call(flip_kernel, [VMEM] * 4, [((WIDTH, LENGTH), bf16)], [], 8, "flip_tokens", (a1, held))(
        *token_slots
    )[0]
    last = step(join_kernel, "last_piece", [(PIECE, WIDTH)], last_in, last_back, deps=(tokens_t,))
    quarters = ((TP - 1, WIDTH, WIDTH), bf16)
    w_in_s, w_back_s, w_out_s, bias_s = call(
        assemble_kernel,
        [SMEM] + [VMEM] * 6,
        [quarters, quarters, ((WIDTH, WIDTH), bf16), ((TP - 1, VEC_ROWS, WIDTH), bf16)],
        [],
        20,
        "assemble",
    )(info, held, hop(held, CORE, 0), last_in, last_back, hop(last, CORE, 0), w_out)

    rows = ((QUARTER, WIDTH), bf16)
    wide = ((QUARTER, TP * WIDTH), bf16)
    rows_f32 = ((QUARTER, WIDTH), f32)
    vec_rows = ((VEC_ROWS, WIDTH), f32)
    out_here, first_in, grad_second, ffn_input, grad_branch, activated, gelu_slope, attended, vectors = call(
        ffn_kernel,
        [SMEM] + [VMEM] * 19,
        [rows, rows_f32, rows_f32, rows, rows, wide, ((QUARTER, TP * WIDTH), f32), rows, vec_rows],
        [],
        20,
        "ffn",
        (tokens_t,),
    )(
        info,
        own_tokens,
        a0,
        a1,
        a2,
        a3,
        bias_out,
        gain_attn,
        shift_attn,
        bias_back,
        gain_ffn,
        shift_ffn,
        bias_in,
        cot,
        w_out_s,
        w_in,
        w_back,
        w_in_s,
        w_back_s,
        bias_s,
    )
    pairs = ((2, SLOTS // 2, 2, SLICE, WIDTH), bf16)
    halves = ((WIDTH, 2 * GROUP_WIDTH), bf16)
    flips = [pltpu.VMEM((WIDTH, QUARTER), bf16), pltpu.VMEM((WIDTH, QUARTER), bf16)]
    back_keep, back_send = call(
        weight_grads, [SMEM] + [VMEM] * 2, [pairs] * 2, flips, 12, "back_grads"
    )(info, grad_branch, activated)
    back_other = hop(back_send, CORE, 0)

    g0, g13, g2, grad_in, vectors, in_keep, in_send, go_keep, go_send = call(
        ffn_back_kernel,
        [SMEM] + [VMEM] * 13,
        [packed, double, packed, rows_f32, vec_rows] + [pairs] * 2 + [halves] * 2,
        [pltpu.VMEM((QUARTER, TP * WIDTH), bf16)] + flips,
        20,
        "ffn_back",
        (back_keep,),
    )(
        info,
        first_in,
        grad_second,
        grad_branch,
        gelu_slope,
        gain_attn,
        vectors,
        w_out_s,
        w_in,
        w_back,
        w_in_s,
        w_back_s,
        ffn_input,
        attended,
    )
    g1 = hop(g13, 0, 1)
    g2 = hop(g2, CORE, 0)
    g3 = hop(g1[PACKED:], CORE, 0)

    first_level = [(2, 2, SLICE, WIDTH)] * 2
    def hop_pair(pair, first, second):
        return hop(pair[0], first, 0), hop(pair[1], second, 0)

    back_sums = step(level_one_kernel, "back_one", first_level, back_keep, back_other, deps=(g13,))
    back_x, back_y = hop_pair(back_sums, X_BIT, Y_BIT)
    in_other = hop(in_send, CORE, 0)
    go_other = hop(go_send, CORE, 0)

    def head_back(h, deps):
        return call(
            functools.partial(attention_back_kernel, h),
            [SMEM] * 3 + [VMEM] * 8,
            [((LENGTH, 3 * HEAD_DIM), bf16), ((8, 3 * HEAD_DIM), f32)],
            [
                pltpu.VMEM((LENGTH, HEAD_DIM), bf16),
                pltpu.VMEM((LENGTH, HEAD_DIM), f32),
                pltpu.VMEM((LENGTH, HEAD_DIM), f32),
                pltpu.VMEM((LENGTH, HEAD_DIM), f32),
            ],
            12,
            f"attention_back_{h}",
            deps,
        )(info, random_own, random_other, *heads[3 * h : 3 * h + 3], lse, g0, g1, g2, g3)

    go_own, go_send = step(go_kernel, "go", [(WIDTH, GROUP_WIDTH)] * 2, go_keep, go_other)
    go_near = hop(go_send, 0, 1)
    gh0, s0 = head_back(0, (go_own, back_sums[0]))
    back_parts = [back_keep, back_other, back_x, back_y]
    to_x, to_y = step(
        middle_kernel,
        "middle",
        [(6, SLICE, WIDTH)] * 2,
        in_keep,
        in_other,
        *back_parts,
        deps=(gh0,),
    )
    mid_x, mid_y = hop(to_x, X_BIT, 0), hop(to_y, Y_BIT, 0)
    in_parts = [in_keep, in_other, mid_x, mid_y]
    z_level = [(2, SLICE, WIDTH)] * 2
    gh1, s1 = head_back(1, (to_x,))
    gh2, s2 = head_back(2, (gh1,))

    la_keep, la_send, lb_keep, lb_send = call(
        qkv_grad_kernel,
        [SMEM] + [VMEM] * 10,
        [((HELD + 2 * VEC_ROWS, HALF), bf16)] * 4,
        [pltpu.VMEM((WIDTH, 4 * GROUP_WIDTH), bf16)],
        16,
        "qkv_grads",
        (gh2,),
    )(info, tokens_t, gh0, gh1, gh2, go_own, go_near, vectors, s0, s1, s2)
    ra = hop(la_send, X_BIT, 0)
    rb = hop(lb_send, Y_BIT, 0)

    keep, send = call(
        token_grad_kernel,
        [VMEM] * 4,
        [((LENGTH // 2, WIDTH), bf16)] * 2,
        [pltpu.VMEM((LENGTH, 3 * GROUP_WIDTH), bf16)],
        16,
        "token_grad",
        (la_keep,),
    )(gh0, gh1, gh2, w_group)
    other = hop(send, CORE, 0)
    near_b, kept_b = step(
        back_plane_kernel, "back_plane", z_level, *back_parts, mid_x, mid_y, deps=(keep,)
    )
    near_b = hop(near_b, 0, 1)
    sums = step(in_two_kernel, "in_two", z_level, *in_parts, deps=(kept_b,))
    in_parts += hop_pair(sums, Y_BIT, X_BIT)
    near_low = step(near_kernel, "near", [(QUARTER, WIDTH)], keep, other, deps=(sums[0],))
    near = hop(near_low, 0, 1)
    far_b = step(far_kernel, "far_back", [(SLICE, WIDTH)], kept_b, near_b, deps=(near_low,))
    far_hop_b = hop(far_b, 0, 2)
    la2, lb2 = step(
        qkv_two_kernel,
        "qkv_two",
        [(TWO + 2 * VEC_ROWS, HALF), (TWO, HALF)],
        la_keep,
        ra,
        lb_keep,
        rb,
        deps=(far_b,),
    )
    ra2 = hop(la2, Y_BIT, 0)
    rb2 = hop(lb2, X_BIT, 0)
    rows_l = (TWO + VEC_ROWS, WIDTH)
    near_a, kept_a = step(in_plane_kernel, "in_plane", z_level, *in_parts, deps=(la2,))
    near_a = hop(near_a, 0, 1)
    partial = step(
        qkv_three_kernel, "qkv_three", [rows_l], la_keep, ra, ra2, lb_keep, rb, rb2, deps=(kept_a, far_hop_b)
    )
    far_a = step(far_kernel, "far_in", [(SLICE, WIDTH)], kept_a, near_a, deps=(partial, far_hop_b))
    far_hop_a = hop(far_a, 0, 2)
    sum_l = step(
        qkv_four_kernel, "qkv_four", [rows_l], partial, hop(partial, 0, 2), deps=(far_a, near)
    )
    for bit in extra_bits:
        sum_l = add_low(sum_l, hop(sum_l, bit, 0))

    own_l = sum_l[:TWO]
    x_own = hop(own_l, X_BIT, 0)
    y_own = hop(own_l, Y_BIT, 0)
    other_l = hop(sum_l, 0, 1)
    to_x, to_y = step(
        mix_l_kernel, "mix_l", [(TWO + SLICE, WIDTH)] * 2, x_own, y_own, other_l
    )
    x_other = hop(to_x, X_BIT, 0)
    y_other = hop(to_y, Y_BIT, 0)
    sum_f = step(
        last_kernel,
        "last",
        [(2, SLICE, WIDTH)],
        kept_a,
        near_a,
        far_hop_a,
        kept_b,
        near_b,
        far_hop_b,
        deps=(to_x,),
    )
    for bit in extra_bits:
        sum_f = add_low(sum_f, hop(sum_f, bit, 0))
    low_outs = step(
        tokens_kernel,
        "tokens",
        [(QUARTER, WIDTH)] * 2,
        keep,
        other,
        near,
        grad_in,
        out_here,
        deps=(sum_f,),
    )
    token_grads, layer_out = place(low_outs[0]), place(low_outs[1])
    f_x = hop(sum_f, X_BIT, 0)
    f_y = hop(sum_f, Y_BIT, 0)
    diag = step(diag_kernel, "diag", [(TWO, WIDTH)] * 2, x_other, y_other, f_x, f_y)
    d_x, d_y = hop_pair(diag, X_BIT, Y_BIT)
    plane = step(
        plane_l_kernel,
        "plane",
        [(FFN_AT + SLOTS * SLICE, WIDTH)],
        sum_l,
        other_l,
        x_own,
        y_own,
        x_other,
        y_other,
        sum_f,
        f_x,
        f_y,
        d_x,
        d_y,
        deps=(token_grads, layer_out),
    )
    square = ((WIDTH, WIDTH), f32)
    halves_out = [((WIDTH, 3 * WIDTH), f32), square, square]
    half_scratch = [
        pltpu.VMEM((WIDTH, 3 * HALF_GROUPS), f32),
        pltpu.VMEM((HALF_GROUPS, WIDTH), f32),
        pltpu.VMEM((WIDTH // 2, WIDTH), f32),
        pltpu.SemaphoreType.DMA((2 * SLOTS + 1,)),
    ]
    as_shape = lambda outs: [jax.ShapeDtypeStruct(shape, dtype) for shape, dtype in outs]
    cheap = pl.CostEstimate(flops=1, bytes_accessed=1, transcendentals=0)
    *half_written, layer_out, grad_tokens = pl.pallas_call(
        first_half_kernel,
        out_shape=as_shape(halves_out + [rows, rows]),
        in_specs=[SMEM] + [VMEM] * 3,
        out_specs=[HBM] * 5,
        scratch_shapes=half_scratch + [pltpu.SemaphoreType.DMA((2,))],
        compiler_params=pltpu.CompilerParams(vmem_limit_bytes=16 * 1024 * 1024),
        cost_estimate=cheap,
        name="first_half",
    )(info, plane, token_grads, layer_out)
    grad_w_qkv, grad_w_out, grad_w_in, grad_w_back, *vec_outs = pl.pallas_call(
        second_half_kernel,
        out_shape=as_shape(halves_out + [square] + [((WIDTH,), f32)] * 9),
        in_specs=[SMEM, VMEM, VMEM] + [HBM] * 3,
        out_specs=[HBM] * 4 + [VMEM] * 9,
        scratch_shapes=half_scratch + [pltpu.VMEM((WIDTH, WIDTH), f32)] * 2 + [pltpu.SemaphoreType.DMA],
        input_output_aliases={3: 0, 4: 1, 5: 2},
        compiler_params=pltpu.CompilerParams(vmem_limit_bytes=24 * 1024 * 1024),
        cost_estimate=cheap,
        name="second_half",
    )(info, plane, hop(plane, CORE, 0), *half_written)
    (
        grad_shift_ffn,
        grad_gain_ffn,
        grad_bias_back,
        grad_shift_attn,
        grad_gain_attn,
        grad_bias_out,
        grad_bias_query,
        grad_bias_value,
        grad_bias_in,
    ) = vec_outs
    return (
        layer_out[None],
        grad_tokens[None],
        grad_w_qkv,
        grad_bias_query,
        grad_bias_value,
        grad_w_out,
        grad_bias_out,
        grad_gain_attn,
        grad_shift_attn,
        grad_w_in,
        grad_bias_in,
        grad_w_back,
        grad_bias_back,
        grad_gain_ffn,
        grad_shift_ffn,
    )


def solution(mesh):
    in_specs = (
        P("dp", "tp", None),
        P(),
        P(),
        P(),
        P(),
        P(),
        P(),
        P(),
        P(None, "tp"),
        P("tp"),
        P("tp", None),
        P(),
        P(),
        P(),
        P("dp", None, None, None),
        P("dp", "tp", None),
    )
    out_specs = (
        P("dp", "tp", None),
        P("dp", "tp", None),
        P(),
        P(),
        P(),
        P(),
        P(),
        P(),
        P(),
        P(None, "tp"),
        P("tp"),
        P("tp", None),
        P(),
        P(),
        P(),
    )
    return jax.shard_map(
        per_device, mesh=mesh, in_specs=in_specs, out_specs=out_specs, check_vma=False
    )
```

```python
import functools

import jax
import jax.numpy as jnp
from jax import lax
from jax.experimental import pallas as pl
from jax.experimental.pallas import tpu as pltpu
from jax.sharding import PartitionSpec as P

HEADS = 12
BLOCK = 64
HEAD_DIM = 64
TP = 4
GROUP = HEADS // TP
QUARTER = 256
LENGTH = TP * QUARTER
WIDTH = HEADS * HEAD_DIM
GROUP_WIDTH = GROUP * HEAD_DIM
SLOTS = 8
SLICE = WIDTH // SLOTS
VEC_ROWS = 16
CORE, X_BIT, Y_BIT = 1, 2, 4
PLANE_MASKS = (0, X_BIT, Y_BIT, X_BIT | Y_BIT)

epsilon = 1e-05
masked_score = -1e30
score_scale = HEAD_DIM ** (-0.5)
f32 = jnp.float32
bf16 = jnp.bfloat16


def mm(left, right):
    return jnp.dot(left, right, preferred_element_type=f32)


def mm_nt(left, right):
    return lax.dot_general(left, right, (((1,), (1,)), ((), ())), preferred_element_type=f32)


def total(*terms):
    acc = terms[0].astype(f32)
    for term in terms[1:]:
        acc = acc + term.astype(f32)
    return acc


def add_low(*terms):
    return total(*terms).astype(bf16)


def hop(array, dp_mask, z_mask):
    dp_count = lax.axis_size("dp")
    pairs = [
        (d * TP + z, (d ^ dp_mask) * TP + (z ^ z_mask)) for d in range(dp_count) for z in range(TP)
    ]
    return lax.ppermute(array, ("dp", "tp"), pairs)


def place(array):
    dp_count = lax.axis_size("dp")
    pairs = []
    for d in range(dp_count):
        for z in range(TP):
            here = d * TP + z
            away = (d ^ CORE) * TP + (z ^ 2)
            pairs.append((here, here if (d & 1) == z // 2 else away))
    return lax.ppermute(array, ("dp", "tp"), pairs)


def piece_kernel(info, w_in_hbm, w_back_ref, bias_ref, piece_ref, flip_scr, sem):
    start = pl.multiple_of(info[1] * SLICE, SLICE)
    copy = pltpu.make_async_copy(
        w_in_hbm.at[pl.ds(start, SLICE), :], piece_ref.at[pl.ds(0, SLICE), :], sem
    )
    copy.start()
    flip_scr[...] = w_back_ref[...].T
    piece_ref[SLICE : 2 * SLICE, :] = flip_scr[pl.ds(start, SLICE), :]
    bias = bias_ref[...].astype(f32).reshape(1, WIDTH)
    piece_ref[2 * SLICE :, :] = jnp.broadcast_to(bias, (VEC_ROWS, WIDTH)).astype(bf16)
    copy.wait()


def group_kernel(info, w_ref, bias_query_ref, bias_value_ref, w_out, b_out):
    bias_query = bias_query_ref[...].astype(f32).reshape(1, WIDTH)
    bias_value = bias_value_ref[...].astype(f32).reshape(1, WIDTH)
    b_out[...] = jnp.zeros_like(b_out)
    for g in range(TP):

        @pl.when(info[0] == g)
        def _(g=g):
            cols = slice(g * GROUP_WIDTH, (g + 1) * GROUP_WIDTH)
            for kind in range(3):
                lo = kind * GROUP_WIDTH
                w_out[:, lo : lo + GROUP_WIDTH] = w_ref[:, kind * WIDTH :][:, cols]
            b_out[:, :GROUP_WIDTH] = bias_query[:, cols]
            b_out[:, 2 * GROUP_WIDTH :] = bias_value[:, cols]


def block_bias(quarter, native, random_refs, head, chunk):
    shape = (LENGTH // BLOCK, QUARTER)
    row = lax.broadcasted_iota(jnp.int32, shape, 0)
    lane_block = lax.broadcasted_iota(jnp.int32, shape, 1) // BLOCK
    key_block = ((row // TP) ^ quarter) * TP + (row % TP)
    base = TP * (quarter ^ chunk)
    query_block = base + lane_block
    last = LENGTH // BLOCK - 1
    allowed = (key_block == 0) | (key_block == last)
    allowed |= (query_block == 0) | (query_block == last)
    allowed |= jnp.abs(key_block - query_block) <= 1
    for pick in range(3):
        chosen = jnp.zeros(shape, jnp.int32)
        for b in range(TP):
            at = (head * (LENGTH // BLOCK) + base + b) * 3 + pick
            value = jnp.where(native == 1, random_refs[0][at], random_refs[1][at])
            chosen = jnp.where(lane_block == b, value, chosen)
        allowed |= key_block == chosen
    return jnp.where(allowed, 0.0, masked_score).astype(f32)


def biased(scores, bias):
    blocks = LENGTH // BLOCK
    spread = scores.reshape(blocks, BLOCK, QUARTER) + bias.reshape(blocks, 1, QUARTER)
    return spread.reshape(LENGTH, QUARTER)


PACKED = QUARTER + QUARTER // 2


def pack_heads(ref, row, pieces):
    end = row + QUARTER
    ref[row:end, 0:64] = pieces[0]
    ref[row:end, 64:128] = pieces[1]
    ref[end : row + PACKED, 0:64] = pieces[2][: QUARTER // 2]
    ref[end : row + PACKED, 64:128] = pieces[2][QUARTER // 2 :]


def unpack_heads(ref, row):
    end = row + QUARTER
    third = jnp.concatenate([ref[end : row + PACKED, 0:64], ref[end : row + PACKED, 64:128]], axis=0)
    return [ref[row:end, 0:64], ref[row:end, 64:128], third]


def attention_kernel(info, rnd_own, rnd_other, t0, t1, t2, t3, w_ref, b_ref, a0, a13, a2, *rest):
    heads, lse_ref, outs = rest[:9], rest[9], rest[10]
    ones = jnp.ones((8, LENGTH), bf16)
    quarter, native = info[0], info[4]
    for slot, t_ref in enumerate((t0, t1, t2, t3)):
        rows = pl.ds(slot * QUARTER, QUARTER)
        proj = mm(t_ref[...], w_ref[...]) + b_ref[...]
        for h in range(GROUP):
            for kind in range(3):
                lo = kind * GROUP_WIDTH + h * HEAD_DIM
                piece = proj[:, lo : lo + HEAD_DIM].astype(bf16)
                if kind == 0:
                    piece = (piece.astype(f32) * score_scale).astype(bf16)
                heads[3 * h + kind][rows, :] = piece
    for h in range(GROUP):
        q_ref, k_ref, v_ref = heads[3 * h : 3 * h + 3]
        keys = k_ref[...]
        values_t = jnp.concatenate([v_ref[...].T, ones], axis=0)

        def chunk_step(chunk, carry, h=h, q_ref=q_ref, keys=keys, values_t=values_t):
            rows = pl.ds(pl.multiple_of(chunk * QUARTER, QUARTER), QUARTER)
            scores = mm_nt(keys, q_ref[rows, :])
            head = quarter * GROUP + h
            scores = biased(scores, block_bias(quarter, native, (rnd_own, rnd_other), head, chunk))
            row_max = jnp.max(scores, axis=0, keepdims=True)
            probs = jnp.exp(scores - row_max)
            out_t = mm(values_t, probs.astype(bf16))
            row_sum = out_t[HEAD_DIM : HEAD_DIM + 1]
            out_t = out_t[:HEAD_DIM] / row_sum
            outs[h, rows, :] = out_t.T.astype(bf16)
            lse_ref[pl.ds(h * TP + chunk, 1), :] = row_max + jnp.log(row_sum)
            return carry

        lax.fori_loop(0, TP, chunk_step, 0, unroll=True)
    for slot, (a_ref, row) in enumerate(((a0, 0), (a13, 0), (a2, 0), (a13, PACKED))):
        rows = slice(slot * QUARTER, (slot + 1) * QUARTER)
        pack_heads(a_ref, row, [outs[h, rows, :] for h in range(GROUP)])


def attention_back_kernel(
    h, info, rnd_own, rnd_other, q_ref, k_ref, v_ref, lse_ref, g0, g13, g2, out_ref, sums_ref, do_scr, dk_scr, dv_scr, dq_scr
):
    quarter, native = info[0], info[4]
    for slot, (g_ref, row) in enumerate(((g0, 0), (g13, 0), (g2, 0), (g13, PACKED))):
        do_scr[slot * QUARTER : (slot + 1) * QUARTER, :] = unpack_heads(g_ref, row)[h]
    keys = k_ref[...]
    keys_t = keys.T
    values = v_ref[...]
    dk_scr[...] = jnp.zeros_like(dk_scr)
    dv_scr[...] = jnp.zeros_like(dv_scr)

    def chunk_step(chunk, carry):
        rows = pl.ds(pl.multiple_of(chunk * QUARTER, QUARTER), QUARTER)
        queries = q_ref[rows, :]
        grad_out = do_scr[rows, :]
        scores = mm_nt(keys, queries)
        head = quarter * GROUP + h
        bias = block_bias(quarter, native, (rnd_own, rnd_other), head, chunk)
        probs = jnp.exp(biased(scores, bias - lse_ref[pl.ds(h * TP + chunk, 1), :]))
        grad_probs = mm_nt(values, grad_out)
        delta = jnp.sum(probs * grad_probs, axis=0, keepdims=True)
        grad_scores = (probs * (grad_probs - delta)).astype(bf16)
        dv_scr[...] += mm(probs.astype(bf16), grad_out)
        dk_scr[...] += mm(grad_scores, queries)
        dq_t = mm(keys_t, grad_scores) * score_scale
        dq_scr[rows, :] = dq_t.T
        return carry

    lax.fori_loop(0, TP, chunk_step, 0, unroll=True)
    for n, scr in enumerate((dq_scr, dk_scr, dv_scr)):
        out_ref[:, n * HEAD_DIM : (n + 1) * HEAD_DIM] = scr[...].astype(bf16)
    sums_ref[...] = jnp.zeros_like(sums_ref)
    sums_ref[0:1, :] = jnp.sum(out_ref[...].astype(f32), axis=0, keepdims=True)


PIECE = 2 * SLICE + VEC_ROWS
ROOT = 0.7978845608028654
CUBE = 0.044715 * ROOT


def held_kernel(own, by_x, by_y, third, third_x, third_y, out):
    for q in range(2):
        for p, ref in enumerate((own, by_x, by_y)):
            at = (4 * q + p) * PIECE
            out[at : at + PIECE] = ref[q * PIECE : (q + 1) * PIECE]
        at = (4 * q + 3) * PIECE
        out[at : at + CUT] = third_y[PIECE + q * CUT : PIECE + (q + 1) * CUT]
        out[at + CUT : at + PIECE] = third_x[PIECE + q * (PIECE - CUT) : PIECE + (q + 1) * (PIECE - CUT)]
    for p, ref in enumerate((third, third_x, third_y)):
        at = (8 + p) * PIECE
        out[at : at + PIECE] = ref[:PIECE]


def assemble_kernel(info, held, other, last_in, last_back, other_last, w_out_ref, w_in_s, w_back_s, w_out_s, bias_s):
    quarter, mine = info[0], info[1]
    for slot in range(TP):
        start = pl.multiple_of((quarter ^ slot) * GROUP_WIDTH, GROUP_WIDTH)
        w_out_s[slot * GROUP_WIDTH : (slot + 1) * GROUP_WIDTH, :] = w_out_ref[pl.ds(start, GROUP_WIDTH), :]
    for side, main in enumerate((held, other)):
        for q in range(TP - 1):
            for p in range(4):
                start = pl.multiple_of((mine ^ PLANE_MASKS[p] ^ side) * SLICE, SLICE)
                at = (4 * q + p) * PIECE
                if q == TP - 2 and p == 3:
                    left = other_last[:SLICE] if side else last_in[...]
                    right = other_last[SLICE : 2 * SLICE] if side else last_back[:SLICE]
                else:
                    left, right = main[at : at + SLICE], main[at + SLICE : at + 2 * SLICE]
                w_in_s[q, pl.ds(start, SLICE), :] = left
                w_back_s[q, pl.ds(start, SLICE), :] = right
                if p == 0 and side == 0:
                    bias_s[q] = main[at + 2 * SLICE : at + PIECE]


def wait_all(copies):
    for copy in copies:
        copy.wait()


def row(ref):
    return ref[...].astype(f32).reshape(1, WIDTH)


def spread(h):
    centred = h - jnp.mean(h, axis=-1, keepdims=True)
    scale = lax.rsqrt(jnp.mean(centred * centred, axis=-1, keepdims=True) + epsilon)
    return centred * scale, scale


def spread_back(grad, gain, normal, scale):
    weighted = grad * gain
    mean_one = jnp.mean(weighted, axis=-1, keepdims=True)
    mean_two = jnp.mean(weighted * normal, axis=-1, keepdims=True)
    return scale * (weighted - mean_one - normal * mean_two)


def ffn_kernel(info, t_ref, a0, a1, a2, a3, *rest):
    bias_out_ref, gain_one_ref, shift_one_ref, bias_back_ref, gain_two_ref, shift_two_ref, bias_in_ref = rest[:7]
    cot_ref, w_out_s, w_in_ref, w_back_ref, w_in_s, w_back_s, bias_s = rest[7:14]
    lo_ref, first_ref, second_ref, x_ref, gb_ref, act_ref, gp_ref, att_ref, vec_ref = rest[14:]
    for slot, a_ref in enumerate((a0, a1, a2, a3)):
        for h, piece in enumerate(unpack_heads(a_ref, 0)):
            lo = slot * GROUP_WIDTH + h * HEAD_DIM
            att_ref[:, lo : lo + HEAD_DIM] = piece
    first_in = t_ref[...].astype(f32) + (mm(att_ref[...], w_out_s[...]) + row(bias_out_ref))
    first_ref[...] = first_in
    first_norm = spread(first_in)[0] * row(gain_one_ref) + row(shift_one_ref)
    x = first_norm.astype(bf16)
    x_ref[...] = x
    branch = jnp.zeros((QUARTER, WIDTH), f32)
    for q in range(TP):
        cols = slice(q * WIDTH, (q + 1) * WIDTH)
        bias_q = bias_s[q - 1, 0:1, :].astype(f32) if q else row(bias_in_ref)
        pre = mm(x, w_in_s[q - 1] if q else w_in_ref[...]) + bias_q
        square = pre * pre
        half = 0.5 + 0.5 * jnp.tanh(pre * (ROOT + CUBE * square))
        wide_act = pre * half
        act = wide_act.astype(bf16)
        act_ref[:, cols] = act
        gp_ref[:, cols] = half + wide_act * (1.0 - half) * (2.0 * ROOT + 6.0 * CUBE * square)
        branch = branch + (mm_nt(act, w_back_s[q - 1]) if q else mm(act, w_back_ref[...]))
    second_in = first_norm + branch + row(bias_back_ref)
    normal_two, scale_two = spread(second_in)
    lo_ref[...] = (normal_two * row(gain_two_ref) + row(shift_two_ref)).astype(bf16)
    grad_out = cot_ref[...].astype(f32)
    grad_second = spread_back(grad_out, row(gain_two_ref), normal_two, scale_two)
    second_ref[...] = grad_second
    grad_branch = grad_second.astype(bf16)
    gb_ref[...] = grad_branch
    vec_ref[...] = jnp.zeros_like(vec_ref)
    vec_ref[0:1, :] = jnp.sum(grad_out, axis=0, keepdims=True)
    vec_ref[1:2, :] = jnp.sum(grad_out * normal_two, axis=0, keepdims=True)
    vec_ref[2:3, :] = jnp.sum(grad_branch.astype(f32), axis=0, keepdims=True)


def position_mask(position, order):
    mask = 0
    for n, bit in enumerate(order):
        if (position >> (2 - n)) & 1:
            mask |= bit
    return mask


FFN_ORDERS = ((CORE, X_BIT, Y_BIT), (CORE, Y_BIT, X_BIT))


def weight_grads(info, left, right, keep, send, flip_scr, lhs_scr):
    mine = info[1]
    flip_scr[...] = left[...].T
    for n, order in enumerate(FFN_ORDERS):
        for p in range(SLOTS):
            start = pl.multiple_of((mine ^ position_mask(p, order)) * SLICE, SLICE)
            lhs_scr[p * SLICE : (p + 1) * SLICE, :] = flip_scr[pl.ds(start, SLICE), :]
        for pair in range(2):
            q = 2 * n + pair
            product = mm(lhs_scr[...], right[:, q * WIDTH : (q + 1) * WIDTH]).astype(bf16)
            for p in range(SLOTS):
                out = send if p >= SLOTS // 2 else keep
                out[n, p % (SLOTS // 2), pair] = product[p * SLICE : (p + 1) * SLICE, :]


def ffn_back_kernel(info, first_ref, second_ref, gb_ref, gp_ref, gain_one_ref, vec_in, *rest):
    w_out_s, w_in_ref, w_back_ref, w_in_s, w_back_s, x_ref, att_ref = rest[:7]
    g0, g1, g23, gin_ref, vec_ref, keep, send, go_keep, go_send = rest[7:16]
    gpre_ref, flip_scr, lhs_scr = rest[16:]
    grad_branch = gb_ref[...]
    grad_first = second_ref[...]
    vec_ref[...] = vec_in[...]
    for q in range(TP):
        cols = slice(q * WIDTH, (q + 1) * WIDTH)
        grad_act = mm(grad_branch, w_back_s[q - 1]) if q else mm_nt(grad_branch, w_back_ref[...])
        grad_pre = (grad_act * gp_ref[:, cols]).astype(bf16)
        gpre_ref[:, cols] = grad_pre
        vec_ref[pl.ds(6 + (info[2] ^ q), 1), :] = jnp.sum(grad_pre.astype(f32), axis=0, keepdims=True)
        grad_first = grad_first + mm_nt(grad_pre, w_in_s[q - 1] if q else w_in_ref[...])
    normal_one, scale_one = spread(first_ref[...])
    vec_ref[3:4, :] = jnp.sum(grad_first, axis=0, keepdims=True)
    vec_ref[4:5, :] = jnp.sum(grad_first * normal_one, axis=0, keepdims=True)
    grad_in = spread_back(grad_first, row(gain_one_ref), normal_one, scale_one)
    gin_ref[...] = grad_in
    grad_mixed = grad_in.astype(bf16)
    vec_ref[5:6, :] = jnp.sum(grad_mixed.astype(f32), axis=0, keepdims=True)
    grad_att = mm_nt(grad_mixed, w_out_s[...]).astype(bf16)
    for slot, (g_ref, row_at) in enumerate(((g0, 0), (g1, 0), (g23, 0), (g23, PACKED))):
        lo = slot * GROUP_WIDTH
        pack_heads(
            g_ref, row_at, [grad_att[:, lo + h * HEAD_DIM : lo + (h + 1) * HEAD_DIM] for h in range(GROUP)]
        )
    weight_grads(info, x_ref, gpre_ref, keep, send, flip_scr, lhs_scr)
    product = mm(grad_mixed.T, att_ref[...]).astype(bf16)
    go_keep[...] = product[:, : 2 * GROUP_WIDTH]
    go_send[...] = product[:, 2 * GROUP_WIDTH :]


ORDER_LA = (4, 2, 1)
ORDER_LB = (2, 4, 1)


HALF = WIDTH // 2
HELD = SLOTS // 2 * SLICE


def flip_kernel(t0, t1, t2, t3, out_ref):
    for slot, t_ref in enumerate((t0, t1, t2, t3)):
        out_ref[:, slot * QUARTER : (slot + 1) * QUARTER] = t_ref[...].T


def qkv_grad_kernel(
    info, tokens_t, gh0, gh1, gh2, go_own, go_near, vec_ref, s0, s1, s2, la_keep, la_send, lb_keep, lb_send, out_scr
):
    quarter, here = info[0], info[3]
    for h, gh_ref in enumerate((gh0, gh1, gh2)):
        product = mm(tokens_t[...], gh_ref[...]).astype(bf16)
        for kind in range(3):
            lo = kind * GROUP_WIDTH + h * HEAD_DIM
            out_scr[:, lo : lo + HEAD_DIM] = product[:, kind * HEAD_DIM : (kind + 1) * HEAD_DIM]
    add_to(out_scr.at[:, 3 * GROUP_WIDTH :], go_own[...], go_near[...])
    for keep, send, order, lo in (
        (la_keep, la_send, ORDER_LA, 0),
        (lb_keep, lb_send, ORDER_LB, HALF),
    ):
        for p in range(SLOTS):
            start = pl.multiple_of((here ^ position_mask(p, order)) * SLICE, SLICE)
            out = send if p >= SLOTS // 2 else keep
            row = p % (SLOTS // 2) * SLICE
            out[row : row + SLICE, :] = out_scr[pl.ds(start, SLICE), lo : lo + HALF]
    placed = []
    for kind in (0, 2):
        cols = slice(kind * HEAD_DIM, (kind + 1) * HEAD_DIM)
        piece = jnp.concatenate([sums[0:1, cols] for sums in (s0, s1, s2)], axis=1)
        placed.append(
            jnp.concatenate([jnp.where(quarter == g, piece, 0.0) for g in range(TP)], axis=1)
        )
    vectors = jnp.concatenate([vec_ref[0:10, :]] + placed + [vec_ref[12:VEC_ROWS, :]], axis=0)
    vectors = vectors.astype(bf16)
    for out in (la_keep, la_send, lb_keep, lb_send):
        out[HELD : HELD + VEC_ROWS, :] = vectors[:, :HALF]
        out[HELD + VEC_ROWS :, :] = vectors[:, HALF:]


def token_grad_kernel(gh0, gh1, gh2, w_ref, keep_ref, send_ref, all_scr):
    for h, gh_ref in enumerate((gh0, gh1, gh2)):
        for kind in range(3):
            lo = kind * GROUP_WIDTH + h * HEAD_DIM
            all_scr[:, lo : lo + HEAD_DIM] = gh_ref[:, kind * HEAD_DIM : (kind + 1) * HEAD_DIM]
    half = LENGTH // 2
    send_ref[...] = mm_nt(all_scr[half:, :], w_ref[...]).astype(bf16)
    keep_ref[...] = mm_nt(all_scr[:half, :], w_ref[...]).astype(bf16)


FFN_AT = 16 * SLICE + VEC_ROWS
HALF_GROUPS = TP // 2 * GROUP_WIDTH


def write_half(info, side, plane, qkv_hbm, out_hbm, w_in_hbm, qkv_scr, out_scr, w_in_scr, sems):
    quarter, mine, here = info[0], info[1], info[3]
    core = (quarter >> 1) ^ side
    first_col = core * HALF_GROUPS
    copies = []

    def send(source, target):
        copies.append(pltpu.make_async_copy(source, target, sems.at[len(copies)]))
        copies[-1].start()

    def piece(at, cols):
        block_off = here ^ at
        xy = ((block_off >> 2) & 1) + (block_off & 2)
        parts = []
        for group in range(2):
            nth = xy * 4 + ((quarter & 1) ^ group) + 2 * (block_off & 1)
            parts.append(plane[pl.ds(pl.multiple_of(nth * SLICE, SLICE), SLICE), cols])
        return jnp.concatenate(parts, axis=1).astype(f32)

    for chunk in range(SLOTS // 2):
        rows = pl.ds(2 * chunk * SLICE, 2 * SLICE)
        for kind in range(3):
            cols = pl.ds(kind * HALF_GROUPS, HALF_GROUPS)
            for at in (2 * chunk, 2 * chunk + 1):
                qkv_scr[at * SLICE : (at + 1) * SLICE, kind * HALF_GROUPS : (kind + 1) * HALF_GROUPS] = piece(
                    at, slice(kind * GROUP_WIDTH, (kind + 1) * GROUP_WIDTH)
                )
            to = pl.ds(pl.multiple_of(kind * WIDTH + first_col, 128), HALF_GROUPS)
            send(qkv_scr.at[rows, cols], qkv_hbm.at[rows, to])
        at = 2 * chunk + core
        mask = mine ^ at
        nth = (((mask >> 1) & 1) + ((mask >> 2) & 1) * 2) * 2
        start = pl.multiple_of(FFN_AT + nth * SLICE, VEC_ROWS)
        here_rows = pl.ds(chunk * SLICE, SLICE)
        w_in_scr[here_rows, :] = plane[pl.ds(start, SLICE), :].astype(f32)
        send(w_in_scr.at[here_rows, :], w_in_hbm.at[pl.ds(pl.multiple_of(at * SLICE, SLICE), SLICE), :])
    cols = slice(3 * GROUP_WIDTH, 4 * GROUP_WIDTH)
    out_scr[...] = jnp.concatenate([piece(at, cols) for at in range(SLOTS)], axis=0).T
    send(out_scr, out_hbm.at[pl.ds(pl.multiple_of(first_col, HALF_GROUPS), HALF_GROUPS), :])
    return copies


def first_half_kernel(info, plane, low_tokens, low_out, qkv_hbm, out_hbm, w_in_hbm, layer_out, token_out, *scratch):
    whole = [
        pltpu.make_async_copy(low_out, layer_out, scratch[4].at[0]),
        pltpu.make_async_copy(low_tokens, token_out, scratch[4].at[1]),
    ]
    for copy in whole:
        copy.start()
    wait_all(write_half(info, 0, plane, qkv_hbm, out_hbm, w_in_hbm, *scratch[:4]) + whole)


def second_half_kernel(info, plane, other, _qkv, _out, _w_in, qkv_hbm, out_hbm, w_in_hbm, w_back_hbm, *rest):
    vec_outs, scratch = rest[:9], rest[9:]
    mine, z_here = info[1], info[2]
    flip_scr, back_scr, sem = scratch[4:]
    for core in range(2):

        @pl.when((mine & 1) == core)
        def _(core=core):
            for at in range(SLOTS):
                mask = mine ^ at
                nth = (((mask >> 1) & 1) + ((mask >> 2) & 1) * 2) * 2 + 1
                start = pl.multiple_of(FFN_AT + nth * SLICE, VEC_ROWS)
                ref = plane if (at & 1) == core else other
                flip_scr[at * SLICE : (at + 1) * SLICE, :] = ref[pl.ds(start, SLICE), :].astype(f32)

    back_scr[...] = flip_scr[...].T
    back_copy = pltpu.make_async_copy(back_scr, w_back_hbm, sem)
    back_copy.start()
    copies = write_half(info, 1, other, qkv_hbm, out_hbm, w_in_hbm, *scratch[:4])
    vec_rows = slice(16 * SLICE, FFN_AT)
    vectors = total(plane[vec_rows, :], other[vec_rows, :])
    bias_in = jnp.zeros((1, WIDTH), f32)
    for q in range(TP):
        bias_in = jnp.where(z_here == q, vectors[6 + q : 7 + q, :], bias_in)
    for out, n in zip(vec_outs[:8], (0, 1, 2, 3, 4, 5, 10, 11)):
        out[...] = vectors[n]
    vec_outs[8][...] = bias_in[0]
    wait_all(copies + [back_copy])


def add_to(out, *terms):
    out[...] = add_low(*terms)


def join_kernel(*refs):
    out, at = refs[-1], 0
    for ref in refs[:-1]:
        out[at : at + ref.shape[0]] = ref[...]
        at += ref.shape[0]


def diag_kernel(by_x, by_y, first, second):
    half = first.shape[0]
    first[...] = by_x[:half]
    second[...] = by_y[half:]


CUT = SLICE


def mix_kernel(by_x, by_y, own, to_x, to_y):
    to_x[:PIECE] = own[...]
    to_y[:PIECE] = own[...]
    for n in range(2):
        to_x[PIECE + n * (PIECE - CUT) : PIECE + (n + 1) * (PIECE - CUT)] = by_y[n * PIECE + CUT : (n + 1) * PIECE]
        to_y[PIECE + n * CUT : PIECE + (n + 1) * CUT] = by_x[n * PIECE : n * PIECE + CUT]


def last_mix_kernel(by_x, by_y, to_x, to_y):
    to_x[...] = by_y[CUT:PIECE]
    to_y[...] = by_x[:CUT]


def to_z_kernel(own, other, out):
    out[:PACKED] = own[...]
    out[PACKED:] = other[PACKED:]


def level_one_kernel(keep, other, first, second):
    add_to(first, keep[0, 2:], other[0, 2:])
    add_to(second, keep[1, 2:], other[1, 2:])


def middle_kernel(in_keep, in_other, back_keep, back_other, back_x, back_y, to_x, to_y):
    for n in range(2):
        out = to_y if n else to_x
        for p in range(2):
            for pair in range(2):
                add_to(out.at[2 * p + pair], in_keep[n, 2 + p, pair], in_other[n, 2 + p, pair])
    for pair in range(2):
        add_to(to_y.at[4 + pair], back_keep[0, 1, pair], back_other[0, 1, pair], back_x[1, pair])
        add_to(to_x.at[4 + pair], back_keep[1, 1, pair], back_other[1, 1, pair], back_y[1, pair])


def in_two_kernel(keep, other, by_x, by_y, first, second):
    for pair in range(2):
        add_to(first.at[pair], keep[0, 1, pair], other[0, 1, pair], by_x[2 + pair])
        add_to(second.at[pair], keep[1, 1, pair], other[1, 1, pair], by_y[2 + pair])


def in_plane_kernel(keep, other, by_x, by_y, by_xy, by_yx, near, kept):
    for q in range(TP):
        order, pair = q // 2, q % 2
        first, second = (by_x, by_xy) if order == 0 else (by_y, by_yx)
        out = near if q % 2 else kept
        add_to(out.at[q // 2], keep[order, 0, pair], other[order, 0, pair], first[pair], second[pair])


def back_plane_kernel(keep, other, by_x, by_y, mid_x, mid_y, near, kept):
    for q in range(TP):
        order, pair = q // 2, q % 2
        first, second = (by_x, mid_y) if order == 0 else (by_y, mid_x)
        out = near if q % 2 else kept
        add_to(out.at[q // 2], keep[order, 0, pair], other[order, 0, pair], first[0, pair], second[4 + pair])


def far_kernel(kept, near, far):
    add_to(far, kept[1], near[1])


def last_kernel(kept_a, near_a, far_a, kept_b, near_b, far_b, out):
    add_to(out.at[0], kept_a[0], near_a[0], far_a[...])
    add_to(out.at[1], kept_b[0], near_b[0], far_b[...])


def go_kernel(keep, other, own, send):
    add_to(own, keep[:, :GROUP_WIDTH], other[:, :GROUP_WIDTH])
    add_to(send, keep[:, GROUP_WIDTH:], other[:, GROUP_WIDTH:])


def near_kernel(keep, other, out):
    add_to(out, keep[QUARTER:], other[QUARTER:])


def tokens_kernel(keep, other, near, grad_in, out_here, tokens, again):
    add_to(tokens, keep[:QUARTER], other[:QUARTER], near[...], grad_in[...])
    again[...] = out_here[...]


TWO = 2 * SLICE


def qkv_two_kernel(la, ra, lb, rb, la_out, lb_out):
    add_to(la_out, la[TWO:], ra[TWO:])
    add_to(lb_out, lb[TWO:HELD], rb[TWO:HELD])


def qkv_three_kernel(la, ra, ra2, lb, rb, rb2, out):
    add_to(out.at[:TWO, :HALF], la[:TWO], ra[:TWO], ra2[:TWO])
    add_to(out.at[:TWO, HALF:], lb[:TWO], rb[:TWO], rb2[...])
    for n in range(2):
        rows = slice(HELD + n * VEC_ROWS, HELD + (n + 1) * VEC_ROWS)
        rows_two = slice(TWO + n * VEC_ROWS, TWO + (n + 1) * VEC_ROWS)
        add_to(out.at[TWO:, n * HALF : (n + 1) * HALF], la[rows], ra[rows], ra2[rows_two])


def qkv_four_kernel(own, other, out):
    add_to(out.at[:SLICE], own[:SLICE], other[SLICE:TWO])
    add_to(out.at[SLICE:TWO], own[SLICE:TWO], other[:SLICE])
    add_to(out.at[TWO:], own[TWO:], other[TWO:])


def mix_l_kernel(by_x, by_y, other, to_x, to_y):
    to_x[:TWO] = other[:TWO]
    to_x[TWO:] = by_y[SLICE:TWO]
    to_y[:TWO] = other[:TWO]
    to_y[TWO:] = by_x[:SLICE]


def diag_kernel(l_x, l_y, f_x, f_y, to_x, to_y):
    to_x[:SLICE] = l_y[SLICE:TWO]
    to_x[SLICE:] = f_y[1]
    to_y[:SLICE] = l_x[:SLICE]
    to_y[SLICE:] = f_x[0]


def plane_l_kernel(own, other, x_own, y_own, x_other, y_other, f_own, f_x, f_y, d_x, d_y, out):
    diag_own = (y_other[TWO:], x_other[TWO:])
    diag_other = (d_y[:SLICE], d_x[:SLICE])
    places = (
        ((own[:SLICE], own[SLICE:TWO]), (other[:SLICE], other[SLICE:TWO])),
        ((x_own[:SLICE], x_own[SLICE:TWO]), (x_other[:SLICE], x_other[SLICE:TWO])),
        ((y_own[:SLICE], y_own[SLICE:TWO]), (y_other[:SLICE], y_other[SLICE:TWO])),
        (diag_own, diag_other),
    )
    for p, (here, there) in enumerate(places):
        for slot in range(TP):
            at = (p * TP + slot) * SLICE
            out[at : at + SLICE] = (there if slot % 2 else here)[slot // 2]
    add_to(out.at[16 * SLICE : FFN_AT], own[TWO:], other[TWO:])
    for n, (left, right) in enumerate(
        ((f_own[0], f_own[1]), (f_x[0], f_x[1]), (f_y[0], f_y[1]), (d_y[SLICE:], d_x[SLICE:]))
    ):
        out[FFN_AT + 2 * n * SLICE : FFN_AT + (2 * n + 1) * SLICE] = left
        out[FFN_AT + (2 * n + 1) * SLICE : FFN_AT + (2 * n + 2) * SLICE] = right


VMEM = pl.BlockSpec(memory_space=pltpu.VMEM)
SMEM = pl.BlockSpec(memory_space=pltpu.SMEM)
HBM = pl.BlockSpec(memory_space=pl.ANY)


def call(kernel, in_specs, outs, scratch, vmem_mib, name, deps=()):
    count, extra = len(in_specs), len(deps)

    def body(*refs):
        kernel(*refs[:count], *refs[count + extra :])

    run = pl.pallas_call(
        body,
        out_shape=[jax.ShapeDtypeStruct(shape, dtype) for shape, dtype in outs],
        in_specs=list(in_specs) + [HBM] * extra,
        out_specs=[VMEM] * len(outs),
        scratch_shapes=scratch,
        compiler_params=pltpu.CompilerParams(vmem_limit_bytes=vmem_mib * 1024 * 1024),
        cost_estimate=pl.CostEstimate(flops=1, bytes_accessed=1, transcendentals=0),
        name=name,
    )
    return lambda *arrays: run(*arrays, *deps)


def step(kernel, name, outs, *arrays, deps=()):
    shapes = [(shape, bf16) for shape in outs]
    result = call(kernel, [VMEM] * len(arrays), shapes, [], 12, name, deps)(*arrays)
    return result[0] if len(outs) == 1 else result


def per_device(
    tokens,
    w_qkv,
    bias_query,
    bias_value,
    w_out,
    bias_out,
    gain_attn,
    shift_attn,
    w_in,
    bias_in,
    w_back,
    bias_back,
    gain_ffn,
    shift_ffn,
    random_blocks,
    cotangent,
):
    dp_count = lax.axis_size("dp")
    d = lax.axis_index("dp")
    z = lax.axis_index("tp")
    core = d & 1
    quarter = (z & 1) + 2 * core
    mine = d & (SLOTS - 1)
    here = ((d >> 1) & 1) * 4 + ((d >> 2) & 1) * 2 + (z >> 1)
    native = (core == z // 2).astype(jnp.int32)
    info = jnp.stack([quarter, mine, z, here, native]).astype(jnp.int32)
    extra_bits = [1 << b for b in range(3, dp_count.bit_length() - 1)]

    own_tokens = place(tokens[0])
    piece = call(
        piece_kernel,
        [SMEM, HBM, VMEM, VMEM],
        [((2 * SLICE + VEC_ROWS, WIDTH), bf16)],
        [pltpu.VMEM((WIDTH, WIDTH), bf16), pltpu.SemaphoreType.DMA],
        8,
        "piece",
    )(info, w_in, w_back, bias_in)[0]
    piece_one = hop(piece, 0, 1)
    piece_two = hop(piece, 0, 2)
    random_own = random_blocks.reshape(-1)
    random_other = hop(random_own, CORE, 0)
    w_group, bias_group = call(
        group_kernel,
        [SMEM, VMEM, VMEM, VMEM],
        [((WIDTH, 3 * GROUP_WIDTH), bf16), ((1, 3 * GROUP_WIDTH), f32)],
        [],
        16,
        "group",
    )(info, w_qkv, bias_query, bias_value)
    near_tokens = hop(own_tokens, 0, 1)
    core_tokens = hop(own_tokens, CORE, 0)
    far_tokens = hop(near_tokens, CORE, 0)
    part_one = step(
        join_kernel, "pair", [(2 * PIECE, WIDTH)], piece_one, piece_two, deps=(own_tokens, w_group, random_other)
    )
    x_one = hop(part_one, X_BIT, 0)
    y_one = hop(part_one, Y_BIT, 0)
    piece_three = hop(piece_two, 0, 1)
    cot = place(cotangent[0])
    to_x, to_y = step(
        mix_kernel,
        "mix",
        [(3 * PIECE - 2 * CUT, WIDTH), (PIECE + 2 * CUT, WIDTH)],
        x_one,
        y_one,
        piece_three,
        deps=(near_tokens,),
    )
    x_three = hop(to_x, X_BIT, 0)
    y_three = hop(to_y, Y_BIT, 0)

    packed = ((PACKED, 2 * HEAD_DIM), bf16)
    double = ((2 * PACKED, 2 * HEAD_DIM), bf16)
    per_head = ((LENGTH, HEAD_DIM), bf16)
    token_slots = (own_tokens, near_tokens, core_tokens, far_tokens)
    a0, a13, a2, *heads = call(
        attention_kernel,
        [SMEM] * 3 + [VMEM] * 6,
        [packed, double, packed] + [per_head] * 9 + [((16, QUARTER), f32)],
        [pltpu.VMEM((GROUP, LENGTH, HEAD_DIM), bf16)],
        24,
        "attention",
        (to_x, core_tokens),
    )(info, random_own, random_other, *token_slots, w_group, bias_group)
    heads, lse = heads[:9], heads[9]
    a1 = hop(a13, 0, 1)
    a2 = hop(a2, CORE, 0)
    a3 = hop(a1[PACKED:], CORE, 0)
    to_x, to_y = step(
        last_mix_kernel,
        "mix_last",
        [(PIECE - CUT, WIDTH), (CUT, WIDTH)],
        x_three,
        y_three,
        deps=(a0, cot),
    )
    last_back = hop(to_x, X_BIT, 0)
    last_in = hop(to_y, Y_BIT, 0)
    held = step(
        held_kernel,
        "held",
        [(11 * PIECE, WIDTH)],
        part_one,
        x_one,
        y_one,
        piece_three,
        x_three,
        y_three,
        deps=(a2, cot),
    )
    tokens_t = call(flip_kernel, [VMEM] * 4, [((WIDTH, LENGTH), bf16)], [], 8, "flip_tokens", (a1, held))(
        *token_slots
    )[0]
    last = step(join_kernel, "last_piece", [(PIECE, WIDTH)], last_in, last_back, deps=(tokens_t,))
    quarters = ((TP - 1, WIDTH, WIDTH), bf16)
    w_in_s, w_back_s, w_out_s, bias_s = call(
        assemble_kernel,
        [SMEM] + [VMEM] * 6,
        [quarters, quarters, ((WIDTH, WIDTH), bf16), ((TP - 1, VEC_ROWS, WIDTH), bf16)],
        [],
        20,
        "assemble",
    )(info, held, hop(held, CORE, 0), last_in, last_back, hop(last, CORE, 0), w_out)

    rows = ((QUARTER, WIDTH), bf16)
    wide = ((QUARTER, TP * WIDTH), bf16)
    rows_f32 = ((QUARTER, WIDTH), f32)
    vec_rows = ((VEC_ROWS, WIDTH), f32)
    out_here, first_in, grad_second, ffn_input, grad_branch, activated, gelu_slope, attended, vectors = call(
        ffn_kernel,
        [SMEM] + [VMEM] * 19,
        [rows, rows_f32, rows_f32, rows, rows, wide, ((QUARTER, TP * WIDTH), f32), rows, vec_rows],
        [],
        20,
        "ffn",
        (tokens_t,),
    )(
        info,
        own_tokens,
        a0,
        a1,
        a2,
        a3,
        bias_out,
        gain_attn,
        shift_attn,
        bias_back,
        gain_ffn,
        shift_ffn,
        bias_in,
        cot,
        w_out_s,
        w_in,
        w_back,
        w_in_s,
        w_back_s,
        bias_s,
    )
    pairs = ((2, SLOTS // 2, 2, SLICE, WIDTH), bf16)
    halves = ((WIDTH, 2 * GROUP_WIDTH), bf16)
    flips = [pltpu.VMEM((WIDTH, QUARTER), bf16), pltpu.VMEM((WIDTH, QUARTER), bf16)]
    back_keep, back_send = call(
        weight_grads, [SMEM] + [VMEM] * 2, [pairs] * 2, flips, 12, "back_grads"
    )(info, grad_branch, activated)
    back_other = hop(back_send, CORE, 0)

    g0, g1_send, g23, grad_in, vectors, in_keep, in_send, go_keep, go_send = call(
        ffn_back_kernel,
        [SMEM] + [VMEM] * 13,
        [packed, packed, double, rows_f32, vec_rows] + [pairs] * 2 + [halves] * 2,
        [pltpu.VMEM((QUARTER, TP * WIDTH), bf16)] + flips,
        20,
        "ffn_back",
        (back_keep,),
    )(
        info,
        first_in,
        grad_second,
        grad_branch,
        gelu_slope,
        gain_attn,
        vectors,
        w_out_s,
        w_in,
        w_back,
        w_in_s,
        w_back_s,
        ffn_input,
        attended,
    )
    g2 = hop(g23, CORE, 0)
    g13 = hop(step(to_z_kernel, "to_z", [double[0]], g1_send, g2), 0, 1)

    first_level = [(2, 2, SLICE, WIDTH)] * 2
    def hop_pair(pair, first, second):
        return hop(pair[0], first, 0), hop(pair[1], second, 0)

    back_sums = step(level_one_kernel, "back_one", first_level, back_keep, back_other, deps=(g0,))
    back_x, back_y = hop_pair(back_sums, X_BIT, Y_BIT)
    in_other = hop(in_send, CORE, 0)
    go_other = hop(go_send, CORE, 0)

    def head_back(h, deps):
        return call(
            functools.partial(attention_back_kernel, h),
            [SMEM] * 3 + [VMEM] * 7,
            [((LENGTH, 3 * HEAD_DIM), bf16), ((8, 3 * HEAD_DIM), f32)],
            [
                pltpu.VMEM((LENGTH, HEAD_DIM), bf16),
                pltpu.VMEM((LENGTH, HEAD_DIM), f32),
                pltpu.VMEM((LENGTH, HEAD_DIM), f32),
                pltpu.VMEM((LENGTH, HEAD_DIM), f32),
            ],
            12,
            f"attention_back_{h}",
            deps,
        )(info, random_own, random_other, *heads[3 * h : 3 * h + 3], lse, g0, g13, g2)

    go_own, go_send = step(go_kernel, "go", [(WIDTH, GROUP_WIDTH)] * 2, go_keep, go_other)
    go_near = hop(go_send, 0, 1)
    gh0, s0 = head_back(0, (go_own, back_sums[0]))
    back_parts = [back_keep, back_other, back_x, back_y]
    to_x, to_y = step(
        middle_kernel,
        "middle",
        [(6, SLICE, WIDTH)] * 2,
        in_keep,
        in_other,
        *back_parts,
        deps=(gh0,),
    )
    mid_x, mid_y = hop(to_x, X_BIT, 0), hop(to_y, Y_BIT, 0)
    in_parts = [in_keep, in_other, mid_x, mid_y]
    z_level = [(2, SLICE, WIDTH)] * 2
    gh1, s1 = head_back(1, (to_x,))
    gh2, s2 = head_back(2, (gh1,))

    la_keep, la_send, lb_keep, lb_send = call(
        qkv_grad_kernel,
        [SMEM] + [VMEM] * 10,
        [((HELD + 2 * VEC_ROWS, HALF), bf16)] * 4,
        [pltpu.VMEM((WIDTH, 4 * GROUP_WIDTH), bf16)],
        16,
        "qkv_grads",
        (gh2,),
    )(info, tokens_t, gh0, gh1, gh2, go_own, go_near, vectors, s0, s1, s2)
    ra = hop(la_send, X_BIT, 0)
    rb = hop(lb_send, Y_BIT, 0)

    keep, send = call(
        token_grad_kernel,
        [VMEM] * 4,
        [((LENGTH // 2, WIDTH), bf16)] * 2,
        [pltpu.VMEM((LENGTH, 3 * GROUP_WIDTH), bf16)],
        16,
        "token_grad",
        (la_keep,),
    )(gh0, gh1, gh2, w_group)
    other = hop(send, CORE, 0)
    near_b, kept_b = step(
        back_plane_kernel, "back_plane", z_level, *back_parts, mid_x, mid_y, deps=(keep,)
    )
    near_b = hop(near_b, 0, 1)
    sums = step(in_two_kernel, "in_two", z_level, *in_parts, deps=(kept_b,))
    in_parts += hop_pair(sums, Y_BIT, X_BIT)
    near_low = step(near_kernel, "near", [(QUARTER, WIDTH)], keep, other, deps=(sums[0],))
    near = hop(near_low, 0, 1)
    far_b = step(far_kernel, "far_back", [(SLICE, WIDTH)], kept_b, near_b, deps=(near_low,))
    far_hop_b = hop(far_b, 0, 2)
    la2, lb2 = step(
        qkv_two_kernel,
        "qkv_two",
        [(TWO + 2 * VEC_ROWS, HALF), (TWO, HALF)],
        la_keep,
        ra,
        lb_keep,
        rb,
        deps=(far_b,),
    )
    ra2 = hop(la2, Y_BIT, 0)
    rb2 = hop(lb2, X_BIT, 0)
    rows_l = (TWO + VEC_ROWS, WIDTH)
    near_a, kept_a = step(in_plane_kernel, "in_plane", z_level, *in_parts, deps=(la2,))
    near_a = hop(near_a, 0, 1)
    partial = step(
        qkv_three_kernel, "qkv_three", [rows_l], la_keep, ra, ra2, lb_keep, rb, rb2, deps=(kept_a, far_hop_b)
    )
    far_a = step(far_kernel, "far_in", [(SLICE, WIDTH)], kept_a, near_a, deps=(partial, far_hop_b))
    far_hop_a = hop(far_a, 0, 2)
    sum_l = step(
        qkv_four_kernel, "qkv_four", [rows_l], partial, hop(partial, 0, 2), deps=(far_a, near)
    )
    for bit in extra_bits:
        sum_l = add_low(sum_l, hop(sum_l, bit, 0))

    own_l = sum_l[:TWO]
    x_own = hop(own_l, X_BIT, 0)
    y_own = hop(own_l, Y_BIT, 0)
    other_l = hop(sum_l, 0, 1)
    to_x, to_y = step(
        mix_l_kernel, "mix_l", [(TWO + SLICE, WIDTH)] * 2, x_own, y_own, other_l
    )
    x_other = hop(to_x, X_BIT, 0)
    y_other = hop(to_y, Y_BIT, 0)
    sum_f = step(
        last_kernel,
        "last",
        [(2, SLICE, WIDTH)],
        kept_a,
        near_a,
        far_hop_a,
        kept_b,
        near_b,
        far_hop_b,
        deps=(to_x,),
    )
    for bit in extra_bits:
        sum_f = add_low(sum_f, hop(sum_f, bit, 0))
    low_outs = step(
        tokens_kernel,
        "tokens",
        [(QUARTER, WIDTH)] * 2,
        keep,
        other,
        near,
        grad_in,
        out_here,
        deps=(sum_f,),
    )
    token_grads, layer_out = place(low_outs[0]), place(low_outs[1])
    f_x = hop(sum_f, X_BIT, 0)
    f_y = hop(sum_f, Y_BIT, 0)
    diag = step(diag_kernel, "diag", [(TWO, WIDTH)] * 2, x_other, y_other, f_x, f_y)
    d_x, d_y = hop_pair(diag, X_BIT, Y_BIT)
    plane = step(
        plane_l_kernel,
        "plane",
        [(FFN_AT + SLOTS * SLICE, WIDTH)],
        sum_l,
        other_l,
        x_own,
        y_own,
        x_other,
        y_other,
        sum_f,
        f_x,
        f_y,
        d_x,
        d_y,
        deps=(token_grads, layer_out),
    )
    square = ((WIDTH, WIDTH), f32)
    halves_out = [((WIDTH, 3 * WIDTH), f32), square, square]
    half_scratch = [
        pltpu.VMEM((WIDTH, 3 * HALF_GROUPS), f32),
        pltpu.VMEM((HALF_GROUPS, WIDTH), f32),
        pltpu.VMEM((WIDTH // 2, WIDTH), f32),
        pltpu.SemaphoreType.DMA((2 * SLOTS + 1,)),
    ]
    as_shape = lambda outs: [jax.ShapeDtypeStruct(shape, dtype) for shape, dtype in outs]
    cheap = pl.CostEstimate(flops=1, bytes_accessed=1, transcendentals=0)
    *half_written, layer_out, grad_tokens = pl.pallas_call(
        first_half_kernel,
        out_shape=as_shape(halves_out + [rows, rows]),
        in_specs=[SMEM] + [VMEM] * 3,
        out_specs=[HBM] * 5,
        scratch_shapes=half_scratch + [pltpu.SemaphoreType.DMA((2,))],
        compiler_params=pltpu.CompilerParams(vmem_limit_bytes=16 * 1024 * 1024),
        cost_estimate=cheap,
        name="first_half",
    )(info, plane, token_grads, layer_out)
    grad_w_qkv, grad_w_out, grad_w_in, grad_w_back, *vec_outs = pl.pallas_call(
        second_half_kernel,
        out_shape=as_shape(halves_out + [square] + [((WIDTH,), f32)] * 9),
        in_specs=[SMEM, VMEM, VMEM] + [HBM] * 3,
        out_specs=[HBM] * 4 + [VMEM] * 9,
        scratch_shapes=half_scratch + [pltpu.VMEM((WIDTH, WIDTH), f32)] * 2 + [pltpu.SemaphoreType.DMA],
        input_output_aliases={3: 0, 4: 1, 5: 2},
        compiler_params=pltpu.CompilerParams(vmem_limit_bytes=24 * 1024 * 1024),
        cost_estimate=cheap,
        name="second_half",
    )(info, plane, hop(plane, CORE, 0), *half_written)
    (
        grad_shift_ffn,
        grad_gain_ffn,
        grad_bias_back,
        grad_shift_attn,
        grad_gain_attn,
        grad_bias_out,
        grad_bias_query,
        grad_bias_value,
        grad_bias_in,
    ) = vec_outs
    return (
        layer_out[None],
        grad_tokens[None],
        grad_w_qkv,
        grad_bias_query,
        grad_bias_value,
        grad_w_out,
        grad_bias_out,
        grad_gain_attn,
        grad_shift_attn,
        grad_w_in,
        grad_bias_in,
        grad_w_back,
        grad_bias_back,
        grad_gain_ffn,
        grad_shift_ffn,
    )


def solution(mesh):
    in_specs = (
        P("dp", "tp", None),
        P(),
        P(),
        P(),
        P(),
        P(),
        P(),
        P(),
        P(None, "tp"),
        P("tp"),
        P("tp", None),
        P(),
        P(),
        P(),
        P("dp", None, None, None),
        P("dp", "tp", None),
    )
    out_specs = (
        P("dp", "tp", None),
        P("dp", "tp", None),
        P(),
        P(),
        P(),
        P(),
        P(),
        P(),
        P(),
        P(None, "tp"),
        P("tp"),
        P("tp", None),
        P(),
        P(),
        P(),
    )
    return jax.shard_map(
        per_device, mesh=mesh, in_specs=in_specs, out_specs=out_specs, check_vma=False
    )
```
